32 devices in a mesh: section: 4 (over y, x), feat: 2 (over core), tensor: 4 (over z).
Axes of the slice: x: 2, y: 2, z: 4, core: 2. Of those that a mesh axis runs over, the one named last changes fastest.
Arguments:
- clean_resid: bfloat16 [32, 8192], P(('section', 'feat'), 'tensor'), may hold values from -6 to 6
- corrupt_resid: bfloat16 [32, 8192], P(('section', 'feat'), 'tensor'), may hold values from -6 to 6
- metric_grad: bfloat16 [32, 8192], P(('section', 'feat'), 'tensor'), may hold values from -0.796875 to 0.796875
- enc_weight: bfloat16 [8192, 4096], P('tensor', ('section', 'feat')), may hold values from -0.0625 to 0.0625
- enc_bias: float32 [4096], P(('section', 'feat')), may hold values from -3 to 3
- dec_weight: bfloat16 [4096, 8192], P(('section', 'feat'), 'tensor'), may hold values from -0.0625 to 0.0625
Outputs:
- feature_effect: float32 [4096], P(('section', 'feat'))
- error_effect: float32 [32], P(('section', 'feat'))
The draws below stay inside these ranges and needn't reach their ends.
All inputs are finite; a program needn't handle non-finite values.
Results may differ from the reference program's by a relative error of at most 0.0003.
Values may be sent and summed in bfloat16 or wider, within the bound.
No kernel may reach another device: no remote copies, remote signals or barrier semaphores. Data moves between devices by JAX's collectives and lax.ppermute only.
A program may use at most 64 MiB of HBM per device.

```python
import jax
import jax.numpy as jnp

D = 8192
FEATURES = 4096
TOKENS = 32


def level_of(key, dims, cuts, smallest, largest):
    level = 1.0
    for dim, parts in cuts:
        draws = jax.random.uniform(jax.random.fold_in(jax.random.fold_in(key, 6), dim), (parts,), jnp.float32, smallest / len(cuts), largest / len(cuts))
        level = level * jnp.repeat(jnp.exp(draws), dims[dim] // parts).reshape((-1,) + (1,) * (len(dims) - 1 - dim))
    return level


def scatter_about(stream_key, shape, scale, reach, pieces=(), held_as=jnp.bfloat16):
    result = scale * jax.random.normal(stream_key, shape, jnp.float32)
    if pieces:
        result = result * level_of(stream_key, shape, pieces, -0.22, 0.18)
    return jnp.clip(result, -reach, reach).astype(held_as)


def setup_inputs(seed: int = 0) -> dict:
    streams_of = jax.random.split(jax.random.key(seed), 7)
    clean_resid = scatter_about(streams_of[0], (TOKENS, D), 1.0, 6.0, ((0, 8), (1, 4)))
    corrupt_resid = scatter_about(streams_of[1], (TOKENS, D), 1.0, 6.0, ((0, 8), (1, 4)))
    metric_grad = scatter_about(streams_of[2], (TOKENS, D), 0.1, 0.796875, ((0, 8), (1, 4)))
    enc_weight = scatter_about(streams_of[3], (D, FEATURES), D ** -0.5, 0.0625, ((0, 4), (1, 8)))
    enc_bias = scatter_about(streams_of[4], (FEATURES,), 0.5, 3.0, ((0, 8),), jnp.float32)
    dec_weight = scatter_about(streams_of[5], (FEATURES, D), D ** -0.5, 0.0625, ((0, 8), (1, 4)))
    return {"clean_resid": clean_resid, "corrupt_resid": corrupt_resid, "metric_grad": metric_grad, "enc_weight": enc_weight, "enc_bias": enc_bias, "dec_weight": dec_weight}


def reference(clean_resid, corrupt_resid, metric_grad, enc_weight, enc_bias, dec_weight):
    act_clean = jax.nn.relu(jnp.dot(clean_resid, enc_weight, preferred_element_type=jnp.float32) + enc_bias)
    act_corrupt = jax.nn.relu(jnp.dot(corrupt_resid, enc_weight, preferred_element_type=jnp.float32) + enc_bias)
    projected = jnp.dot(metric_grad, dec_weight.T, preferred_element_type=jnp.float32)
    attribution = (act_corrupt - act_clean) * projected
    feature_effect = jnp.sum(attribution, axis=0)
    token_total = jnp.sum(attribution, axis=1)
    shifted = corrupt_resid.astype(jnp.float32) - clean_resid.astype(jnp.float32)
    inner_sum = jnp.sum(shifted * metric_grad.astype(jnp.float32), axis=1)
    return feature_effect, inner_sum - token_total
```

```python
import jax
import jax.numpy as jnp
from jax import lax
from jax.sharding import PartitionSpec as P

OWNERS = ("section", "feat")
EVERY = ("section", "feat", "tensor")


def add_up(values):
    while len(values) > 1:
        values = [a + b for a, b in zip(values[::2], values[1::2])]
    return values[0]


def per_device(groups, parts, clean_resid, corrupt_resid, metric_grad, enc_weight, enc_bias, dec_weight):
    tokens = clean_resid.shape[0]
    features = enc_weight.shape[1]
    run = groups // parts
    me = lax.axis_index("tensor")

    stacked = jnp.stack([clean_resid, corrupt_resid, metric_grad])
    blocks = [stacked] + [
        lax.ppermute(stacked, OWNERS, [(g, g ^ k) for g in range(groups)]) for k in range(1, groups)
    ]
    rows = jnp.concatenate(blocks, axis=1)
    encoded = jnp.einsum("srd,df->srf", rows[:2], enc_weight, preferred_element_type=jnp.float32)
    projected = lax.dot_general(
        rows[2], dec_weight, (((1,), (1,)), ((), ())), preferred_element_type=jnp.float32
    )
    preact = jnp.concatenate([encoded, projected[None]], axis=0)
    preact = preact.reshape(3, parts, run * tokens, features)

    terms = [lax.dynamic_index_in_dim(preact, me, 1, keepdims=False)]
    for m in range(1, parts):
        chunk = lax.dynamic_index_in_dim(preact, me ^ m, 1, keepdims=False)
        terms.append(lax.ppermute(chunk, "tensor", [(t, t ^ m) for t in range(parts)]))
    total = add_up(terms)

    act_clean = jax.nn.relu(total[0] + enc_bias)
    act_corrupt = jax.nn.relu(total[1] + enc_bias)
    attribution = (act_corrupt - act_clean) * total[2]
    feature_part = jnp.sum(attribution, axis=0)
    token_part = jnp.sum(attribution, axis=1).reshape(run, tokens)
    shifted = corrupt_resid.astype(jnp.float32) - clean_resid.astype(jnp.float32)
    inner_part = jnp.sum(shifted * metric_grad.astype(jnp.float32), axis=1)

    both = jnp.concatenate([feature_part, inner_part])
    sums = [both] + [
        lax.ppermute(both, "tensor", [(t, t ^ m) for t in range(parts)]) for m in range(1, parts)
    ]
    sums = add_up(sums)
    feature_effect, inner_sum = sums[:features], sums[features:]
    totals = []
    for m in range(parts):
        arrived = []
        for j in range(run):
            pairs = [
                (g * parts + t, (g ^ (t * run + j)) * parts + (t ^ m))
                for g in range(groups)
                for t in range(parts)
            ]
            arrived.append(lax.ppermute(token_part[j], EVERY, pairs))
        totals.append(sum(arrived))
    error_sum = inner_sum - add_up(totals)
    return (feature_effect, error_sum)


def solution(mesh):
    groups = mesh.shape["section"] * mesh.shape["feat"]
    parts = mesh.shape["tensor"]
    in_specs = (
        P(("section", "feat"), "tensor"),
        P(("section", "feat"), "tensor"),
        P(("section", "feat"), "tensor"),
        P("tensor", ("section", "feat")),
        P(("section", "feat")),
        P(("section", "feat"), "tensor"),
    )
    out_specs = (P(("section", "feat")), P(("section", "feat")))

    def run(*args):
        return per_device(groups, parts, *args)

    return jax.shard_map(run, mesh=mesh, in_specs=in_specs, out_specs=out_specs, check_vma=False)
```

```python
import jax
import jax.numpy as jnp
from jax import lax
from jax.sharding import PartitionSpec as P

EVERY = ("section", "feat", "tensor")


def add_up(values):
    while len(values) > 1:
        values = [a + b for a, b in zip(values[::2], values[1::2])]
    return values[0]


def swap_all(value, axis, size):
    return [value] + [
        lax.ppermute(value, axis, [(i, i ^ k) for i in range(size)]) for k in range(1, size)
    ]


def per_device(sizes, clean_resid, corrupt_resid, metric_grad, enc_weight, enc_bias, dec_weight):
    sections, feats, parts = sizes
    groups = sections * feats
    tokens = clean_resid.shape[0]
    features = enc_weight.shape[1]
    share = features // parts

    stacked = jnp.stack([clean_resid, corrupt_resid, metric_grad])
    near = jnp.concatenate(swap_all(stacked, "section", sections), axis=1)
    rows = jnp.concatenate(swap_all(near, "feat", feats), axis=1)
    encoded = jnp.einsum("srd,df->srf", rows[:2], enc_weight, preferred_element_type=jnp.float32)
    projected = lax.dot_general(
        rows[2], dec_weight, (((1,), (1,)), ((), ())), preferred_element_type=jnp.float32
    )
    preact = jnp.concatenate([encoded, projected[None]], axis=0)
    preact = preact.reshape(3, groups * tokens, parts, share)

    total = add_up([*lax.all_to_all(preact.transpose(2, 0, 1, 3), "tensor", 0, 0)])
    bias = lax.dynamic_index_in_dim(enc_bias.reshape(parts, share), lax.axis_index("tensor"), 0)

    act_clean = jax.nn.relu(total[0] + bias)
    act_corrupt = jax.nn.relu(total[1] + bias)
    attribution = (act_corrupt - act_clean) * total[2]
    feature_part = jnp.sum(attribution, axis=0)
    token_part = jnp.sum(attribution, axis=1)
    shifted = corrupt_resid.astype(jnp.float32) - clean_resid.astype(jnp.float32)
    inner_part = jnp.sum(shifted * metric_grad.astype(jnp.float32), axis=1)
    token_part = token_part - jnp.pad(inner_part, (0, (groups - 1) * tokens))

    both = jnp.concatenate([feature_part, token_part])
    every = lax.all_to_all(jnp.broadcast_to(both, (groups * parts, both.size)), EVERY, 0, 0)
    section, feat = lax.axis_index("section"), lax.axis_index("feat")
    mine = lax.dynamic_slice_in_dim(every, (section * feats + feat) * parts, parts, 0)
    feature_effect = mine[:, :share].reshape(features)
    arrived = every[:, share:].reshape(sections, feats, parts, feats, sections, tokens)
    wanted = (
        jnp.arange(sections)[:, None, None, None] ^ section == jnp.arange(sections)
    ) & ((jnp.arange(feats)[:, None] ^ feat == jnp.arange(feats))[:, :, None])
    kept = jnp.where(wanted[:, :, None, :, :, None], arrived, 0.0)
    return (feature_effect, -jnp.sum(kept, axis=(0, 1, 2, 3, 4)))


def solution(mesh):
    sizes = [mesh.shape[name] for name in EVERY]
    in_specs = (
        P(("section", "feat"), "tensor"),
        P(("section", "feat"), "tensor"),
        P(("section", "feat"), "tensor"),
        P("tensor", ("section", "feat")),
        P(("section", "feat")),
        P(("section", "feat"), "tensor"),
    )
    out_specs = (P(("section", "feat")), P(("section", "feat")))

    def run(*args):
        return per_device(sizes, *args)

    return jax.shard_map(run, mesh=mesh, in_specs=in_specs, out_specs=out_specs, check_vma=False)
```

```python
import functools

import jax
import jax.numpy as jnp
from jax import lax
from jax.experimental import pallas as pl
from jax.experimental.pallas import tpu as pltpu
from jax.sharding import PartitionSpec as P

LANES = 128
TILE = 8


def exchange(value, axis, size, k):
    return lax.ppermute(value, axis, [(i, i ^ k) for i in range(size)])


def pack_kernel(*refs):
    *parts, packed, sems = refs
    copies = [
        pltpu.make_async_copy(part, packed.at[i], sems.at[i]) for i, part in enumerate(parts)
    ]
    for copy in copies:
        copy.start()
    for copy in copies:
        copy.wait()


def pack(*parts):
    tokens, width = parts[0].shape
    return pl.pallas_call(
        pack_kernel,
        out_shape=jax.ShapeDtypeStruct((len(parts), tokens, width), parts[0].dtype),
        in_specs=[pl.BlockSpec(memory_space=pl.ANY)] * len(parts),
        out_specs=pl.BlockSpec(memory_space=pl.ANY),
        scratch_shapes=[pltpu.SemaphoreType.DMA((len(parts),))],
        name="pack_rows",
    )(*parts)


def product_kernel(groups, parts, *refs):
    blocks = refs[:groups]
    enc, dec = refs[groups : groups + 2]
    outs = refs[groups + 2 : groups + 2 + parts]
    inner, rows, held = refs[groups + 2 + parts :]
    tokens = blocks[0].shape[1]
    total = groups * tokens
    share = LANES
    for k, block in enumerate(blocks):
        for a in range(3):
            rows[pl.ds(a * total + k * tokens, tokens), :] = block[a].astype(jnp.float32)
    encoded = jnp.dot(
        rows[pl.ds(0, 2 * total), :].astype(jnp.bfloat16),
        enc[...],
        preferred_element_type=jnp.float32,
    )
    projected = lax.dot_general(
        rows[pl.ds(2 * total, total), :].astype(jnp.bfloat16),
        dec[...],
        (((1,), (1,)), ((), ())),
        preferred_element_type=jnp.float32,
    )
    for c in range(parts):
        held[c, pl.ds(0, 2 * total), :] = encoded[:, c * share : (c + 1) * share]
        held[c, pl.ds(2 * total, total), :] = projected[:, c * share : (c + 1) * share]
    me = lax.axis_index("tensor")
    for m, out in enumerate(outs):
        out[...] = held[me ^ m]
    own = [rows[pl.ds(a * total, tokens), :] for a in range(3)]
    inner_part = jnp.sum((own[1] - own[0]) * own[2], axis=1, keepdims=True)
    inner[pl.ds(0, tokens), :] = jnp.broadcast_to(inner_part, (tokens, LANES))


def products(parts, blocks, enc_weight, dec_weight):
    groups = len(blocks)
    _, tokens, width = blocks[0].shape
    features = enc_weight.shape[1]
    rows = 3 * groups * tokens
    part = jax.ShapeDtypeStruct((rows, features // parts), jnp.float32)
    inner = jax.ShapeDtypeStruct((TILE, LANES), jnp.float32)
    vmem = pl.BlockSpec(memory_space=pltpu.VMEM)
    return pl.pallas_call(
        functools.partial(product_kernel, groups, parts),
        out_shape=[part] * parts + [inner],
        in_specs=[vmem] * (groups + 2),
        out_specs=[vmem] * (parts + 1),
        scratch_shapes=[
            pltpu.VMEM((rows, width), jnp.float32),
            pltpu.VMEM((parts, rows, features // parts), jnp.float32),
        ],
        compiler_params=pltpu.CompilerParams(vmem_limit_bytes=48 * 2**20),
        name="products",
    )(*blocks, enc_weight, dec_weight)


def attribution_kernel(sizes, *refs):
    sections, feats, parts = sizes
    groups = sections * feats
    terms = refs[:parts]
    bias, inner, sums = refs[parts:]
    total = terms[0].shape[0] // 3
    tokens = total // groups
    values = [term[...] for term in terms]
    while len(values) > 1:
        values = [a + b for a, b in zip(values[::2], values[1::2])]
    preact = values[0]
    me = lax.axis_index("tensor")
    b = bias[pl.ds(me, 1), :]
    act_clean = jnp.maximum(preact[:total] + b, 0.0)
    act_corrupt = jnp.maximum(preact[total : 2 * total] + b, 0.0)
    attribution = (act_corrupt - act_clean) * preact[2 * total :]

    head = sums.shape[0] - groups
    sums[pl.ds(0, head), :] = jnp.zeros((head, LANES), jnp.float32)
    sums[pl.ds(me, 1), :] = jnp.sum(attribution, axis=0, keepdims=True)
    token_part = jnp.sum(attribution, axis=1, keepdims=True)
    lane = lax.broadcasted_iota(jnp.int32, (tokens, LANES), 1)
    place = lane == lax.broadcasted_iota(jnp.int32, (tokens, LANES), 0)
    section, feat = lax.axis_index("section"), lax.axis_index("feat")
    for p in range(feats):
        for q in range(sections):
            k = p * sections + q
            column = jnp.broadcast_to(token_part[k * tokens : (k + 1) * tokens], (tokens, LANES))
            if k == 0:
                column = column - inner[pl.ds(0, tokens), :]
            row = jnp.sum(jnp.where(place, column, 0.0), axis=0, keepdims=True)
            owner = (section ^ q) * feats + (feat ^ p)
            sums[pl.ds(head + owner, 1), :] = row


def attributions(sizes, terms, bias, inner):
    sections, feats, parts = sizes
    head = -(-parts // TILE) * TILE
    vmem = pl.BlockSpec(memory_space=pltpu.VMEM)
    return pl.pallas_call(
        functools.partial(attribution_kernel, sizes),
        out_shape=jax.ShapeDtypeStruct((head + sections * feats, LANES), jnp.float32),
        in_specs=[vmem] * (parts + 2),
        out_specs=vmem,
        compiler_params=pltpu.CompilerParams(vmem_limit_bytes=16 * 2**20),
        name="attributions",
    )(*terms, bias, inner)


def per_device(sizes, clean_resid, corrupt_resid, metric_grad, enc_weight, enc_bias, dec_weight):
    sections, feats, parts = sizes
    tokens = clean_resid.shape[0]
    features = enc_weight.shape[1]

    packed = pack(clean_resid, corrupt_resid, metric_grad)
    near = [packed] + [exchange(packed, "section", sections, q) for q in range(1, sections)]
    blocks = near + [exchange(block, "feat", feats, p) for p in range(1, feats) for block in near]

    *terms, inner = products(parts, blocks, enc_weight, dec_weight)
    arrived = [terms[0]] + [exchange(terms[m], "tensor", parts, m) for m in range(1, parts)]
    sums = attributions(sizes, arrived, enc_bias.reshape(parts, features // parts), inner)

    step = 1
    while step < parts:
        sums = sums + exchange(sums, "tensor", parts, step)
        step *= 2
    feature_effect = sums[:parts].reshape(features)
    owed = sums[-sections * feats :]
    for axis, size in (("section", sections), ("feat", feats)):
        step = 1
        while step < size:
            owed = owed + exchange(owed, axis, size, step)
            step *= 2
    owner = lax.axis_index("section") * feats + lax.axis_index("feat")
    return (feature_effect, -lax.dynamic_slice(owed, (owner, 0), (1, tokens)).reshape(tokens))


def solution(mesh):
    sizes = [mesh.shape[name] for name in ("section", "feat", "tensor")]
    in_specs = (
        P(("section", "feat"), "tensor"),
        P(("section", "feat"), "tensor"),
        P(("section", "feat"), "tensor"),
        P("tensor", ("section", "feat")),
        P(("section", "feat")),
        P(("section", "feat"), "tensor"),
    )
    out_specs = (P(("section", "feat")), P(("section", "feat")))
    return jax.shard_map(
        functools.partial(per_device, sizes),
        mesh=mesh,
        in_specs=in_specs,
        out_specs=out_specs,
        check_vma=False,
    )
```

```python
import functools

import jax
import jax.numpy as jnp
from jax import lax
from jax.experimental import pallas as pl
from jax.experimental.pallas import tpu as pltpu
from jax.sharding import PartitionSpec as P

LANES = 128
TILE = 8


EVERY = ("section", "feat", "tensor")
SUMMER = 1


def far_first(size, send):
    sent = {k: send(k) for k in reversed(range(1, size))}
    return [sent[k] for k in range(1, size)]


def exchange(value, axis, size, k):
    return lax.ppermute(value, axis, [(i, i ^ k) for i in range(size)])


def load_kernel(pieces, *refs):
    count = (len(refs) - 1) // 2
    sems = refs[-1]
    copies = []
    for i in range(count):
        source, target = refs[i], refs[count + i]
        step = source.shape[0] // pieces
        for j in range(pieces):
            part = pl.ds(j * step, step)
            copies.append(
                pltpu.make_async_copy(source.at[part], target.at[part], sems.at[i, j])
            )
    for copy in copies:
        copy.start()
    for copy in copies:
        copy.wait()


def load(*arrays, pieces=4):
    size = sum(array.size * array.dtype.itemsize for array in arrays)
    return pl.pallas_call(
        functools.partial(load_kernel, pieces),
        out_shape=[jax.ShapeDtypeStruct(array.shape, array.dtype) for array in arrays],
        in_specs=[pl.BlockSpec(memory_space=pl.ANY)] * len(arrays),
        out_specs=[pl.BlockSpec(memory_space=pltpu.VMEM)] * len(arrays),
        scratch_shapes=[pltpu.SemaphoreType.DMA((len(arrays), pieces))],
        compiler_params=pltpu.CompilerParams(vmem_limit_bytes=16 * 2**20),
        cost_estimate=pl.CostEstimate(flops=0, bytes_accessed=2 * size, transcendentals=0),
        name="load_weights",
    )(*arrays)


def product_kernel(groups, parts, *refs):
    blocks = refs[:groups]
    enc, dec = refs[groups : groups + 2]
    outs = refs[groups + 2 : groups + 2 + parts]
    inner, rows, held = refs[groups + 2 + parts :]
    tokens = blocks[0].shape[1]
    total = groups * tokens
    share = LANES
    for k, block in enumerate(blocks):
        for a in range(3):
            rows[pl.ds(a * total + k * tokens, tokens), :] = block[a].astype(jnp.float32)
    encoded = jnp.dot(
        rows[pl.ds(0, 2 * total), :].astype(jnp.bfloat16),
        enc[...],
        preferred_element_type=jnp.float32,
    )
    projected = lax.dot_general(
        rows[pl.ds(2 * total, total), :].astype(jnp.bfloat16),
        dec[...],
        (((1,), (1,)), ((), ())),
        preferred_element_type=jnp.float32,
    )
    for c in range(parts):
        held[c, pl.ds(0, 2 * total), :] = encoded[:, c * share : (c + 1) * share]
        held[c, pl.ds(2 * total, total), :] = projected[:, c * share : (c + 1) * share]
    me = lax.axis_index("tensor")
    for m, out in enumerate(outs):
        out[...] = held[me ^ m]
    own = [rows[pl.ds(a * total, tokens), :] for a in range(3)]
    inner_part = jnp.sum((own[1] - own[0]) * own[2], axis=1, keepdims=True)
    inner[pl.ds(0, tokens), :] = jnp.broadcast_to(inner_part, (tokens, LANES))


def products(parts, blocks, enc_weight, dec_weight):
    groups = len(blocks)
    _, tokens, width = blocks[0].shape
    features = enc_weight.shape[1]
    rows = 3 * groups * tokens
    part = jax.ShapeDtypeStruct((rows, features // parts), jnp.float32)
    inner = jax.ShapeDtypeStruct((TILE, LANES), jnp.float32)
    vmem = pl.BlockSpec(memory_space=pltpu.VMEM)
    return pl.pallas_call(
        functools.partial(product_kernel, groups, parts),
        out_shape=[part] * parts + [inner],
        in_specs=[vmem] * (groups + 2),
        out_specs=[vmem] * (parts + 1),
        scratch_shapes=[
            pltpu.VMEM((rows, width), jnp.float32),
            pltpu.VMEM((parts, rows, features // parts), jnp.float32),
        ],
        compiler_params=pltpu.CompilerParams(vmem_limit_bytes=48 * 2**20),
        name="products",
    )(*blocks, enc_weight, dec_weight)


def add_up(values):
    while len(values) > 1:
        values = [a + b for a, b in zip(values[::2], values[1::2])]
    return values[0]


def attribution_kernel(sizes, *refs):
    sections, feats, parts = sizes
    groups = sections * feats
    terms = refs[:parts]
    bias, inner, sums = refs[parts:]
    total = terms[0].shape[0] // 3
    tokens = total // groups
    preact = add_up([term[...] for term in terms])
    section, feat = lax.axis_index("section"), lax.axis_index("feat")
    b = bias[pl.ds(lax.axis_index("tensor"), 1), :]
    act_clean = jnp.maximum(preact[:total] + b, 0.0)
    act_corrupt = jnp.maximum(preact[total : 2 * total] + b, 0.0)
    attribution = (act_corrupt - act_clean) * preact[2 * total :]

    tail = sums.shape[0] - groups
    sums[pl.ds(groups, tail), :] = jnp.zeros((tail, LANES), jnp.float32)
    sums[pl.ds(groups + feat, 1), :] = jnp.sum(attribution, axis=0, keepdims=True)
    token_part = jnp.sum(attribution, axis=1, keepdims=True)
    lane = lax.broadcasted_iota(jnp.int32, (tokens, LANES), 1)
    place = lane == lax.broadcasted_iota(jnp.int32, (tokens, LANES), 0)
    for p in range(feats):
        for q in range(sections):
            k = p * sections + q
            column = jnp.broadcast_to(token_part[k * tokens : (k + 1) * tokens], (tokens, LANES))
            if k == 0:
                column = column - inner[pl.ds(0, tokens), :]
            row = jnp.sum(jnp.where(place, column, 0.0), axis=0, keepdims=True)
            owner = (section ^ q) * feats + (feat ^ p)
            sums[pl.ds(owner, 1), :] = row


def round_up(size):
    return -(-size // TILE) * TILE


def attributions(sizes, terms, bias, inner):
    sections, feats, parts = sizes
    vmem = pl.BlockSpec(memory_space=pltpu.VMEM)
    return pl.pallas_call(
        functools.partial(attribution_kernel, sizes),
        out_shape=jax.ShapeDtypeStruct(
            (sections * feats + round_up(feats), LANES), jnp.float32
        ),
        in_specs=[vmem] * (parts + 2),
        out_specs=vmem,
        compiler_params=pltpu.CompilerParams(vmem_limit_bytes=16 * 2**20),
        name="attributions",
    )(*terms, bias, inner)


def total_kernel(sizes, *refs):
    sections, feats, parts = sizes
    groups = sections * feats
    sums, outs = refs[: sections * parts], refs[sections * parts :]
    me, section = lax.axis_index("tensor"), lax.axis_index("section")
    owed = add_up([part[pl.ds(0, groups), :] for part in sums])
    for f, out in enumerate(outs):
        for m in range(parts):
            out[pl.ds(me ^ m, 1), :] = sums[m][pl.ds(groups + f, 1), :]
        row = lax.broadcasted_iota(jnp.int32, (groups, LANES), 0) == section * feats + f
        out[pl.ds(parts, 1), :] = -jnp.sum(jnp.where(row, owed, 0.0), axis=0, keepdims=True)


def totals(sizes, sums):
    feats, parts = sizes[1:]
    vmem = pl.BlockSpec(memory_space=pltpu.VMEM)
    result = jax.ShapeDtypeStruct((round_up(parts + 1), LANES), jnp.float32)
    return pl.pallas_call(
        functools.partial(total_kernel, sizes),
        out_shape=[result] * feats,
        in_specs=[vmem] * len(sums),
        out_specs=[vmem] * feats,
        compiler_params=pltpu.CompilerParams(vmem_limit_bytes=32 * 2**20),
        name="totals",
    )(*sums)


def final_kernel(parts, *refs):
    *results, feature_out, error_out = refs
    feat = lax.axis_index("feat")
    value = results[0][...]
    for f, result in enumerate(results[1:]):
        value = jnp.where(feat == (f if f < SUMMER else f + 1), result[...], value)
    for i in range(parts):
        feature_out[pl.ds(i * LANES, LANES)] = value[i]
    error_out[...] = value[parts, : error_out.shape[0]]


def final(parts, tokens, results):
    vmem = pl.BlockSpec(memory_space=pltpu.VMEM)
    return pl.pallas_call(
        functools.partial(final_kernel, parts),
        out_shape=[
            jax.ShapeDtypeStruct((parts * LANES,), jnp.float32),
            jax.ShapeDtypeStruct((tokens,), jnp.float32),
        ],
        in_specs=[vmem] * len(results),
        out_specs=[vmem] * 2,
        name="final",
    )(*results)


def per_device(sizes, clean_resid, corrupt_resid, metric_grad, enc_weight, enc_bias, dec_weight):
    sections, feats, parts = sizes
    tokens = clean_resid.shape[0]
    features = enc_weight.shape[1]

    packed = jnp.stack([clean_resid, corrupt_resid, metric_grad])
    near = [packed] + far_first(sections, lambda q: exchange(packed, "section", sections, q))
    enc_weight, dec_weight = load(enc_weight, dec_weight)
    blocks = near + [exchange(block, "feat", feats, p) for p in range(1, feats) for block in near]

    *terms, inner = products(parts, blocks, enc_weight, dec_weight)
    arrived = far_first(parts, lambda m: exchange(terms[m], "tensor", parts, m))
    bias = enc_bias.reshape(parts, features // parts)
    sums = attributions(sizes, [terms[0]] + arrived, bias, inner)

    device = lambda s, f, t: (s * feats + f) * parts + t
    places = [(s, t) for s in range(sections) for t in range(parts)]
    for f in range(1, feats):
        pairs = [(device(s, f, t), device(s, 0, t)) for s, t in places]
        sums = sums + lax.ppermute(sums, EVERY, pairs)
    spread = {}
    for q, m in reversed(places):
        pairs = [(device(s, 0, t), device(s ^ q, SUMMER, t ^ m)) for s, t in places]
        spread[q, m] = lax.ppermute(sums, EVERY, pairs)
    results = totals(sizes, [spread[place] for place in places])
    handed = [results[SUMMER]]
    for f in range(feats):
        if f != SUMMER:
            pairs = [(device(s, SUMMER, t), device(s, f, t)) for s, t in places]
            handed.append(lax.ppermute(results[f], EVERY, pairs))
    return tuple(final(parts, tokens, handed))


def solution(mesh):
    sizes = [mesh.shape[name] for name in ("section", "feat", "tensor")]
    in_specs = (
        P(("section", "feat"), "tensor"),
        P(("section", "feat"), "tensor"),
        P(("section", "feat"), "tensor"),
        P("tensor", ("section", "feat")),
        P(("section", "feat")),
        P(("section", "feat"), "tensor"),
    )
    out_specs = (P(("section", "feat")), P(("section", "feat")))
    return jax.shard_map(
        functools.partial(per_device, sizes),
        mesh=mesh,
        in_specs=in_specs,
        out_specs=out_specs,
        check_vma=False,
    )
```

```python
import functools

import jax
import jax.numpy as jnp
from jax import lax
from jax.experimental import pallas as pl
from jax.experimental.pallas import tpu as pltpu
from jax.sharding import PartitionSpec as P

LANES = 128
TILE = 8


EVERY = ("section", "feat", "tensor")


def far_first(size, send):
    sent = {k: send(k) for k in reversed(range(1, size))}
    return [sent[k] for k in range(1, size)]


def exchange(value, axis, size, k):
    return lax.ppermute(value, axis, [(i, i ^ k) for i in range(size)])


def inner_kernel(packed, inner):
    tokens = packed.shape[1]
    clean, corrupt, grad = [packed[a].astype(jnp.float32) for a in range(3)]
    part = jnp.sum((corrupt - clean) * grad, axis=1, keepdims=True)
    inner[pl.ds(0, tokens), :] = jnp.broadcast_to(part, (tokens, LANES))


def inner_products(packed):
    vmem = pl.BlockSpec(memory_space=pltpu.VMEM)
    return pl.pallas_call(
        inner_kernel,
        out_shape=jax.ShapeDtypeStruct((TILE, LANES), jnp.float32),
        in_specs=[vmem],
        out_specs=vmem,
        name="inner_products",
    )(packed)


def load_kernel(pieces, *refs):
    count = (len(refs) - 2) // 2
    sems = refs[-1]
    copies = []
    for i in range(count):
        source, target = refs[1 + i], refs[1 + count + i]
        step = source.shape[0] // pieces
        for j in range(pieces):
            part = pl.ds(j * step, step)
            copies.append(
                pltpu.make_async_copy(source.at[part], target.at[part], sems.at[i, j])
            )
    for copy in copies:
        copy.start()
    for copy in copies:
        copy.wait()


def load(after, *arrays, pieces=4):
    size = sum(array.size * array.dtype.itemsize for array in arrays)
    return pl.pallas_call(
        functools.partial(load_kernel, pieces),
        out_shape=[jax.ShapeDtypeStruct(array.shape, array.dtype) for array in arrays],
        in_specs=[pl.BlockSpec(memory_space=pltpu.VMEM)]
        + [pl.BlockSpec(memory_space=pltpu.HBM)] * len(arrays),
        out_specs=[pl.BlockSpec(memory_space=pltpu.VMEM)] * len(arrays),
        scratch_shapes=[pltpu.SemaphoreType.DMA((len(arrays), pieces))],
        compiler_params=pltpu.CompilerParams(vmem_limit_bytes=48 * 2**20),
        cost_estimate=pl.CostEstimate(flops=0, bytes_accessed=2 * size, transcendentals=0),
        name="load_weights",
    )(after, *arrays)


def product_kernel(groups, parts, *refs):
    blocks = refs[:groups]
    enc, dec = refs[groups : groups + 2]
    outs = refs[groups + 2 : groups + 2 + parts]
    rows, held = refs[groups + 2 + parts :]
    tokens = blocks[0].shape[1]
    total = groups * tokens
    share = LANES
    for k, block in enumerate(blocks):
        for a in range(3):
            rows[pl.ds(a * total + k * tokens, tokens), :] = block[a].astype(jnp.float32)
    encoded = jnp.dot(
        rows[pl.ds(0, 2 * total), :].astype(jnp.bfloat16),
        enc[...],
        preferred_element_type=jnp.float32,
    )
    projected = lax.dot_general(
        rows[pl.ds(2 * total, total), :].astype(jnp.bfloat16),
        dec[...],
        (((1,), (1,)), ((), ())),
        preferred_element_type=jnp.float32,
    )
    for c in range(parts):
        held[c, pl.ds(0, 2 * total), :] = encoded[:, c * share : (c + 1) * share]
        held[c, pl.ds(2 * total, total), :] = projected[:, c * share : (c + 1) * share]
    me = lax.axis_index("tensor")
    for m, out in enumerate(outs):
        out[...] = held[me ^ m]


def products(parts, blocks, enc_weight, dec_weight):
    groups = len(blocks)
    _, tokens, width = blocks[0].shape
    features = enc_weight.shape[1]
    rows = 3 * groups * tokens
    part = jax.ShapeDtypeStruct((rows, features // parts), jnp.float32)
    vmem = pl.BlockSpec(memory_space=pltpu.VMEM)
    return pl.pallas_call(
        functools.partial(product_kernel, groups, parts),
        out_shape=[part] * parts,
        in_specs=[vmem] * (groups + 2),
        out_specs=[vmem] * parts,
        scratch_shapes=[
            pltpu.VMEM((rows, width), jnp.float32),
            pltpu.VMEM((parts, rows, features // parts), jnp.float32),
        ],
        compiler_params=pltpu.CompilerParams(vmem_limit_bytes=48 * 2**20),
        name="products",
    )(*blocks, enc_weight, dec_weight)


def add_up(values):
    while len(values) > 1:
        values = [a + b for a, b in zip(values[::2], values[1::2])]
    return values[0]


def attribution_kernel(sizes, *refs):
    sections, feats, parts = sizes
    groups = sections * feats
    terms = refs[:parts]
    bias, inner, sums = refs[parts:]
    total = terms[0].shape[0] // 3
    tokens = total // groups
    preact = add_up([term[...] for term in terms])
    section, feat = lax.axis_index("section"), lax.axis_index("feat")
    b = bias[pl.ds(lax.axis_index("tensor"), 1), :]
    act_clean = jnp.maximum(preact[:total] + b, 0.0)
    act_corrupt = jnp.maximum(preact[total : 2 * total] + b, 0.0)
    attribution = (act_corrupt - act_clean) * preact[2 * total :]

    devices = groups * parts
    feature_part = jnp.sum(attribution, axis=0, keepdims=True)
    sums[:, 0, :] = jnp.broadcast_to(feature_part, (devices, LANES))
    token_part = jnp.sum(attribution, axis=1, keepdims=True)
    lane = lax.broadcasted_iota(jnp.int32, (tokens, LANES), 1)
    place = lane == lax.broadcasted_iota(jnp.int32, (tokens, LANES), 0)
    for p in range(feats):
        for q in range(sections):
            k = p * sections + q
            column = jnp.broadcast_to(token_part[k * tokens : (k + 1) * tokens], (tokens, LANES))
            if k == 0:
                column = column - inner[pl.ds(0, tokens), :]
            row = jnp.sum(jnp.where(place, column, 0.0), axis=0, keepdims=True)
            owner = (section ^ q) * feats + (feat ^ p)
            sums[pl.ds(owner * parts, parts), 1, :] = jnp.broadcast_to(row, (parts, LANES))


def attributions(sizes, terms, bias, inner):
    sections, feats, parts = sizes
    vmem = pl.BlockSpec(memory_space=pltpu.VMEM)
    return pl.pallas_call(
        functools.partial(attribution_kernel, sizes),
        out_shape=jax.ShapeDtypeStruct((sections * feats * parts, 2, LANES), jnp.float32),
        in_specs=[vmem] * (parts + 2),
        out_specs=vmem,
        compiler_params=pltpu.CompilerParams(vmem_limit_bytes=16 * 2**20),
        name="attributions",
    )(*terms, bias, inner)


def final_kernel(sizes, arrived, feature_out, error_out, features, errors, sems):
    sections, feats, parts = sizes
    group = lax.axis_index("section") * feats + lax.axis_index("feat")
    mine = arrived[pl.ds(group * parts, parts), 0, :]
    for i in range(parts):
        features[pl.ds(i * LANES, LANES)] = mine[i]
    feature_copy = pltpu.make_async_copy(features, feature_out, sems.at[0])
    feature_copy.start()
    owed = add_up([arrived[i, 1:2, :] for i in range(sections * feats * parts)])
    errors[...] = -owed[0, : errors.shape[0]]
    error_copy = pltpu.make_async_copy(errors, error_out, sems.at[1])
    error_copy.start()
    feature_copy.wait()
    error_copy.wait()


def final(sizes, tokens, arrived):
    features = (sizes[2] * LANES,)
    return pl.pallas_call(
        functools.partial(final_kernel, sizes),
        out_shape=[
            jax.ShapeDtypeStruct(features, jnp.float32),
            jax.ShapeDtypeStruct((tokens,), jnp.float32),
        ],
        in_specs=[pl.BlockSpec(memory_space=pltpu.VMEM)],
        out_specs=[pl.BlockSpec(memory_space=pltpu.HBM)] * 2,
        scratch_shapes=[
            pltpu.VMEM(features, jnp.float32),
            pltpu.VMEM((tokens,), jnp.float32),
            pltpu.SemaphoreType.DMA((2,)),
        ],
        name="final",
    )(arrived)


def per_device(sizes, clean_resid, corrupt_resid, metric_grad, enc_weight, enc_bias, dec_weight):
    sections, feats, parts = sizes
    tokens = clean_resid.shape[0]
    features = enc_weight.shape[1]

    packed = jnp.stack([clean_resid, corrupt_resid, metric_grad])
    near = [packed] + far_first(sections, lambda q: exchange(packed, "section", sections, q))
    inner = inner_products(packed)
    enc_weight, dec_weight = load(packed, enc_weight, dec_weight)
    blocks = near + [exchange(block, "feat", feats, p) for p in range(1, feats) for block in near]

    terms = products(parts, blocks, enc_weight, dec_weight)
    arrived = far_first(parts, lambda m: exchange(terms[m], "tensor", parts, m))
    bias = enc_bias.reshape(parts, features // parts)
    sums = attributions(sizes, [terms[0]] + arrived, bias, inner)

    return tuple(final(sizes, tokens, lax.all_to_all(sums, EVERY, 0, 0)))


def solution(mesh):
    sizes = [mesh.shape[name] for name in ("section", "feat", "tensor")]
    in_specs = (
        P(("section", "feat"), "tensor"),
        P(("section", "feat"), "tensor"),
        P(("section", "feat"), "tensor"),
        P("tensor", ("section", "feat")),
        P(("section", "feat")),
        P(("section", "feat"), "tensor"),
    )
    out_specs = (P(("section", "feat")), P(("section", "feat")))
    return jax.shard_map(
        functools.partial(per_device, sizes),
        mesh=mesh,
        in_specs=in_specs,
        out_specs=out_specs,
        check_vma=False,
    )
```

```python
import functools

import jax
import jax.numpy as jnp
from jax import lax
from jax.experimental import pallas as pl
from jax.experimental.pallas import tpu as pltpu
from jax.sharding import PartitionSpec as P

LANES = 128
TILE = 8


EVERY = ("section", "feat", "tensor")


def far_first(size, send):
    sent = {k: send(k) for k in reversed(range(1, size))}
    return [sent[k] for k in range(1, size)]


def exchange(value, axis, size, k):
    return lax.ppermute(value, axis, [(i, i ^ k) for i in range(size)])


def inner_kernel(packed, inner):
    tokens = packed.shape[1]
    clean, corrupt, grad = [packed[a].astype(jnp.float32) for a in range(3)]
    part = jnp.sum((corrupt - clean) * grad, axis=1, keepdims=True)
    inner[pl.ds(0, tokens), :] = jnp.broadcast_to(part, (tokens, LANES))


def inner_products(packed):
    vmem = pl.BlockSpec(memory_space=pltpu.VMEM)
    return pl.pallas_call(
        inner_kernel,
        out_shape=jax.ShapeDtypeStruct((TILE, LANES), jnp.float32),
        in_specs=[vmem],
        out_specs=vmem,
        compiler_params=pltpu.CompilerParams(vmem_limit_bytes=4 * 2**20),
        name="inner_products",
    )(packed)


def load_kernel(pieces, *refs):
    count = (len(refs) - 2) // 2
    sems = refs[-1]
    copies = []
    for i in range(count):
        source, target = refs[1 + i], refs[1 + count + i]
        count_here = min(pieces, source.shape[0] // 16) or 1
        step = source.shape[0] // count_here
        for j in range(count_here):
            part = pl.ds(j * step, step)
            copies.append(
                pltpu.make_async_copy(source.at[part], target.at[part], sems.at[i, j])
            )
    for copy in copies:
        copy.start()
    for copy in copies:
        copy.wait()


def load(after, *arrays, pieces=16):
    size = sum(array.size * array.dtype.itemsize for array in arrays)
    return pl.pallas_call(
        functools.partial(load_kernel, pieces),
        out_shape=[jax.ShapeDtypeStruct(array.shape, array.dtype) for array in arrays],
        in_specs=[pl.BlockSpec(memory_space=pltpu.VMEM)]
        + [pl.BlockSpec(memory_space=pltpu.HBM)] * len(arrays),
        out_specs=[pl.BlockSpec(memory_space=pltpu.VMEM)] * len(arrays),
        scratch_shapes=[pltpu.SemaphoreType.DMA((len(arrays), pieces))],
        compiler_params=pltpu.CompilerParams(vmem_limit_bytes=50 * 2**20),
        cost_estimate=pl.CostEstimate(flops=0, bytes_accessed=2 * size, transcendentals=0),
        name="load_weights",
    )(after, *arrays)


def product_kernel(groups, parts, *refs):
    blocks = refs[:groups]
    enc, dec = refs[groups : groups + 2]
    outs = refs[groups + 2 : groups + 2 + parts]
    rows, held = refs[groups + 2 + parts :]
    tokens = blocks[0].shape[1]
    total = groups * tokens
    share = LANES
    for k, block in enumerate(blocks):
        for a in range(3):
            rows[pl.ds(a * total + k * tokens, tokens), :] = block[a].astype(jnp.float32)
    encoded = jnp.dot(
        rows[pl.ds(0, 2 * total), :].astype(jnp.bfloat16),
        enc[...],
        preferred_element_type=jnp.float32,
    )
    projected = lax.dot_general(
        rows[pl.ds(2 * total, total), :].astype(jnp.bfloat16),
        dec[...],
        (((1,), (1,)), ((), ())),
        preferred_element_type=jnp.float32,
    )
    for c in range(parts):
        held[c, pl.ds(0, 2 * total), :] = encoded[:, c * share : (c + 1) * share]
        held[c, pl.ds(2 * total, total), :] = projected[:, c * share : (c + 1) * share]
    me = lax.axis_index("tensor")
    for m, out in enumerate(outs):
        out[...] = held[me ^ m]


def products(parts, blocks, enc_weight, dec_weight):
    groups = len(blocks)
    _, tokens, width = blocks[0].shape
    features = enc_weight.shape[1]
    rows = 3 * groups * tokens
    part = jax.ShapeDtypeStruct((rows, features // parts), jnp.float32)
    vmem = pl.BlockSpec(memory_space=pltpu.VMEM)
    return pl.pallas_call(
        functools.partial(product_kernel, groups, parts),
        out_shape=[part] * parts,
        in_specs=[vmem] * (groups + 2),
        out_specs=[vmem] * parts,
        scratch_shapes=[
            pltpu.VMEM((rows, width), jnp.float32),
            pltpu.VMEM((parts, rows, features // parts), jnp.float32),
        ],
        compiler_params=pltpu.CompilerParams(vmem_limit_bytes=48 * 2**20),
        name="products",
    )(*blocks, enc_weight, dec_weight)


def add_up(values):
    while len(values) > 1:
        values = [a + b for a, b in zip(values[::2], values[1::2])]
    return values[0]


def attribution_kernel(sizes, *refs):
    sections, feats, parts = sizes
    groups = sections * feats
    terms = refs[:parts]
    bias, inner, sums = refs[parts:]
    total = terms[0].shape[0] // 3
    tokens = total // groups
    preact = add_up([term[...] for term in terms])
    section, feat = lax.axis_index("section"), lax.axis_index("feat")
    b = bias[pl.ds(lax.axis_index("tensor"), 1), :]
    act_clean = jnp.maximum(preact[:total] + b, 0.0)
    act_corrupt = jnp.maximum(preact[total : 2 * total] + b, 0.0)
    attribution = (act_corrupt - act_clean) * preact[2 * total :]

    devices = groups * parts
    feature_part = jnp.sum(attribution, axis=0, keepdims=True)
    sums[:, 0, :] = jnp.broadcast_to(feature_part, (devices, LANES))
    token_part = jnp.sum(attribution, axis=1, keepdims=True)
    lane = lax.broadcasted_iota(jnp.int32, (tokens, LANES), 1)
    place = lane == lax.broadcasted_iota(jnp.int32, (tokens, LANES), 0)
    for p in range(feats):
        for q in range(sections):
            k = p * sections + q
            column = jnp.broadcast_to(token_part[k * tokens : (k + 1) * tokens], (tokens, LANES))
            if k == 0:
                column = column - inner[pl.ds(0, tokens), :]
            row = jnp.sum(jnp.where(place, column, 0.0), axis=0, keepdims=True)
            owner = (section ^ q) * feats + (feat ^ p)
            sums[pl.ds(owner * parts, parts), 1, :] = jnp.broadcast_to(row, (parts, LANES))


def attributions(sizes, terms, bias, inner):
    sections, feats, parts = sizes
    vmem = pl.BlockSpec(memory_space=pltpu.VMEM)
    return pl.pallas_call(
        functools.partial(attribution_kernel, sizes),
        out_shape=jax.ShapeDtypeStruct((sections * feats * parts, 2, LANES), jnp.float32),
        in_specs=[vmem] * (parts + 2),
        out_specs=vmem,
        compiler_params=pltpu.CompilerParams(vmem_limit_bytes=16 * 2**20),
        name="attributions",
    )(*terms, bias, inner)


def final_kernel(sizes, arrived, feature_out, error_out, features, errors, sems):
    sections, feats, parts = sizes
    group = lax.axis_index("section") * feats + lax.axis_index("feat")
    mine = arrived[pl.ds(group * parts, parts), 0, :]
    for i in range(parts):
        features[pl.ds(i * LANES, LANES)] = mine[i]
    feature_copy = pltpu.make_async_copy(features, feature_out, sems.at[0])
    feature_copy.start()
    owed = add_up([arrived[i, 1:2, :] for i in range(sections * feats * parts)])
    errors[...] = -owed[0, : errors.shape[0]]
    error_copy = pltpu.make_async_copy(errors, error_out, sems.at[1])
    error_copy.start()
    feature_copy.wait()
    error_copy.wait()


def final(sizes, tokens, arrived):
    features = (sizes[2] * LANES,)
    return pl.pallas_call(
        functools.partial(final_kernel, sizes),
        out_shape=[
            jax.ShapeDtypeStruct(features, jnp.float32),
            jax.ShapeDtypeStruct((tokens,), jnp.float32),
        ],
        in_specs=[pl.BlockSpec(memory_space=pltpu.VMEM)],
        out_specs=[pl.BlockSpec(memory_space=pltpu.HBM)] * 2,
        scratch_shapes=[
            pltpu.VMEM(features, jnp.float32),
            pltpu.VMEM((tokens,), jnp.float32),
            pltpu.SemaphoreType.DMA((2,)),
        ],
        compiler_params=pltpu.CompilerParams(vmem_limit_bytes=4 * 2**20),
        name="final",
    )(arrived)


def per_device(sizes, clean_resid, corrupt_resid, metric_grad, enc_weight, enc_bias, dec_weight):
    sections, feats, parts = sizes
    tokens = clean_resid.shape[0]
    features = enc_weight.shape[1]

    packed = jnp.stack([clean_resid, corrupt_resid, metric_grad])
    near = [packed] + far_first(sections, lambda q: exchange(packed, "section", sections, q))
    inner = inner_products(packed)
    bias = enc_bias.reshape(parts, features // parts)
    (enc_weight,) = load(packed, enc_weight)
    far = []
    for p in range(1, feats):
        for block in near:
            if block is packed:
                block, _ = lax.optimization_barrier((block, enc_weight))
            far.append(exchange(block, "feat", feats, p))
    (dec_weight,) = load(near[-1], dec_weight)
    blocks = near + far

    terms = products(parts, blocks, enc_weight, dec_weight)
    arrived = far_first(parts, lambda m: exchange(terms[m], "tensor", parts, m))
    sums = attributions(sizes, [terms[0]] + arrived, bias, inner)

    return tuple(final(sizes, tokens, lax.all_to_all(sums, EVERY, 0, 0)))


def solution(mesh):
    sizes = [mesh.shape[name] for name in ("section", "feat", "tensor")]
    in_specs = (
        P(("section", "feat"), "tensor"),
        P(("section", "feat"), "tensor"),
        P(("section", "feat"), "tensor"),
        P("tensor", ("section", "feat")),
        P(("section", "feat")),
        P(("section", "feat"), "tensor"),
    )
    out_specs = (P(("section", "feat")), P(("section", "feat")))
    return jax.shard_map(
        functools.partial(per_device, sizes),
        mesh=mesh,
        in_specs=in_specs,
        out_specs=out_specs,
        check_vma=False,
    )
```

```python
import functools

import jax
import jax.numpy as jnp
from jax import lax
from jax.experimental import pallas as pl
from jax.experimental.pallas import tpu as pltpu
from jax.sharding import PartitionSpec as P

LANES = 128
TILE = 8


EVERY = ("section", "feat", "tensor")


def far_first(size):
    return [0, *reversed(range(1, size))]


def exchange(value, axis, size, k):
    return lax.ppermute(value, axis, [(i, i ^ k) for i in range(size)])


def inner_kernel(packed, inner):
    tokens = packed.shape[1]
    clean, corrupt, grad = [packed[a].astype(jnp.float32) for a in range(3)]
    part = jnp.sum((corrupt - clean) * grad, axis=1, keepdims=True)
    inner[pl.ds(0, tokens), :] = jnp.broadcast_to(part, (tokens, LANES))


def inner_products(packed):
    vmem = pl.BlockSpec(memory_space=pltpu.VMEM)
    return pl.pallas_call(
        inner_kernel,
        out_shape=jax.ShapeDtypeStruct((TILE, LANES), jnp.float32),
        in_specs=[vmem],
        out_specs=vmem,
        compiler_params=pltpu.CompilerParams(vmem_limit_bytes=4 * 2**20),
        name="inner_products",
    )(packed)


def load_kernel(pieces, *refs):
    count = (len(refs) - 2) // 2
    sems = refs[-1]
    copies = []
    for i in range(count):
        source, target = refs[1 + i], refs[1 + count + i]
        count_here = min(pieces, source.shape[0] // 16) or 1
        step = source.shape[0] // count_here
        for j in range(count_here):
            part = pl.ds(j * step, step)
            copies.append(
                pltpu.make_async_copy(source.at[part], target.at[part], sems.at[i, j])
            )
    for copy in copies:
        copy.start()
    for copy in copies:
        copy.wait()


def load(after, *arrays, pieces=16):
    size = sum(array.size * array.dtype.itemsize for array in arrays)
    return pl.pallas_call(
        functools.partial(load_kernel, pieces),
        out_shape=[jax.ShapeDtypeStruct(array.shape, array.dtype) for array in arrays],
        in_specs=[pl.BlockSpec(memory_space=pltpu.VMEM)]
        + [pl.BlockSpec(memory_space=pltpu.HBM)] * len(arrays),
        out_specs=[pl.BlockSpec(memory_space=pltpu.VMEM)] * len(arrays),
        scratch_shapes=[pltpu.SemaphoreType.DMA((len(arrays), pieces))],
        compiler_params=pltpu.CompilerParams(vmem_limit_bytes=48 * 2**20),
        cost_estimate=pl.CostEstimate(flops=0, bytes_accessed=2 * size, transcendentals=0),
        name="load_weights",
    )(after, *arrays)


def product_kernel(groups, parts, *refs):
    blocks = refs[:groups]
    enc, dec = refs[groups : groups + 2]
    outs = refs[groups + 2 : groups + 2 + parts]
    rows, held = refs[groups + 2 + parts :]
    tokens = blocks[0].shape[1]
    total = groups * tokens
    share = LANES
    for k, block in enumerate(blocks):
        for a in range(3):
            rows[pl.ds(a * total + k * tokens, tokens), :] = block[a].astype(jnp.float32)
    encoded = jnp.dot(
        rows[pl.ds(0, 2 * total), :].astype(jnp.bfloat16),
        enc[...],
        preferred_element_type=jnp.float32,
    )
    projected = lax.dot_general(
        rows[pl.ds(2 * total, total), :].astype(jnp.bfloat16),
        dec[...],
        (((1,), (1,)), ((), ())),
        preferred_element_type=jnp.float32,
    )
    for c in range(parts):
        held[c, pl.ds(0, 2 * total), :] = encoded[:, c * share : (c + 1) * share]
        held[c, pl.ds(2 * total, total), :] = projected[:, c * share : (c + 1) * share]
    me = lax.axis_index("tensor")
    for m, out in enumerate(outs):
        out[...] = held[me ^ m]


def products(parts, blocks, enc_weight, dec_weight):
    groups = len(blocks)
    _, tokens, width = blocks[0].shape
    features = enc_weight.shape[1]
    rows = 3 * groups * tokens
    part = jax.ShapeDtypeStruct((rows, features // parts), jnp.float32)
    vmem = pl.BlockSpec(memory_space=pltpu.VMEM)
    return pl.pallas_call(
        functools.partial(product_kernel, groups, parts),
        out_shape=[part] * parts,
        in_specs=[vmem] * (groups + 2),
        out_specs=[vmem] * parts,
        scratch_shapes=[
            pltpu.VMEM((rows, width), jnp.float32),
            pltpu.VMEM((parts, rows, features // parts), jnp.float32),
        ],
        compiler_params=pltpu.CompilerParams(vmem_limit_bytes=48 * 2**20),
        name="products",
    )(*blocks, enc_weight, dec_weight)


def add_up(values):
    while len(values) > 1:
        values = [a + b for a, b in zip(values[::2], values[1::2])]
    return values[0]


def attribution_kernel(sizes, *refs):
    sections, feats, parts = sizes
    groups = sections * feats
    terms = [refs[far_first(parts).index(m)] for m in range(parts)]
    bias, inner, sums = refs[parts:]
    total = terms[0].shape[0] // 3
    tokens = total // groups
    preact = add_up([term[...] for term in terms])
    section, feat = lax.axis_index("section"), lax.axis_index("feat")
    b = bias[pl.ds(lax.axis_index("tensor"), 1), :]
    act_clean = jnp.maximum(preact[:total] + b, 0.0)
    act_corrupt = jnp.maximum(preact[total : 2 * total] + b, 0.0)
    attribution = (act_corrupt - act_clean) * preact[2 * total :]

    devices = groups * parts
    feature_part = jnp.sum(attribution, axis=0, keepdims=True)
    sums[:, 0, :] = jnp.broadcast_to(feature_part, (devices, LANES))
    token_part = jnp.sum(attribution, axis=1, keepdims=True)
    lane = lax.broadcasted_iota(jnp.int32, (tokens, LANES), 1)
    place = lane == lax.broadcasted_iota(jnp.int32, (tokens, LANES), 0)
    for p in range(feats):
        for i, q in enumerate(far_first(sections)):
            k = p * sections + i
            column = jnp.broadcast_to(token_part[k * tokens : (k + 1) * tokens], (tokens, LANES))
            if k == 0:
                column = column - inner[pl.ds(0, tokens), :]
            row = jnp.sum(jnp.where(place, column, 0.0), axis=0, keepdims=True)
            owner = (section ^ q) * feats + (feat ^ p)
            sums[pl.ds(owner * parts, parts), 1, :] = jnp.broadcast_to(row, (parts, LANES))


def attributions(sizes, terms, bias, inner):
    sections, feats, parts = sizes
    vmem = pl.BlockSpec(memory_space=pltpu.VMEM)
    return pl.pallas_call(
        functools.partial(attribution_kernel, sizes),
        out_shape=jax.ShapeDtypeStruct((sections * feats * parts, 2, LANES), jnp.float32),
        in_specs=[vmem] * (parts + 2),
        out_specs=vmem,
        compiler_params=pltpu.CompilerParams(vmem_limit_bytes=16 * 2**20),
        name="attributions",
    )(*terms, bias, inner)


def final_kernel(sizes, arrived, feature_out, error_out, features, errors, sems):
    sections, feats, parts = sizes
    group = lax.axis_index("section") * feats + lax.axis_index("feat")
    mine = arrived[pl.ds(group * parts, parts), 0, :]
    for i in range(parts):
        features[pl.ds(i * LANES, LANES)] = mine[i]
    feature_copy = pltpu.make_async_copy(features, feature_out, sems.at[0])
    feature_copy.start()
    owed = add_up([arrived[i, 1:2, :] for i in range(sections * feats * parts)])
    errors[...] = -owed[0, : errors.shape[0]]
    error_copy = pltpu.make_async_copy(errors, error_out, sems.at[1])
    error_copy.start()
    feature_copy.wait()
    error_copy.wait()


def final(sizes, tokens, arrived):
    features = (sizes[2] * LANES,)
    return pl.pallas_call(
        functools.partial(final_kernel, sizes),
        out_shape=[
            jax.ShapeDtypeStruct(features, jnp.float32),
            jax.ShapeDtypeStruct((tokens,), jnp.float32),
        ],
        in_specs=[pl.BlockSpec(memory_space=pltpu.VMEM)],
        out_specs=[pl.BlockSpec(memory_space=pltpu.HBM)] * 2,
        scratch_shapes=[
            pltpu.VMEM(features, jnp.float32),
            pltpu.VMEM((tokens,), jnp.float32),
            pltpu.SemaphoreType.DMA((2,)),
        ],
        compiler_params=pltpu.CompilerParams(vmem_limit_bytes=4 * 2**20),
        name="final",
    )(arrived)


def per_device(sizes, clean_resid, corrupt_resid, metric_grad, enc_weight, enc_bias, dec_weight):
    sections, feats, parts = sizes
    tokens = clean_resid.shape[0]
    features = enc_weight.shape[1]

    packed = jnp.stack([clean_resid, corrupt_resid, metric_grad])
    near = [packed] + [exchange(packed, "section", sections, q) for q in far_first(sections)[1:]]
    inner = inner_products(packed)
    bias = enc_bias.reshape(parts, features // parts)
    enc_weight, dec_weight = load(packed, enc_weight, dec_weight)
    far = []
    for p in range(1, feats):
        for block in near:
            if block is packed:
                block, _ = lax.optimization_barrier((block, enc_weight))
            far.append(exchange(block, "feat", feats, p))
    blocks = near + far

    terms = products(parts, blocks, enc_weight, dec_weight)
    arrived = [exchange(terms[m], "tensor", parts, m) for m in far_first(parts)[1:]]
    sums = attributions(sizes, [terms[0]] + arrived, bias, inner)
    return tuple(final(sizes, tokens, lax.all_to_all(sums, EVERY, 0, 0)))


def solution(mesh):
    sizes = [mesh.shape[name] for name in ("section", "feat", "tensor")]
    in_specs = (
        P(("section", "feat"), "tensor"),
        P(("section", "feat"), "tensor"),
        P(("section", "feat"), "tensor"),
        P("tensor", ("section", "feat")),
        P(("section", "feat")),
        P(("section", "feat"), "tensor"),
    )
    out_specs = (P(("section", "feat")), P(("section", "feat")))
    return jax.shard_map(
        functools.partial(per_device, sizes),
        mesh=mesh,
        in_specs=in_specs,
        out_specs=out_specs,
        check_vma=False,
    )
```

```python
import functools

import jax
import jax.numpy as jnp
from jax import lax
from jax.experimental import pallas as pl
from jax.experimental.pallas import tpu as pltpu
from jax.sharding import PartitionSpec as P

LANES = 128
TILE = 8


EVERY = ("section", "feat", "tensor")


def far_first(size):
    return [0, *reversed(range(1, size))]


def exchange(value, axis, size, k):
    return lax.ppermute(value, axis, [(i, i ^ k) for i in range(size)])


def inner_kernel(packed, inner):
    tokens = packed.shape[1]
    clean, corrupt, grad = [packed[a].astype(jnp.float32) for a in range(3)]
    part = jnp.sum((corrupt - clean) * grad, axis=1, keepdims=True)
    inner[pl.ds(0, tokens), :] = jnp.broadcast_to(part, (tokens, LANES))


def inner_products(packed):
    vmem = pl.BlockSpec(memory_space=pltpu.VMEM)
    return pl.pallas_call(
        inner_kernel,
        out_shape=jax.ShapeDtypeStruct((TILE, LANES), jnp.float32),
        in_specs=[vmem],
        out_specs=vmem,
        compiler_params=pltpu.CompilerParams(vmem_limit_bytes=4 * 2**20),
        cost_estimate=pl.CostEstimate(flops=2**32, bytes_accessed=2**24, transcendentals=0),
        name="inner_products",
    )(packed)


def inner_kernel(packed, inner):
    tokens = packed.shape[1]
    clean, corrupt, grad = [packed[a].astype(jnp.float32) for a in range(3)]
    part = jnp.sum((corrupt - clean) * grad, axis=1, keepdims=True)
    inner[pl.ds(0, tokens), :] = jnp.broadcast_to(part, (tokens, LANES))


def inner_products(packed):
    vmem = pl.BlockSpec(memory_space=pltpu.VMEM)
    return pl.pallas_call(
        inner_kernel,
        out_shape=jax.ShapeDtypeStruct((TILE, LANES), jnp.float32),
        in_specs=[vmem],
        out_specs=vmem,
        compiler_params=pltpu.CompilerParams(vmem_limit_bytes=4 * 2**20),
        cost_estimate=pl.CostEstimate(flops=2**32, bytes_accessed=2**24, transcendentals=0),
        name="inner_products",
    )(packed)


def load_kernel(pieces, *refs):
    count = (len(refs) - 2) // 2
    sems = refs[-1]
    copies = []
    for i in range(count):
        source, target = refs[1 + i], refs[1 + count + i]
        count_here = min(pieces, source.shape[0] // 16) or 1
        step = source.shape[0] // count_here
        for j in range(count_here):
            part = pl.ds(j * step, step)
            copies.append(
                pltpu.make_async_copy(source.at[part], target.at[part], sems.at[i, j])
            )
    for copy in copies:
        copy.start()
    for copy in copies:
        copy.wait()


def load(after, *arrays, pieces=4):
    size = sum(array.size * array.dtype.itemsize for array in arrays)
    return pl.pallas_call(
        functools.partial(load_kernel, pieces),
        out_shape=[jax.ShapeDtypeStruct(array.shape, array.dtype) for array in arrays],
        in_specs=[pl.BlockSpec(memory_space=pltpu.VMEM)]
        + [pl.BlockSpec(memory_space=pltpu.HBM)] * len(arrays),
        out_specs=[pl.BlockSpec(memory_space=pltpu.VMEM)] * len(arrays),
        scratch_shapes=[pltpu.SemaphoreType.DMA((len(arrays), pieces))],
        compiler_params=pltpu.CompilerParams(vmem_limit_bytes=16 * 2**20),
        cost_estimate=pl.CostEstimate(flops=0, bytes_accessed=2 * size, transcendentals=0),
        name="load_weights",
    )(after, *arrays)


def product_kernel(groups, parts, *refs):
    blocks = refs[:groups]
    enc, dec = refs[groups : groups + 2]
    outs = refs[groups + 2 : groups + 2 + parts]
    rows, held = refs[groups + 2 + parts :]
    tokens = blocks[0].shape[1]
    total = groups * tokens
    share = LANES
    for k, block in enumerate(blocks):
        for a in range(3):
            rows[pl.ds(a * total + k * tokens, tokens), :] = block[a].astype(jnp.float32)
    encoded = jnp.dot(
        rows[pl.ds(0, 2 * total), :].astype(jnp.bfloat16),
        enc[...],
        preferred_element_type=jnp.float32,
    )
    projected = lax.dot_general(
        rows[pl.ds(2 * total, total), :].astype(jnp.bfloat16),
        dec[...],
        (((1,), (1,)), ((), ())),
        preferred_element_type=jnp.float32,
    )
    for c in range(parts):
        held[c, pl.ds(0, 2 * total), :] = encoded[:, c * share : (c + 1) * share]
        held[c, pl.ds(2 * total, total), :] = projected[:, c * share : (c + 1) * share]
    me = lax.axis_index("tensor")
    for m, out in enumerate(outs):
        out[...] = held[me ^ m]


def products(parts, blocks, enc_weight, dec_weight):
    groups = len(blocks)
    _, tokens, width = blocks[0].shape
    features = enc_weight.shape[1]
    rows = 3 * groups * tokens
    part = jax.ShapeDtypeStruct((rows, features // parts), jnp.float32)
    vmem = pl.BlockSpec(memory_space=pltpu.VMEM)
    return pl.pallas_call(
        functools.partial(product_kernel, groups, parts),
        out_shape=[part] * parts,
        in_specs=[vmem] * (groups + 2),
        out_specs=[vmem] * parts,
        scratch_shapes=[
            pltpu.VMEM((rows, width), jnp.float32),
            pltpu.VMEM((parts, rows, features // parts), jnp.float32),
        ],
        compiler_params=pltpu.CompilerParams(vmem_limit_bytes=48 * 2**20),
        name="products",
    )(*blocks, enc_weight, dec_weight)


def add_up(values):
    while len(values) > 1:
        values = [a + b for a, b in zip(values[::2], values[1::2])]
    return values[0]


def attribution_kernel(sizes, *refs):
    sections, feats, parts = sizes
    groups = sections * feats
    terms = [refs[far_first(parts).index(m)] for m in range(parts)]
    bias, inner, sums = refs[parts:]
    total = terms[0].shape[0] // 3
    tokens = total // groups
    preact = add_up([term[...] for term in terms])
    section, feat = lax.axis_index("section"), lax.axis_index("feat")
    b = bias[pl.ds(lax.axis_index("tensor"), 1), :]
    act_clean = jnp.maximum(preact[:total] + b, 0.0)
    act_corrupt = jnp.maximum(preact[total : 2 * total] + b, 0.0)
    attribution = (act_corrupt - act_clean) * preact[2 * total :]

    devices = groups * parts
    feature_part = jnp.sum(attribution, axis=0, keepdims=True)
    sums[:, 0, :] = jnp.broadcast_to(feature_part, (devices, LANES))
    token_part = jnp.sum(attribution, axis=1, keepdims=True)
    lane = lax.broadcasted_iota(jnp.int32, (tokens, LANES), 1)
    place = lane == lax.broadcasted_iota(jnp.int32, (tokens, LANES), 0)
    for p in range(feats):
        for q in range(sections):
            k = p * sections + q
            column = jnp.broadcast_to(token_part[k * tokens : (k + 1) * tokens], (tokens, LANES))
            if k == 0:
                column = column - inner[pl.ds(0, tokens), :]
            row = jnp.sum(jnp.where(place, column, 0.0), axis=0, keepdims=True)
            owner = (section ^ q) * feats + (feat ^ p)
            sums[pl.ds(owner * parts, parts), 1, :] = jnp.broadcast_to(row, (parts, LANES))


def attributions(sizes, terms, bias, inner):
    sections, feats, parts = sizes
    vmem = pl.BlockSpec(memory_space=pltpu.VMEM)
    return pl.pallas_call(
        functools.partial(attribution_kernel, sizes),
        out_shape=jax.ShapeDtypeStruct((sections * feats * parts, 2, LANES), jnp.float32),
        in_specs=[vmem] * (parts + 2),
        out_specs=vmem,
        compiler_params=pltpu.CompilerParams(vmem_limit_bytes=16 * 2**20),
        name="attributions",
    )(*terms, bias, inner)


def final_kernel(sizes, arrived, feature_out, error_out, features, errors, sems):
    sections, feats, parts = sizes
    group = lax.axis_index("section") * feats + lax.axis_index("feat")
    mine = arrived[pl.ds(group * parts, parts), 0, :]
    for i in range(parts):
        features[pl.ds(i * LANES, LANES)] = mine[i]
    feature_copy = pltpu.make_async_copy(features, feature_out, sems.at[0])
    feature_copy.start()
    owed = add_up([arrived[i, 1:2, :] for i in range(sections * feats * parts)])
    errors[...] = -owed[0, : errors.shape[0]]
    error_copy = pltpu.make_async_copy(errors, error_out, sems.at[1])
    error_copy.start()
    feature_copy.wait()
    error_copy.wait()


def final(sizes, tokens, arrived):
    features = (sizes[2] * LANES,)
    return pl.pallas_call(
        functools.partial(final_kernel, sizes),
        out_shape=[
            jax.ShapeDtypeStruct(features, jnp.float32),
            jax.ShapeDtypeStruct((tokens,), jnp.float32),
        ],
        in_specs=[pl.BlockSpec(memory_space=pltpu.VMEM)],
        out_specs=[pl.BlockSpec(memory_space=pltpu.HBM)] * 2,
        scratch_shapes=[
            pltpu.VMEM(features, jnp.float32),
            pltpu.VMEM((tokens,), jnp.float32),
            pltpu.SemaphoreType.DMA((2,)),
        ],
        compiler_params=pltpu.CompilerParams(vmem_limit_bytes=4 * 2**20),
        name="final",
    )(arrived)


def per_device(sizes, clean_resid, corrupt_resid, metric_grad, enc_weight, enc_bias, dec_weight):
    sections, feats, parts = sizes
    tokens = clean_resid.shape[0]
    features = enc_weight.shape[1]

    packed = jnp.stack([clean_resid, corrupt_resid, metric_grad])
    near = [packed] + [exchange(packed, "section", sections, q) for q in range(1, sections)]
    inner = inner_products(packed)
    bias = enc_bias.reshape(parts, features // parts)
    far = []
    for p in range(1, feats):
        for block in near:
            if block is packed:
                block, inner = lax.optimization_barrier((block, inner))
            far.append(exchange(block, "feat", feats, p))
    blocks = near + far

    terms = products(parts, blocks, enc_weight, dec_weight)
    arrived = [exchange(terms[m], "tensor", parts, m) for m in far_first(parts)[1:]]
    sums = attributions(sizes, [terms[0]] + arrived, bias, inner)
    return tuple(final(sizes, tokens, lax.all_to_all(sums, EVERY, 0, 0)))


def solution(mesh):
    sizes = [mesh.shape[name] for name in ("section", "feat", "tensor")]
    in_specs = (
        P(("section", "feat"), "tensor"),
        P(("section", "feat"), "tensor"),
        P(("section", "feat"), "tensor"),
        P("tensor", ("section", "feat")),
        P(("section", "feat")),
        P(("section", "feat"), "tensor"),
    )
    out_specs = (P(("section", "feat")), P(("section", "feat")))
    return jax.shard_map(
        functools.partial(per_device, sizes),
        mesh=mesh,
        in_specs=in_specs,
        out_specs=out_specs,
        check_vma=False,
    )
```

```python
import functools

import jax
import jax.numpy as jnp
from jax import lax
from jax.experimental import pallas as pl
from jax.experimental.pallas import tpu as pltpu
from jax.sharding import PartitionSpec as P

LANES = 128
TILE = 8


EVERY = ("section", "feat", "tensor")


def far_first(size):
    return [0, *reversed(range(1, size))]


def exchange(value, axis, size, k):
    return lax.ppermute(value, axis, [(i, i ^ k) for i in range(size)])


def inner_kernel(packed, inner):
    tokens = packed.shape[1]
    clean, corrupt, grad = [packed[a].astype(jnp.float32) for a in range(3)]
    part = jnp.sum((corrupt - clean) * grad, axis=1, keepdims=True)
    inner[pl.ds(0, tokens), :] = jnp.broadcast_to(part, (tokens, LANES))


def inner_products(packed):
    vmem = pl.BlockSpec(memory_space=pltpu.VMEM)
    return pl.pallas_call(
        inner_kernel,
        out_shape=jax.ShapeDtypeStruct((TILE, LANES), jnp.float32),
        in_specs=[vmem],
        out_specs=vmem,
        compiler_params=pltpu.CompilerParams(vmem_limit_bytes=4 * 2**20),
        cost_estimate=pl.CostEstimate(flops=2**32, bytes_accessed=2**24, transcendentals=0),
        name="inner_products",
    )(packed)


def inner_kernel(packed, inner):
    tokens = packed.shape[1]
    clean, corrupt, grad = [packed[a].astype(jnp.float32) for a in range(3)]
    part = jnp.sum((corrupt - clean) * grad, axis=1, keepdims=True)
    inner[pl.ds(0, tokens), :] = jnp.broadcast_to(part, (tokens, LANES))


def inner_products(packed):
    vmem = pl.BlockSpec(memory_space=pltpu.VMEM)
    return pl.pallas_call(
        inner_kernel,
        out_shape=jax.ShapeDtypeStruct((TILE, LANES), jnp.float32),
        in_specs=[vmem],
        out_specs=vmem,
        compiler_params=pltpu.CompilerParams(vmem_limit_bytes=4 * 2**20),
        cost_estimate=pl.CostEstimate(flops=2**32, bytes_accessed=2**24, transcendentals=0),
        name="inner_products",
    )(packed)


def load_kernel(pieces, *refs):
    count = (len(refs) - 2) // 2
    sems = refs[-1]
    copies = []
    for i in range(count):
        source, target = refs[1 + i], refs[1 + count + i]
        count_here = min(pieces, source.shape[0] // 16) or 1
        step = source.shape[0] // count_here
        for j in range(count_here):
            part = pl.ds(j * step, step)
            copies.append(
                pltpu.make_async_copy(source.at[part], target.at[part], sems.at[i, j])
            )
    for copy in copies:
        copy.start()
    for copy in copies:
        copy.wait()


def load(after, *arrays, pieces=4):
    size = sum(array.size * array.dtype.itemsize for array in arrays)
    return pl.pallas_call(
        functools.partial(load_kernel, pieces),
        out_shape=[jax.ShapeDtypeStruct(array.shape, array.dtype) for array in arrays],
        in_specs=[pl.BlockSpec(memory_space=pltpu.VMEM)]
        + [pl.BlockSpec(memory_space=pltpu.HBM)] * len(arrays),
        out_specs=[pl.BlockSpec(memory_space=pltpu.VMEM)] * len(arrays),
        scratch_shapes=[pltpu.SemaphoreType.DMA((len(arrays), pieces))],
        compiler_params=pltpu.CompilerParams(vmem_limit_bytes=16 * 2**20),
        cost_estimate=pl.CostEstimate(flops=0, bytes_accessed=2 * size, transcendentals=0),
        name="load_weights",
    )(after, *arrays)


def product_kernel(groups, parts, *refs):
    blocks = refs[:groups]
    enc, dec = refs[groups : groups + 2]
    outs = refs[groups + 2 : groups + 2 + parts]
    rows, held = refs[groups + 2 + parts :]
    tokens = blocks[0].shape[1]
    total = groups * tokens
    share = LANES
    for k, block in enumerate(blocks):
        for a in range(3):
            rows[pl.ds(a * total + k * tokens, tokens), :] = block[a].astype(jnp.float32)
    encoded = jnp.dot(
        rows[pl.ds(0, 2 * total), :].astype(jnp.bfloat16),
        enc[...],
        preferred_element_type=jnp.float32,
    )
    projected = lax.dot_general(
        rows[pl.ds(2 * total, total), :].astype(jnp.bfloat16),
        dec[...],
        (((1,), (1,)), ((), ())),
        preferred_element_type=jnp.float32,
    )
    for c in range(parts):
        held[c, pl.ds(0, 2 * total), :] = encoded[:, c * share : (c + 1) * share]
        held[c, pl.ds(2 * total, total), :] = projected[:, c * share : (c + 1) * share]
    me = lax.axis_index("tensor")
    for m, out in enumerate(outs):
        out[...] = held[me ^ m]


def products(parts, blocks, enc_weight, dec_weight):
    groups = len(blocks)
    _, tokens, width = blocks[0].shape
    features = enc_weight.shape[1]
    rows = 3 * groups * tokens
    part = jax.ShapeDtypeStruct((rows, features // parts), jnp.float32)
    vmem = pl.BlockSpec(memory_space=pltpu.VMEM)
    return pl.pallas_call(
        functools.partial(product_kernel, groups, parts),
        out_shape=[part] * parts,
        in_specs=[vmem] * (groups + 2),
        out_specs=[vmem] * parts,
        scratch_shapes=[
            pltpu.VMEM((rows, width), jnp.float32),
            pltpu.VMEM((parts, rows, features // parts), jnp.float32),
        ],
        compiler_params=pltpu.CompilerParams(vmem_limit_bytes=48 * 2**20),
        name="products",
    )(*blocks, enc_weight, dec_weight)


def add_up(values):
    while len(values) > 1:
        values = [a + b for a, b in zip(values[::2], values[1::2])]
    return values[0]


def attribution_kernel(sizes, *refs):
    sections, feats, parts = sizes
    groups = sections * feats
    terms = [refs[far_first(parts).index(m)] for m in range(parts)]
    bias, inner, sums = refs[parts:]
    total = terms[0].shape[0] // 3
    tokens = total // groups
    preact = add_up([term[...] for term in terms])
    section, feat = lax.axis_index("section"), lax.axis_index("feat")
    b = bias[pl.ds(lax.axis_index("tensor"), 1), :]
    act_clean = jnp.maximum(preact[:total] + b, 0.0)
    act_corrupt = jnp.maximum(preact[total : 2 * total] + b, 0.0)
    attribution = (act_corrupt - act_clean) * preact[2 * total :]

    devices = groups * parts
    feature_part = jnp.sum(attribution, axis=0, keepdims=True)
    sums[:, 0, :] = jnp.broadcast_to(feature_part, (devices, LANES))
    token_part = jnp.sum(attribution, axis=1, keepdims=True)
    lane = lax.broadcasted_iota(jnp.int32, (tokens, LANES), 1)
    place = lane == lax.broadcasted_iota(jnp.int32, (tokens, LANES), 0)
    for p in range(feats):
        for q in range(sections):
            k = p * sections + q
            column = jnp.broadcast_to(token_part[k * tokens : (k + 1) * tokens], (tokens, LANES))
            if k == 0:
                column = column - inner[pl.ds(0, tokens), :]
            row = jnp.sum(jnp.where(place, column, 0.0), axis=0, keepdims=True)
            owner = (section ^ q) * feats + (feat ^ p)
            sums[pl.ds((groups - 1 - owner) * parts, parts), 1, :] = jnp.broadcast_to(row, (parts, LANES))


def attributions(sizes, terms, bias, inner):
    sections, feats, parts = sizes
    vmem = pl.BlockSpec(memory_space=pltpu.VMEM)
    return pl.pallas_call(
        functools.partial(attribution_kernel, sizes),
        out_shape=jax.ShapeDtypeStruct((sections * feats * parts, 2, LANES), jnp.float32),
        in_specs=[vmem] * (parts + 2),
        out_specs=vmem,
        compiler_params=pltpu.CompilerParams(vmem_limit_bytes=16 * 2**20),
        name="attributions",
    )(*terms, bias, inner)


def final_kernel(sizes, arrived, feature_out, error_out, features, errors, sems):
    sections, feats, parts = sizes
    group = lax.axis_index("section") * feats + lax.axis_index("feat")
    mine = arrived[pl.ds((sections * feats - 1 - group) * parts, parts), 0, :]
    for i in range(parts):
        features[pl.ds(i * LANES, LANES)] = mine[parts - 1 - i]
    feature_copy = pltpu.make_async_copy(features, feature_out, sems.at[0])
    feature_copy.start()
    owed = add_up([arrived[i, 1:2, :] for i in range(sections * feats * parts)])
    errors[...] = -owed[0, : errors.shape[0]]
    error_copy = pltpu.make_async_copy(errors, error_out, sems.at[1])
    error_copy.start()
    feature_copy.wait()
    error_copy.wait()


def final(sizes, tokens, arrived):
    features = (sizes[2] * LANES,)
    return pl.pallas_call(
        functools.partial(final_kernel, sizes),
        out_shape=[
            jax.ShapeDtypeStruct(features, jnp.float32),
            jax.ShapeDtypeStruct((tokens,), jnp.float32),
        ],
        in_specs=[pl.BlockSpec(memory_space=pltpu.VMEM)],
        out_specs=[pl.BlockSpec(memory_space=pltpu.HBM)] * 2,
        scratch_shapes=[
            pltpu.VMEM(features, jnp.float32),
            pltpu.VMEM((tokens,), jnp.float32),
            pltpu.SemaphoreType.DMA((2,)),
        ],
        compiler_params=pltpu.CompilerParams(vmem_limit_bytes=4 * 2**20),
        name="final",
    )(arrived)


def per_device(sizes, clean_resid, corrupt_resid, metric_grad, enc_weight, enc_bias, dec_weight):
    sections, feats, parts = sizes
    tokens = clean_resid.shape[0]
    features = enc_weight.shape[1]

    packed = jnp.stack([clean_resid, corrupt_resid, metric_grad])
    near = [packed] + [exchange(packed, "section", sections, q) for q in range(1, sections)]
    inner = inner_products(packed)
    bias = enc_bias.reshape(parts, features // parts)
    far = []
    for p in range(1, feats):
        for block in near:
            if block is packed:
                block, inner = lax.optimization_barrier((block, inner))
            far.append(exchange(block, "feat", feats, p))
    blocks = near + far

    terms = products(parts, blocks, enc_weight, dec_weight)
    arrived = [exchange(terms[m], "tensor", parts, m) for m in far_first(parts)[1:]]
    sums = attributions(sizes, [terms[0]] + arrived, bias, inner)
    far_end = [list(reversed(range(sections * feats * parts)))]
    arrived = lax.all_to_all(sums, EVERY, 0, 0, axis_index_groups=far_end)
    return tuple(final(sizes, tokens, arrived))


def solution(mesh):
    sizes = [mesh.shape[name] for name in ("section", "feat", "tensor")]
    in_specs = (
        P(("section", "feat"), "tensor"),
        P(("section", "feat"), "tensor"),
        P(("section", "feat"), "tensor"),
        P("tensor", ("section", "feat")),
        P(("section", "feat")),
        P(("section", "feat"), "tensor"),
    )
    out_specs = (P(("section", "feat")), P(("section", "feat")))
    return jax.shard_map(
        functools.partial(per_device, sizes),
        mesh=mesh,
        in_specs=in_specs,
        out_specs=out_specs,
        check_vma=False,
    )
```

```python
import functools

import jax
import jax.numpy as jnp
from jax import lax
from jax.experimental import pallas as pl
from jax.experimental.pallas import tpu as pltpu
from jax.sharding import PartitionSpec as P

LANES = 128
TILE = 8


EVERY = ("section", "feat", "tensor")


def far_first(size):
    return [0, *reversed(range(1, size))]


def row_blocks(sections, feats):
    places = [(p, q) for p in range(feats) for q in range(sections)]
    return sorted(places, key=lambda place: (place[0] > 0 and place[1] != 1, place[1], place[0]))


def exchange(value, axis, size, k):
    return lax.ppermute(value, axis, [(i, i ^ k) for i in range(size)])


def inner_kernel(packed, inner):
    tokens = packed.shape[1]
    clean, corrupt, grad = [packed[a].astype(jnp.float32) for a in range(3)]
    part = jnp.sum((corrupt - clean) * grad, axis=1, keepdims=True)
    inner[pl.ds(0, tokens), :] = jnp.broadcast_to(part, (tokens, LANES))


def inner_products(packed):
    vmem = pl.BlockSpec(memory_space=pltpu.VMEM)
    return pl.pallas_call(
        inner_kernel,
        out_shape=jax.ShapeDtypeStruct((TILE, LANES), jnp.float32),
        in_specs=[vmem],
        out_specs=vmem,
        compiler_params=pltpu.CompilerParams(vmem_limit_bytes=4 * 2**20),
        cost_estimate=pl.CostEstimate(flops=2**32, bytes_accessed=2**24, transcendentals=0),
        name="inner_products",
    )(packed)


def inner_kernel(packed, inner):
    tokens = packed.shape[1]
    clean, corrupt, grad = [packed[a].astype(jnp.float32) for a in range(3)]
    part = jnp.sum((corrupt - clean) * grad, axis=1, keepdims=True)
    inner[pl.ds(0, tokens), :] = jnp.broadcast_to(part, (tokens, LANES))


def inner_products(packed):
    vmem = pl.BlockSpec(memory_space=pltpu.VMEM)
    return pl.pallas_call(
        inner_kernel,
        out_shape=jax.ShapeDtypeStruct((TILE, LANES), jnp.float32),
        in_specs=[vmem],
        out_specs=vmem,
        compiler_params=pltpu.CompilerParams(vmem_limit_bytes=4 * 2**20),
        cost_estimate=pl.CostEstimate(flops=2**32, bytes_accessed=2**24, transcendentals=0),
        name="inner_products",
    )(packed)


def load_kernel(pieces, *refs):
    count = (len(refs) - 2) // 2
    sems = refs[-1]
    copies = []
    for i in range(count):
        source, target = refs[1 + i], refs[1 + count + i]
        count_here = min(pieces, source.shape[0] // 16) or 1
        step = source.shape[0] // count_here
        for j in range(count_here):
            part = pl.ds(j * step, step)
            copies.append(
                pltpu.make_async_copy(source.at[part], target.at[part], sems.at[i, j])
            )
    for copy in copies:
        copy.start()
    for copy in copies:
        copy.wait()


def load(after, *arrays, pieces=4):
    size = sum(array.size * array.dtype.itemsize for array in arrays)
    return pl.pallas_call(
        functools.partial(load_kernel, pieces),
        out_shape=[jax.ShapeDtypeStruct(array.shape, array.dtype) for array in arrays],
        in_specs=[pl.BlockSpec(memory_space=pltpu.VMEM)]
        + [pl.BlockSpec(memory_space=pltpu.HBM)] * len(arrays),
        out_specs=[pl.BlockSpec(memory_space=pltpu.VMEM)] * len(arrays),
        scratch_shapes=[pltpu.SemaphoreType.DMA((len(arrays), pieces))],
        compiler_params=pltpu.CompilerParams(vmem_limit_bytes=16 * 2**20),
        cost_estimate=pl.CostEstimate(flops=0, bytes_accessed=2 * size, transcendentals=0),
        name="load_weights",
    )(after, *arrays)


def product_kernel(groups, parts, *refs):
    blocks = refs[:groups]
    enc, dec = refs[groups : groups + 2]
    outs = refs[groups + 2 : groups + 2 + parts]
    rows, held = refs[groups + 2 + parts :]
    tokens = blocks[0].shape[1]
    total = groups * tokens
    share = LANES
    for k, block in enumerate(blocks):
        for a in range(3):
            rows[pl.ds(a * total + k * tokens, tokens), :] = block[a].astype(jnp.float32)
    encoded = jnp.dot(
        rows[pl.ds(0, 2 * total), :].astype(jnp.bfloat16),
        enc[...],
        preferred_element_type=jnp.float32,
    )
    projected = lax.dot_general(
        rows[pl.ds(2 * total, total), :].astype(jnp.bfloat16),
        dec[...],
        (((1,), (1,)), ((), ())),
        preferred_element_type=jnp.float32,
    )
    for c in range(parts):
        held[c, pl.ds(0, 2 * total), :] = encoded[:, c * share : (c + 1) * share]
        held[c, pl.ds(2 * total, total), :] = projected[:, c * share : (c + 1) * share]
    me = lax.axis_index("tensor")
    for m, out in enumerate(outs):
        out[...] = held[me ^ m]


def products(parts, blocks, enc_weight, dec_weight):
    groups = len(blocks)
    _, tokens, width = blocks[0].shape
    features = enc_weight.shape[1]
    rows = 3 * groups * tokens
    part = jax.ShapeDtypeStruct((rows, features // parts), jnp.float32)
    vmem = pl.BlockSpec(memory_space=pltpu.VMEM)
    return pl.pallas_call(
        functools.partial(product_kernel, groups, parts),
        out_shape=[part] * parts,
        in_specs=[vmem] * (groups + 2),
        out_specs=[vmem] * parts,
        scratch_shapes=[
            pltpu.VMEM((rows, width), jnp.float32),
            pltpu.VMEM((parts, rows, features // parts), jnp.float32),
        ],
        compiler_params=pltpu.CompilerParams(vmem_limit_bytes=48 * 2**20),
        name="products",
    )(*blocks, enc_weight, dec_weight)


def add_up(values):
    while len(values) > 1:
        values = [a + b for a, b in zip(values[::2], values[1::2])]
    return values[0]


def attribution_kernel(sizes, *refs):
    sections, feats, parts = sizes
    groups = sections * feats
    terms = [refs[far_first(parts).index(m)] for m in range(parts)]
    bias, inner, sums = refs[parts:]
    total = terms[0].shape[0] // 3
    tokens = total // groups
    preact = add_up([term[...] for term in terms])
    section, feat = lax.axis_index("section"), lax.axis_index("feat")
    b = bias[pl.ds(lax.axis_index("tensor"), 1), :]
    act_clean = jnp.maximum(preact[:total] + b, 0.0)
    act_corrupt = jnp.maximum(preact[total : 2 * total] + b, 0.0)
    attribution = (act_corrupt - act_clean) * preact[2 * total :]

    devices = groups * parts
    feature_part = jnp.sum(attribution, axis=0, keepdims=True)
    sums[:, 0, :] = jnp.broadcast_to(feature_part, (devices, LANES))
    token_part = jnp.sum(attribution, axis=1, keepdims=True)
    lane = lax.broadcasted_iota(jnp.int32, (tokens, LANES), 1)
    place = lane == lax.broadcasted_iota(jnp.int32, (tokens, LANES), 0)
    for k, (p, q) in enumerate(row_blocks(sections, feats)):
        column = jnp.broadcast_to(token_part[k * tokens : (k + 1) * tokens], (tokens, LANES))
        if k == 0:
            column = column - inner[pl.ds(0, tokens), :]
        row = jnp.sum(jnp.where(place, column, 0.0), axis=0, keepdims=True)
        owner = (section ^ q) * feats + (feat ^ p)
        sums[pl.ds(owner * parts, parts), 1, :] = jnp.broadcast_to(row, (parts, LANES))


def attributions(sizes, terms, bias, inner):
    sections, feats, parts = sizes
    vmem = pl.BlockSpec(memory_space=pltpu.VMEM)
    return pl.pallas_call(
        functools.partial(attribution_kernel, sizes),
        out_shape=jax.ShapeDtypeStruct((sections * feats * parts, 2, LANES), jnp.float32),
        in_specs=[vmem] * (parts + 2),
        out_specs=vmem,
        compiler_params=pltpu.CompilerParams(vmem_limit_bytes=16 * 2**20),
        name="attributions",
    )(*terms, bias, inner)


def final_kernel(sizes, arrived, feature_out, error_out, features, errors, sems):
    sections, feats, parts = sizes
    group = lax.axis_index("section") * feats + lax.axis_index("feat")
    mine = arrived[pl.ds(group * parts, parts), 0, :]
    for i in range(parts):
        features[pl.ds(i * LANES, LANES)] = mine[i]
    feature_copy = pltpu.make_async_copy(features, feature_out, sems.at[0])
    feature_copy.start()
    owed = add_up([arrived[i, 1:2, :] for i in range(sections * feats * parts)])
    errors[...] = -owed[0, : errors.shape[0]]
    error_copy = pltpu.make_async_copy(errors, error_out, sems.at[1])
    error_copy.start()
    feature_copy.wait()
    error_copy.wait()


def final(sizes, tokens, arrived):
    features = (sizes[2] * LANES,)
    return pl.pallas_call(
        functools.partial(final_kernel, sizes),
        out_shape=[
            jax.ShapeDtypeStruct(features, jnp.float32),
            jax.ShapeDtypeStruct((tokens,), jnp.float32),
        ],
        in_specs=[pl.BlockSpec(memory_space=pltpu.VMEM)],
        out_specs=[pl.BlockSpec(memory_space=pltpu.HBM)] * 2,
        scratch_shapes=[
            pltpu.VMEM(features, jnp.float32),
            pltpu.VMEM((tokens,), jnp.float32),
            pltpu.SemaphoreType.DMA((2,)),
        ],
        compiler_params=pltpu.CompilerParams(vmem_limit_bytes=4 * 2**20),
        name="final",
    )(arrived)


def per_device(sizes, clean_resid, corrupt_resid, metric_grad, enc_weight, enc_bias, dec_weight):
    sections, feats, parts = sizes
    tokens = clean_resid.shape[0]
    features = enc_weight.shape[1]

    packed = jnp.stack([clean_resid, corrupt_resid, metric_grad])
    inner = inner_products(packed)
    bias = enc_bias.reshape(parts, features // parts)
    held = {(0, 0): packed}
    for p, q in row_blocks(sections, feats):
        if q > 0 and (p == 0 or q == 1):
            pairs = [
                (s * feats + f, (s ^ q) * feats + (f ^ p))
                for s in range(sections)
                for f in range(feats)
            ]
            held[p, q] = lax.ppermute(packed, ("section", "feat"), pairs)
        elif p > 0:
            block = held[0, q]
            if q == 0:
                block, inner = lax.optimization_barrier((block, inner))
            held[p, q] = exchange(block, "feat", feats, p)
    blocks = [held[place] for place in row_blocks(sections, feats)]

    terms = products(parts, blocks, enc_weight, dec_weight)
    arrived = [exchange(terms[m], "tensor", parts, m) for m in far_first(parts)[1:]]
    sums = attributions(sizes, [terms[0]] + arrived, bias, inner)
    return tuple(final(sizes, tokens, lax.all_to_all(sums, EVERY, 0, 0)))


def solution(mesh):
    sizes = [mesh.shape[name] for name in ("section", "feat", "tensor")]
    in_specs = (
        P(("section", "feat"), "tensor"),
        P(("section", "feat"), "tensor"),
        P(("section", "feat"), "tensor"),
        P("tensor", ("section", "feat")),
        P(("section", "feat")),
        P(("section", "feat"), "tensor"),
    )
    out_specs = (P(("section", "feat")), P(("section", "feat")))
    return jax.shard_map(
        functools.partial(per_device, sizes),
        mesh=mesh,
        in_specs=in_specs,
        out_specs=out_specs,
        check_vma=False,
    )
```

```python
import functools

import jax
import jax.numpy as jnp
from jax import lax
from jax.experimental import pallas as pl
from jax.experimental.pallas import tpu as pltpu
from jax.sharding import PartitionSpec as P

LANES = 128
TILE = 8
STEPS = 4


EVERY = ("section", "feat", "tensor")


def rotations(size):
    return sorted(range(1, size), key=lambda r: (r != size // 2, r))


def turned(index, r, size):
    place = jnp.where(index % 2 == 0, index // 2, size - 1 - index // 2)
    place = (place + r) % size
    return jnp.where(place < size // 2, 2 * place, 2 * (size - 1 - place) + 1)


def turn(value, axis, size, r):
    ring = [*range(0, size, 2), *reversed(range(1, size, 2))]
    pairs = [(ring[i], ring[(i + r) % size]) for i in range(size)]
    return lax.ppermute(value, axis, pairs)


def row_blocks(sections, feats):
    places = [(p, q) for p in range(feats) for q in range(sections)]
    return sorted(places, key=lambda place: (place[0] > 0 and place[1] != 1, place[1], place[0]))


def exchange(value, axis, size, k):
    return lax.ppermute(value, axis, [(i, i ^ k) for i in range(size)])


def inner_kernel(packed, inner):
    tokens = packed.shape[1]
    clean, corrupt, grad = [packed[a].astype(jnp.float32) for a in range(3)]
    part = jnp.sum((corrupt - clean) * grad, axis=1, keepdims=True)
    inner[pl.ds(0, tokens), :] = jnp.broadcast_to(part, (tokens, LANES))


def inner_products(packed):
    vmem = pl.BlockSpec(memory_space=pltpu.VMEM)
    return pl.pallas_call(
        inner_kernel,
        out_shape=jax.ShapeDtypeStruct((TILE, LANES), jnp.float32),
        in_specs=[vmem],
        out_specs=vmem,
        compiler_params=pltpu.CompilerParams(vmem_limit_bytes=4 * 2**20),
        cost_estimate=pl.CostEstimate(flops=2**32, bytes_accessed=2**24, transcendentals=0),
        name="inner_products",
    )(packed)


def inner_kernel(packed, inner):
    tokens = packed.shape[1]
    clean, corrupt, grad = [packed[a].astype(jnp.float32) for a in range(3)]
    part = jnp.sum((corrupt - clean) * grad, axis=1, keepdims=True)
    inner[pl.ds(0, tokens), :] = jnp.broadcast_to(part, (tokens, LANES))


def inner_products(packed):
    vmem = pl.BlockSpec(memory_space=pltpu.VMEM)
    return pl.pallas_call(
        inner_kernel,
        out_shape=jax.ShapeDtypeStruct((TILE, LANES), jnp.float32),
        in_specs=[vmem],
        out_specs=vmem,
        compiler_params=pltpu.CompilerParams(vmem_limit_bytes=4 * 2**20),
        cost_estimate=pl.CostEstimate(flops=2**32, bytes_accessed=2**24, transcendentals=0),
        name="inner_products",
    )(packed)


def load_kernel(pieces, *refs):
    count = (len(refs) - 2) // 2
    sems = refs[-1]
    copies = []
    for i in range(count):
        source, target = refs[1 + i], refs[1 + count + i]
        count_here = min(pieces, source.shape[0] // 16) or 1
        step = source.shape[0] // count_here
        for j in range(count_here):
            part = pl.ds(j * step, step)
            copies.append(
                pltpu.make_async_copy(source.at[part], target.at[part], sems.at[i, j])
            )
    for copy in copies:
        copy.start()
    for copy in copies:
        copy.wait()


def load(after, *arrays, pieces=4):
    size = sum(array.size * array.dtype.itemsize for array in arrays)
    return pl.pallas_call(
        functools.partial(load_kernel, pieces),
        out_shape=[jax.ShapeDtypeStruct(array.shape, array.dtype) for array in arrays],
        in_specs=[pl.BlockSpec(memory_space=pltpu.VMEM)]
        + [pl.BlockSpec(memory_space=pltpu.HBM)] * len(arrays),
        out_specs=[pl.BlockSpec(memory_space=pltpu.VMEM)] * len(arrays),
        scratch_shapes=[pltpu.SemaphoreType.DMA((len(arrays), pieces))],
        compiler_params=pltpu.CompilerParams(vmem_limit_bytes=16 * 2**20),
        cost_estimate=pl.CostEstimate(flops=0, bytes_accessed=2 * size, transcendentals=0),
        name="load_weights",
    )(after, *arrays)


def product_kernel(groups, parts, *refs):
    blocks = refs[:groups]
    enc, dec = refs[groups : groups + 2]
    outs = refs[groups + 2 : groups + 2 + parts]
    rows, held = refs[groups + 2 + parts :]
    tokens = blocks[0].shape[1]
    total = groups * tokens
    steps, _, depth = rows.shape
    encoded = projected = 0.0
    for j in range(steps):
        part = pl.ds(j * depth, depth)
        for k, block in enumerate(blocks):
            for a in range(3):
                piece = block[a, :, part].astype(jnp.float32)
                rows[j, pl.ds(a * total + k * tokens, tokens), :] = piece
        encoded += jnp.dot(
            rows[j, pl.ds(0, 2 * total), :].astype(jnp.bfloat16),
            enc[part, :],
            preferred_element_type=jnp.float32,
        )
        projected += lax.dot_general(
            rows[j, pl.ds(2 * total, total), :].astype(jnp.bfloat16),
            dec[:, part],
            (((1,), (1,)), ((), ())),
            preferred_element_type=jnp.float32,
        )
    for c in range(parts):
        held[c, pl.ds(0, 2 * total), :] = encoded[:, c * LANES : (c + 1) * LANES]
        held[c, pl.ds(2 * total, total), :] = projected[:, c * LANES : (c + 1) * LANES]
    me = lax.axis_index("tensor")
    outs[0][...] = held[me]
    for r, out in zip(rotations(parts), outs[1:]):
        out[...] = held[turned(me, r, parts)]


def products(parts, blocks, enc_weight, dec_weight):
    groups = len(blocks)
    _, tokens, width = blocks[0].shape
    features = enc_weight.shape[1]
    rows = 3 * groups * tokens
    part = jax.ShapeDtypeStruct((rows, features // parts), jnp.float32)
    vmem = pl.BlockSpec(memory_space=pltpu.VMEM)
    return pl.pallas_call(
        functools.partial(product_kernel, groups, parts),
        out_shape=[part] * parts,
        in_specs=[vmem] * (groups + 2),
        out_specs=[vmem] * parts,
        scratch_shapes=[
            pltpu.VMEM((STEPS, rows, width // STEPS), jnp.float32),
            pltpu.VMEM((parts, rows, features // parts), jnp.float32),
        ],
        compiler_params=pltpu.CompilerParams(vmem_limit_bytes=48 * 2**20),
        name="products",
    )(*blocks, enc_weight, dec_weight)


def add_up(values):
    while len(values) > 1:
        values = [a + b for a, b in zip(values[::2], values[1::2])]
    return values[0]


def attribution_kernel(sizes, *refs):
    sections, feats, parts = sizes
    groups = sections * feats
    terms = refs[:parts]
    bias, inner, sums = refs[parts:]
    total = terms[0].shape[0] // 3
    tokens = total // groups
    preact = add_up([term[...] for term in terms])
    section, feat = lax.axis_index("section"), lax.axis_index("feat")
    b = bias[pl.ds(lax.axis_index("tensor"), 1), :]
    act_clean = jnp.maximum(preact[:total] + b, 0.0)
    act_corrupt = jnp.maximum(preact[total : 2 * total] + b, 0.0)
    attribution = (act_corrupt - act_clean) * preact[2 * total :]

    devices = groups * parts
    feature_part = jnp.sum(attribution, axis=0, keepdims=True)
    sums[:, 0, :] = jnp.broadcast_to(feature_part, (devices, LANES))
    token_part = jnp.sum(attribution, axis=1, keepdims=True)
    lane = lax.broadcasted_iota(jnp.int32, (tokens, LANES), 1)
    place = lane == lax.broadcasted_iota(jnp.int32, (tokens, LANES), 0)
    for k, (p, q) in enumerate(row_blocks(sections, feats)):
        column = jnp.broadcast_to(token_part[k * tokens : (k + 1) * tokens], (tokens, LANES))
        if k == 0:
            column = column - inner[pl.ds(0, tokens), :]
        row = jnp.sum(jnp.where(place, column, 0.0), axis=0, keepdims=True)
        owner = (section ^ q) * feats + (feat ^ p)
        sums[pl.ds(owner * parts, parts), 1, :] = jnp.broadcast_to(row, (parts, LANES))


def attributions(sizes, terms, bias, inner):
    sections, feats, parts = sizes
    vmem = pl.BlockSpec(memory_space=pltpu.VMEM)
    return pl.pallas_call(
        functools.partial(attribution_kernel, sizes),
        out_shape=jax.ShapeDtypeStruct((sections * feats * parts, 2, LANES), jnp.float32),
        in_specs=[vmem] * (parts + 2),
        out_specs=vmem,
        compiler_params=pltpu.CompilerParams(vmem_limit_bytes=16 * 2**20),
        name="attributions",
    )(*terms, bias, inner)


def final_kernel(sizes, arrived, feature_out, error_out, features, errors, sems):
    sections, feats, parts = sizes
    group = lax.axis_index("section") * feats + lax.axis_index("feat")
    mine = arrived[pl.ds(group * parts, parts), 0, :]
    for i in range(parts):
        features[pl.ds(i * LANES, LANES)] = mine[i]
    feature_copy = pltpu.make_async_copy(features, feature_out, sems.at[0])
    feature_copy.start()
    owed = add_up([arrived[i, 1:2, :] for i in range(sections * feats * parts)])
    errors[...] = -owed[0, : errors.shape[0]]
    error_copy = pltpu.make_async_copy(errors, error_out, sems.at[1])
    error_copy.start()
    feature_copy.wait()
    error_copy.wait()


def final(sizes, tokens, arrived):
    features = (sizes[2] * LANES,)
    return pl.pallas_call(
        functools.partial(final_kernel, sizes),
        out_shape=[
            jax.ShapeDtypeStruct(features, jnp.float32),
            jax.ShapeDtypeStruct((tokens,), jnp.float32),
        ],
        in_specs=[pl.BlockSpec(memory_space=pltpu.VMEM)],
        out_specs=[pl.BlockSpec(memory_space=pltpu.HBM)] * 2,
        scratch_shapes=[
            pltpu.VMEM(features, jnp.float32),
            pltpu.VMEM((tokens,), jnp.float32),
            pltpu.SemaphoreType.DMA((2,)),
        ],
        compiler_params=pltpu.CompilerParams(vmem_limit_bytes=4 * 2**20),
        name="final",
    )(arrived)


def per_device(sizes, clean_resid, corrupt_resid, metric_grad, enc_weight, enc_bias, dec_weight):
    sections, feats, parts = sizes
    tokens = clean_resid.shape[0]
    features = enc_weight.shape[1]

    packed = jnp.stack([clean_resid, corrupt_resid, metric_grad])
    inner = inner_products(packed)
    bias = enc_bias.reshape(parts, features // parts)
    held = {(0, 0): packed}
    for p, q in row_blocks(sections, feats):
        if q > 0 and (p == 0 or q == 1):
            pairs = [
                (s * feats + f, (s ^ q) * feats + (f ^ p))
                for s in range(sections)
                for f in range(feats)
            ]
            held[p, q] = lax.ppermute(packed, ("section", "feat"), pairs)
        elif p > 0:
            block = held[0, q]
            if q == 0:
                block, inner = lax.optimization_barrier((block, inner))
            held[p, q] = exchange(block, "feat", feats, p)
    blocks = [held[place] for place in row_blocks(sections, feats)]

    terms = products(parts, blocks, enc_weight, dec_weight)
    arrived = [turn(term, "tensor", parts, r) for r, term in zip(rotations(parts), terms[1:])]
    sums = attributions(sizes, [terms[0]] + arrived, bias, inner)
    return tuple(final(sizes, tokens, lax.all_to_all(sums, EVERY, 0, 0)))


def solution(mesh):
    sizes = [mesh.shape[name] for name in ("section", "feat", "tensor")]
    in_specs = (
        P(("section", "feat"), "tensor"),
        P(("section", "feat"), "tensor"),
        P(("section", "feat"), "tensor"),
        P("tensor", ("section", "feat")),
        P(("section", "feat")),
        P(("section", "feat"), "tensor"),
    )
    out_specs = (P(("section", "feat")), P(("section", "feat")))
    return jax.shard_map(
        functools.partial(per_device, sizes),
        mesh=mesh,
        in_specs=in_specs,
        out_specs=out_specs,
        check_vma=False,
    )
```

```python
import functools

import jax
import jax.numpy as jnp
from jax import lax
from jax.experimental import pallas as pl
from jax.experimental.pallas import tpu as pltpu
from jax.sharding import PartitionSpec as P

LANES = 128
TILE = 8


EVERY = ("section", "feat", "tensor")


def rotations(size):
    return sorted(range(1, size), key=lambda r: (r != size // 2, r == 1, -r))


def turn(value, axis, size, r):
    return lax.ppermute(value, axis, [(i, (i + r) % size) for i in range(size)])


def row_blocks(sections, feats):
    places = [(p, q) for p in range(feats) for q in range(sections)]
    return sorted(places, key=lambda place: (place[0] > 0 and place[1] != 1, place[1], place[0]))


def exchange(value, axis, size, k):
    return lax.ppermute(value, axis, [(i, i ^ k) for i in range(size)])


def inner_kernel(packed, inner):
    tokens = packed.shape[1]
    clean, corrupt, grad = [packed[a].astype(jnp.float32) for a in range(3)]
    part = jnp.sum((corrupt - clean) * grad, axis=1, keepdims=True)
    inner[pl.ds(0, tokens), :] = jnp.broadcast_to(part, (tokens, LANES))


def inner_products(packed):
    vmem = pl.BlockSpec(memory_space=pltpu.VMEM)
    return pl.pallas_call(
        inner_kernel,
        out_shape=jax.ShapeDtypeStruct((TILE, LANES), jnp.float32),
        in_specs=[vmem],
        out_specs=vmem,
        compiler_params=pltpu.CompilerParams(vmem_limit_bytes=4 * 2**20),
        cost_estimate=pl.CostEstimate(flops=2**32, bytes_accessed=2**24, transcendentals=0),
        name="inner_products",
    )(packed)


def inner_kernel(packed, inner):
    tokens = packed.shape[1]
    clean, corrupt, grad = [packed[a].astype(jnp.float32) for a in range(3)]
    part = jnp.sum((corrupt - clean) * grad, axis=1, keepdims=True)
    inner[pl.ds(0, tokens), :] = jnp.broadcast_to(part, (tokens, LANES))


def inner_products(packed):
    vmem = pl.BlockSpec(memory_space=pltpu.VMEM)
    return pl.pallas_call(
        inner_kernel,
        out_shape=jax.ShapeDtypeStruct((TILE, LANES), jnp.float32),
        in_specs=[vmem],
        out_specs=vmem,
        compiler_params=pltpu.CompilerParams(vmem_limit_bytes=4 * 2**20),
        cost_estimate=pl.CostEstimate(flops=2**32, bytes_accessed=2**24, transcendentals=0),
        name="inner_products",
    )(packed)


def load_kernel(pieces, *refs):
    count = (len(refs) - 2) // 2
    sems = refs[-1]
    copies = []
    for i in range(count):
        source, target = refs[1 + i], refs[1 + count + i]
        count_here = min(pieces, source.shape[0] // 16) or 1
        step = source.shape[0] // count_here
        for j in range(count_here):
            part = pl.ds(j * step, step)
            copies.append(
                pltpu.make_async_copy(source.at[part], target.at[part], sems.at[i, j])
            )
    for copy in copies:
        copy.start()
    for copy in copies:
        copy.wait()


def load(after, *arrays, pieces=4):
    size = sum(array.size * array.dtype.itemsize for array in arrays)
    return pl.pallas_call(
        functools.partial(load_kernel, pieces),
        out_shape=[jax.ShapeDtypeStruct(array.shape, array.dtype) for array in arrays],
        in_specs=[pl.BlockSpec(memory_space=pltpu.VMEM)]
        + [pl.BlockSpec(memory_space=pltpu.HBM)] * len(arrays),
        out_specs=[pl.BlockSpec(memory_space=pltpu.VMEM)] * len(arrays),
        scratch_shapes=[pltpu.SemaphoreType.DMA((len(arrays), pieces))],
        compiler_params=pltpu.CompilerParams(vmem_limit_bytes=16 * 2**20),
        cost_estimate=pl.CostEstimate(flops=0, bytes_accessed=2 * size, transcendentals=0),
        name="load_weights",
    )(after, *arrays)


def product_kernel(groups, parts, *refs):
    blocks = refs[:groups]
    enc, dec = refs[groups : groups + 2]
    outs = refs[groups + 2 : groups + 2 + parts]
    rows, held = refs[groups + 2 + parts :]
    tokens = blocks[0].shape[1]
    total = groups * tokens
    share = LANES
    for k, block in enumerate(blocks):
        for a in range(3):
            rows[pl.ds(a * total + k * tokens, tokens), :] = block[a].astype(jnp.float32)
    encoded = jnp.dot(
        rows[pl.ds(0, 2 * total), :].astype(jnp.bfloat16),
        enc[...],
        preferred_element_type=jnp.float32,
    )
    projected = lax.dot_general(
        rows[pl.ds(2 * total, total), :].astype(jnp.bfloat16),
        dec[...],
        (((1,), (1,)), ((), ())),
        preferred_element_type=jnp.float32,
    )
    for c in range(parts):
        held[c, pl.ds(0, 2 * total), :] = encoded[:, c * share : (c + 1) * share]
        held[c, pl.ds(2 * total, total), :] = projected[:, c * share : (c + 1) * share]
    me = lax.axis_index("tensor")
    for r, out in zip([0, *rotations(parts)], outs):
        out[...] = held[lax.rem(me + r, parts)]


def products(parts, blocks, enc_weight, dec_weight):
    groups = len(blocks)
    _, tokens, width = blocks[0].shape
    features = enc_weight.shape[1]
    rows = 3 * groups * tokens
    part = jax.ShapeDtypeStruct((rows, features // parts), jnp.float32)
    vmem = pl.BlockSpec(memory_space=pltpu.VMEM)
    return pl.pallas_call(
        functools.partial(product_kernel, groups, parts),
        out_shape=[part] * parts,
        in_specs=[vmem] * (groups + 2),
        out_specs=[vmem] * parts,
        scratch_shapes=[
            pltpu.VMEM((rows, width), jnp.float32),
            pltpu.VMEM((parts, rows, features // parts), jnp.float32),
        ],
        compiler_params=pltpu.CompilerParams(vmem_limit_bytes=48 * 2**20),
        name="products",
    )(*blocks, enc_weight, dec_weight)


def add_up(values):
    while len(values) > 1:
        values = [a + b for a, b in zip(values[::2], values[1::2])]
    return values[0]


def attribution_kernel(sizes, *refs):
    sections, feats, parts = sizes
    groups = sections * feats
    terms = refs[:parts]
    bias, inner, sums = refs[parts:]
    total = terms[0].shape[0] // 3
    tokens = total // groups
    preact = add_up([term[...] for term in terms])
    section, feat = lax.axis_index("section"), lax.axis_index("feat")
    b = bias[pl.ds(lax.axis_index("tensor"), 1), :]
    act_clean = jnp.maximum(preact[:total] + b, 0.0)
    act_corrupt = jnp.maximum(preact[total : 2 * total] + b, 0.0)
    attribution = (act_corrupt - act_clean) * preact[2 * total :]

    devices = groups * parts
    feature_part = jnp.sum(attribution, axis=0, keepdims=True)
    sums[:, 0, :] = jnp.broadcast_to(feature_part, (devices, LANES))
    token_part = jnp.sum(attribution, axis=1, keepdims=True)
    lane = lax.broadcasted_iota(jnp.int32, (tokens, LANES), 1)
    place = lane == lax.broadcasted_iota(jnp.int32, (tokens, LANES), 0)
    for k, (p, q) in enumerate(row_blocks(sections, feats)):
        column = jnp.broadcast_to(token_part[k * tokens : (k + 1) * tokens], (tokens, LANES))
        if k == 0:
            column = column - inner[pl.ds(0, tokens), :]
        row = jnp.sum(jnp.where(place, column, 0.0), axis=0, keepdims=True)
        owner = (section ^ q) * feats + (feat ^ p)
        sums[pl.ds(owner * parts, parts), 1, :] = jnp.broadcast_to(row, (parts, LANES))


def attributions(sizes, terms, bias, inner):
    sections, feats, parts = sizes
    vmem = pl.BlockSpec(memory_space=pltpu.VMEM)
    return pl.pallas_call(
        functools.partial(attribution_kernel, sizes),
        out_shape=jax.ShapeDtypeStruct((sections * feats * parts, 2, LANES), jnp.float32),
        in_specs=[vmem] * (parts + 2),
        out_specs=vmem,
        compiler_params=pltpu.CompilerParams(vmem_limit_bytes=16 * 2**20),
        name="attributions",
    )(*terms, bias, inner)


def final_kernel(sizes, arrived, feature_out, error_out, features, errors, sems):
    sections, feats, parts = sizes
    group = lax.axis_index("section") * feats + lax.axis_index("feat")
    mine = arrived[pl.ds(group * parts, parts), 0, :]
    for i in range(parts):
        features[pl.ds(i * LANES, LANES)] = mine[i]
    feature_copy = pltpu.make_async_copy(features, feature_out, sems.at[0])
    feature_copy.start()
    owed = add_up([arrived[i, 1:2, :] for i in range(sections * feats * parts)])
    errors[...] = -owed[0, : errors.shape[0]]
    error_copy = pltpu.make_async_copy(errors, error_out, sems.at[1])
    error_copy.start()
    feature_copy.wait()
    error_copy.wait()


def final(sizes, tokens, arrived):
    features = (sizes[2] * LANES,)
    return pl.pallas_call(
        functools.partial(final_kernel, sizes),
        out_shape=[
            jax.ShapeDtypeStruct(features, jnp.float32),
            jax.ShapeDtypeStruct((tokens,), jnp.float32),
        ],
        in_specs=[pl.BlockSpec(memory_space=pltpu.VMEM)],
        out_specs=[pl.BlockSpec(memory_space=pltpu.HBM)] * 2,
        scratch_shapes=[
            pltpu.VMEM(features, jnp.float32),
            pltpu.VMEM((tokens,), jnp.float32),
            pltpu.SemaphoreType.DMA((2,)),
        ],
        compiler_params=pltpu.CompilerParams(vmem_limit_bytes=4 * 2**20),
        name="final",
    )(arrived)


def per_device(sizes, clean_resid, corrupt_resid, metric_grad, enc_weight, enc_bias, dec_weight):
    sections, feats, parts = sizes
    tokens = clean_resid.shape[0]
    features = enc_weight.shape[1]

    packed = jnp.stack([clean_resid, corrupt_resid, metric_grad])
    inner = inner_products(packed)
    bias = enc_bias.reshape(parts, features // parts)
    held = {(0, 0): packed}
    for p, q in row_blocks(sections, feats):
        if q > 0 and (p == 0 or q == 1):
            pairs = [
                (s * feats + f, (s ^ q) * feats + (f ^ p))
                for s in range(sections)
                for f in range(feats)
            ]
            held[p, q] = lax.ppermute(packed, ("section", "feat"), pairs)
        elif p > 0:
            block = held[0, q]
            if q == 0:
                block, inner = lax.optimization_barrier((block, inner))
            held[p, q] = exchange(block, "feat", feats, p)
    blocks = [held[place] for place in row_blocks(sections, feats)]

    terms = products(parts, blocks, enc_weight, dec_weight)
    arrived = [turn(term, "tensor", parts, r) for r, term in zip(rotations(parts), terms[1:])]
    sums = attributions(sizes, [terms[0]] + arrived, bias, inner)
    return tuple(final(sizes, tokens, lax.all_to_all(sums, EVERY, 0, 0)))


def solution(mesh):
    sizes = [mesh.shape[name] for name in ("section", "feat", "tensor")]
    in_specs = (
        P(("section", "feat"), "tensor"),
        P(("section", "feat"), "tensor"),
        P(("section", "feat"), "tensor"),
        P("tensor", ("section", "feat")),
        P(("section", "feat")),
        P(("section", "feat"), "tensor"),
    )
    out_specs = (P(("section", "feat")), P(("section", "feat")))
    return jax.shard_map(
        functools.partial(per_device, sizes),
        mesh=mesh,
        in_specs=in_specs,
        out_specs=out_specs,
        check_vma=False,
    )
```

```python
import functools

import jax
import jax.numpy as jnp
from jax import lax
from jax.experimental import pallas as pl
from jax.experimental.pallas import tpu as pltpu
from jax.sharding import PartitionSpec as P

LANES = 128
TILE = 8


EVERY = ("section", "feat", "tensor")


def row_blocks(sections, feats):
    places = [(p, q) for p in range(feats) for q in range(sections)]
    return sorted(places, key=lambda place: (place[0] > 0 and place[1] != 1, place[1], -place[0]))


def exchange(value, axis, size, k):
    return lax.ppermute(value, axis, [(i, i ^ k) for i in range(size)])


def inner_kernel(packed, inner):
    tokens = packed.shape[1]
    clean, corrupt, grad = [packed[a].astype(jnp.float32) for a in range(3)]
    part = jnp.sum((corrupt - clean) * grad, axis=1, keepdims=True)
    inner[pl.ds(0, tokens), :] = jnp.broadcast_to(part, (tokens, LANES))


def inner_products(packed):
    vmem = pl.BlockSpec(memory_space=pltpu.VMEM)
    return pl.pallas_call(
        inner_kernel,
        out_shape=jax.ShapeDtypeStruct((TILE, LANES), jnp.float32),
        in_specs=[vmem],
        out_specs=vmem,
        compiler_params=pltpu.CompilerParams(vmem_limit_bytes=4 * 2**20),
        cost_estimate=pl.CostEstimate(flops=2**32, bytes_accessed=2**24, transcendentals=0),
        name="inner_products",
    )(packed)


def inner_kernel(packed, inner):
    tokens = packed.shape[1]
    clean, corrupt, grad = [packed[a].astype(jnp.float32) for a in range(3)]
    part = jnp.sum((corrupt - clean) * grad, axis=1, keepdims=True)
    inner[pl.ds(0, tokens), :] = jnp.broadcast_to(part, (tokens, LANES))


def inner_products(packed):
    vmem = pl.BlockSpec(memory_space=pltpu.VMEM)
    return pl.pallas_call(
        inner_kernel,
        out_shape=jax.ShapeDtypeStruct((TILE, LANES), jnp.float32),
        in_specs=[vmem],
        out_specs=vmem,
        compiler_params=pltpu.CompilerParams(vmem_limit_bytes=4 * 2**20),
        cost_estimate=pl.CostEstimate(flops=2**32, bytes_accessed=2**24, transcendentals=0),
        name="inner_products",
    )(packed)


def load_kernel(pieces, *refs):
    count = (len(refs) - 2) // 2
    sems = refs[-1]
    copies = []
    for i in range(count):
        source, target = refs[1 + i], refs[1 + count + i]
        count_here = min(pieces, source.shape[0] // 16) or 1
        step = source.shape[0] // count_here
        for j in range(count_here):
            part = pl.ds(j * step, step)
            copies.append(
                pltpu.make_async_copy(source.at[part], target.at[part], sems.at[i, j])
            )
    for copy in copies:
        copy.start()
    for copy in copies:
        copy.wait()


def load(after, *arrays, pieces=4):
    size = sum(array.size * array.dtype.itemsize for array in arrays)
    return pl.pallas_call(
        functools.partial(load_kernel, pieces),
        out_shape=[jax.ShapeDtypeStruct(array.shape, array.dtype) for array in arrays],
        in_specs=[pl.BlockSpec(memory_space=pltpu.VMEM)]
        + [pl.BlockSpec(memory_space=pltpu.HBM)] * len(arrays),
        out_specs=[pl.BlockSpec(memory_space=pltpu.VMEM)] * len(arrays),
        scratch_shapes=[pltpu.SemaphoreType.DMA((len(arrays), pieces))],
        compiler_params=pltpu.CompilerParams(vmem_limit_bytes=16 * 2**20),
        cost_estimate=pl.CostEstimate(flops=0, bytes_accessed=2 * size, transcendentals=0),
        name="load_weights",
    )(after, *arrays)


def product_kernel(groups, parts, *refs):
    blocks = refs[:groups]
    enc, dec, bias = refs[groups : groups + 3]
    outs = refs[groups + 3 : groups + 3 + parts]
    rows, held = refs[groups + 3 + parts :]
    tokens = blocks[0].shape[1]
    total = groups * tokens
    share = LANES
    for k, block in enumerate(blocks):
        for a in range(3):
            rows[pl.ds(a * total + k * tokens, tokens), :] = block[a].astype(jnp.float32)
    encoded = jnp.dot(
        rows[pl.ds(0, 2 * total), :].astype(jnp.bfloat16),
        enc[...],
        preferred_element_type=jnp.float32,
    )
    projected = lax.dot_general(
        rows[pl.ds(2 * total, total), :].astype(jnp.bfloat16),
        dec[...],
        (((1,), (1,)), ((), ())),
        preferred_element_type=jnp.float32,
    )
    for c in range(parts):
        held[c, pl.ds(0, 2 * total), :] = encoded[:, c * share : (c + 1) * share]
        held[c, pl.ds(2 * total, total), :] = projected[:, c * share : (c + 1) * share]
    me = lax.axis_index("tensor")
    for m, out in enumerate(outs):
        out[...] = held[me ^ m]
    outs[0][pl.ds(0, 2 * total), :] += bias[pl.ds(me, 1), :]


def products(parts, blocks, enc_weight, dec_weight, bias):
    groups = len(blocks)
    _, tokens, width = blocks[0].shape
    features = enc_weight.shape[1]
    rows = 3 * groups * tokens
    part = jax.ShapeDtypeStruct((rows, features // parts), jnp.float32)
    vmem = pl.BlockSpec(memory_space=pltpu.VMEM)
    return pl.pallas_call(
        functools.partial(product_kernel, groups, parts),
        out_shape=[part] * parts,
        in_specs=[vmem] * (groups + 3),
        out_specs=[vmem] * parts,
        scratch_shapes=[
            pltpu.VMEM((rows, width), jnp.float32),
            pltpu.VMEM((parts, rows, features // parts), jnp.float32),
        ],
        compiler_params=pltpu.CompilerParams(vmem_limit_bytes=48 * 2**20),
        name="products",
    )(*blocks, enc_weight, dec_weight, bias)


def add_up(values):
    while len(values) > 1:
        values = [a + b for a, b in zip(values[::2], values[1::2])]
    return values[0]


def attribution_kernel(sizes, *refs):
    sections, feats, parts = sizes
    groups = sections * feats
    terms = refs[:parts]
    inner, sums = refs[parts:]
    total = terms[0].shape[0] // 3
    tokens = total // groups
    preact = add_up([term[...] for term in terms])
    section, feat = lax.axis_index("section"), lax.axis_index("feat")
    act_clean = jnp.maximum(preact[:total], 0.0)
    act_corrupt = jnp.maximum(preact[total : 2 * total], 0.0)
    attribution = (act_corrupt - act_clean) * preact[2 * total :]

    devices = groups * parts
    feature_part = jnp.sum(attribution, axis=0, keepdims=True)
    sums[:, 0, :] = jnp.broadcast_to(feature_part, (devices, LANES))
    token_part = jnp.sum(attribution, axis=1, keepdims=True)
    lane = lax.broadcasted_iota(jnp.int32, (tokens, LANES), 1)
    place = lane == lax.broadcasted_iota(jnp.int32, (tokens, LANES), 0)
    for k, (p, q) in enumerate(row_blocks(sections, feats)):
        column = jnp.broadcast_to(token_part[k * tokens : (k + 1) * tokens], (tokens, LANES))
        if (p, q) == (1, 0):
            column = column - inner[pl.ds(0, tokens), :]
        row = jnp.sum(jnp.where(place, column, 0.0), axis=0, keepdims=True)
        owner = (section ^ q) * feats + (feat ^ 1 ^ p)
        sums[pl.ds(owner * parts, parts), 1, :] = jnp.broadcast_to(row, (parts, LANES))


def attributions(sizes, terms, inner):
    sections, feats, parts = sizes
    vmem = pl.BlockSpec(memory_space=pltpu.VMEM)
    return pl.pallas_call(
        functools.partial(attribution_kernel, sizes),
        out_shape=jax.ShapeDtypeStruct((sections * feats * parts, 2, LANES), jnp.float32),
        in_specs=[vmem] * (parts + 1),
        out_specs=vmem,
        compiler_params=pltpu.CompilerParams(vmem_limit_bytes=16 * 2**20),
        name="attributions",
    )(*terms, inner)


def final_kernel(sizes, arrived, feature_out, error_out, features, errors, sems):
    sections, feats, parts = sizes
    group = lax.axis_index("section") * feats + (lax.axis_index("feat") ^ 1)
    mine = arrived[pl.ds(group * parts, parts), 0, :]
    for i in range(parts):
        features[pl.ds(i * LANES, LANES)] = mine[i]
    feature_copy = pltpu.make_async_copy(features, feature_out, sems.at[0])
    feature_copy.start()
    owed = add_up([arrived[i, 1:2, :] for i in range(sections * feats * parts)])
    errors[...] = -owed[0, : errors.shape[0]]
    error_copy = pltpu.make_async_copy(errors, error_out, sems.at[1])
    error_copy.start()
    feature_copy.wait()
    error_copy.wait()


def final(sizes, tokens, arrived):
    features = (sizes[2] * LANES,)
    return pl.pallas_call(
        functools.partial(final_kernel, sizes),
        out_shape=[
            jax.ShapeDtypeStruct(features, jnp.float32),
            jax.ShapeDtypeStruct((tokens,), jnp.float32),
        ],
        in_specs=[pl.BlockSpec(memory_space=pltpu.VMEM)],
        out_specs=[pl.BlockSpec(memory_space=pltpu.HBM)] * 2,
        scratch_shapes=[
            pltpu.VMEM(features, jnp.float32),
            pltpu.VMEM((tokens,), jnp.float32),
            pltpu.SemaphoreType.DMA((2,)),
        ],
        compiler_params=pltpu.CompilerParams(vmem_limit_bytes=4 * 2**20),
        name="final",
    )(arrived)


def per_device(sizes, clean_resid, corrupt_resid, metric_grad, enc_weight, enc_bias, dec_weight):
    sections, feats, parts = sizes
    tokens = clean_resid.shape[0]
    features = enc_weight.shape[1]

    packed = jnp.stack([clean_resid, corrupt_resid, metric_grad])
    inner = inner_products(packed)
    bias = enc_bias.reshape(parts, features // parts)
    held = {(0, 0): packed}
    for p, q in row_blocks(sections, feats):
        if q > 0 and (p == 0 or q == 1):
            pairs = [
                (s * feats + f, (s ^ q) * feats + (f ^ p))
                for s in range(sections)
                for f in range(feats)
            ]
            held[p, q] = lax.ppermute(packed, ("section", "feat"), pairs)
        elif p > 0:
            block = held[0, q]
            if q == 0:
                block, inner = lax.optimization_barrier((block, inner))
            held[p, q] = exchange(block, "feat", feats, p)
    blocks = [held[place] for place in row_blocks(sections, feats)]

    terms = products(parts, blocks, enc_weight, dec_weight, bias)
    arrived = [
        lax.ppermute(
            terms[m],
            ("feat", "tensor"),
            [(f * parts + t, (f ^ 1) * parts + (t ^ m)) for f in range(feats) for t in range(parts)],
        )
        for m in reversed(range(parts))
    ]
    sums = attributions(sizes, arrived, inner)
    return tuple(final(sizes, tokens, lax.all_to_all(sums, EVERY, 0, 0)))


def solution(mesh):
    sizes = [mesh.shape[name] for name in ("section", "feat", "tensor")]
    in_specs = (
        P(("section", "feat"), "tensor"),
        P(("section", "feat"), "tensor"),
        P(("section", "feat"), "tensor"),
        P("tensor", ("section", "feat")),
        P(("section", "feat")),
        P(("section", "feat"), "tensor"),
    )
    out_specs = (P(("section", "feat")), P(("section", "feat")))
    return jax.shard_map(
        functools.partial(per_device, sizes),
        mesh=mesh,
        in_specs=in_specs,
        out_specs=out_specs,
        check_vma=False,
    )
```

```python
import functools

import jax
import jax.numpy as jnp
from jax import lax
from jax.experimental import pallas as pl
from jax.experimental.pallas import tpu as pltpu
from jax.sharding import PartitionSpec as P

LANES = 128
TILE = 8


EVERY = ("section", "feat", "tensor")


def row_blocks(sections, feats):
    places = [(p, q) for p in range(feats) for q in range(sections)]
    return sorted(places, key=lambda place: (place[0] > 0 and place[1] != 1, place[1], place[0]))


def exchange(value, axis, size, k):
    return lax.ppermute(value, axis, [(i, i ^ k) for i in range(size)])


def inner_kernel(packed, inner):
    tokens = packed.shape[1]
    clean, corrupt, grad = [packed[a].astype(jnp.float32) for a in range(3)]
    part = jnp.sum((corrupt - clean) * grad, axis=1, keepdims=True)
    inner[pl.ds(0, tokens), :] = jnp.broadcast_to(part, (tokens, LANES))


def inner_products(packed):
    vmem = pl.BlockSpec(memory_space=pltpu.VMEM)
    return pl.pallas_call(
        inner_kernel,
        out_shape=jax.ShapeDtypeStruct((TILE, LANES), jnp.float32),
        in_specs=[vmem],
        out_specs=vmem,
        compiler_params=pltpu.CompilerParams(vmem_limit_bytes=4 * 2**20),
        cost_estimate=pl.CostEstimate(flops=2**32, bytes_accessed=2**24, transcendentals=0),
        name="inner_products",
    )(packed)


def inner_kernel(packed, inner):
    tokens = packed.shape[1]
    clean, corrupt, grad = [packed[a].astype(jnp.float32) for a in range(3)]
    part = jnp.sum((corrupt - clean) * grad, axis=1, keepdims=True)
    inner[pl.ds(0, tokens), :] = jnp.broadcast_to(part, (tokens, LANES))


def inner_products(packed):
    vmem = pl.BlockSpec(memory_space=pltpu.VMEM)
    return pl.pallas_call(
        inner_kernel,
        out_shape=jax.ShapeDtypeStruct((TILE, LANES), jnp.float32),
        in_specs=[vmem],
        out_specs=vmem,
        compiler_params=pltpu.CompilerParams(vmem_limit_bytes=4 * 2**20),
        cost_estimate=pl.CostEstimate(flops=2**32, bytes_accessed=2**24, transcendentals=0),
        name="inner_products",
    )(packed)


def load_kernel(pieces, *refs):
    count = (len(refs) - 2) // 2
    sems = refs[-1]
    copies = []
    for i in range(count):
        source, target = refs[1 + i], refs[1 + count + i]
        count_here = min(pieces, source.shape[0] // 16) or 1
        step = source.shape[0] // count_here
        for j in range(count_here):
            part = pl.ds(j * step, step)
            copies.append(
                pltpu.make_async_copy(source.at[part], target.at[part], sems.at[i, j])
            )
    for copy in copies:
        copy.start()
    for copy in copies:
        copy.wait()


def load(after, *arrays, pieces=4):
    size = sum(array.size * array.dtype.itemsize for array in arrays)
    return pl.pallas_call(
        functools.partial(load_kernel, pieces),
        out_shape=[jax.ShapeDtypeStruct(array.shape, array.dtype) for array in arrays],
        in_specs=[pl.BlockSpec(memory_space=pltpu.VMEM)]
        + [pl.BlockSpec(memory_space=pltpu.HBM)] * len(arrays),
        out_specs=[pl.BlockSpec(memory_space=pltpu.VMEM)] * len(arrays),
        scratch_shapes=[pltpu.SemaphoreType.DMA((len(arrays), pieces))],
        compiler_params=pltpu.CompilerParams(vmem_limit_bytes=16 * 2**20),
        cost_estimate=pl.CostEstimate(flops=0, bytes_accessed=2 * size, transcendentals=0),
        name="load_weights",
    )(after, *arrays)


def product_kernel(groups, parts, *refs):
    blocks = refs[:groups]
    enc, dec, bias = refs[groups : groups + 3]
    outs = refs[groups + 3 : groups + 3 + parts]
    rows, held = refs[groups + 3 + parts :]
    tokens = blocks[0].shape[1]
    total = groups * tokens
    share = LANES
    for k, block in enumerate(blocks):
        for a in range(3):
            rows[pl.ds(a * total + k * tokens, tokens), :] = block[a].astype(jnp.float32)
    encoded = jnp.dot(
        rows[pl.ds(0, 2 * total), :].astype(jnp.bfloat16),
        enc[...],
        preferred_element_type=jnp.float32,
    )
    projected = lax.dot_general(
        rows[pl.ds(2 * total, total), :].astype(jnp.bfloat16),
        dec[...],
        (((1,), (1,)), ((), ())),
        preferred_element_type=jnp.float32,
    )
    for c in range(parts):
        held[c, pl.ds(0, 2 * total), :] = encoded[:, c * share : (c + 1) * share]
        held[c, pl.ds(2 * total, total), :] = projected[:, c * share : (c + 1) * share]
    me = lax.axis_index("tensor")
    for m, out in enumerate(outs):
        out[...] = held[me ^ m]
    outs[0][pl.ds(0, 2 * total), :] += bias[pl.ds(me, 1), :]


def products(parts, blocks, enc_weight, dec_weight, bias):
    groups = len(blocks)
    _, tokens, width = blocks[0].shape
    features = enc_weight.shape[1]
    rows = 3 * groups * tokens
    part = jax.ShapeDtypeStruct((rows, features // parts), jnp.float32)
    vmem = pl.BlockSpec(memory_space=pltpu.VMEM)
    return pl.pallas_call(
        functools.partial(product_kernel, groups, parts),
        out_shape=[part] * parts,
        in_specs=[vmem] * (groups + 3),
        out_specs=[vmem] * parts,
        scratch_shapes=[
            pltpu.VMEM((rows, width), jnp.float32),
            pltpu.VMEM((parts, rows, features // parts), jnp.float32),
        ],
        compiler_params=pltpu.CompilerParams(vmem_limit_bytes=48 * 2**20),
        name="products",
    )(*blocks, enc_weight, dec_weight, bias)


def add_up(values):
    while len(values) > 1:
        values = [a + b for a, b in zip(values[::2], values[1::2])]
    return values[0]


def attribution_kernel(sizes, *refs):
    sections, feats, parts = sizes
    groups = sections * feats
    terms = refs[:parts]
    inner, sums = refs[parts:]
    total = terms[0].shape[0] // 3
    tokens = total // groups
    preact = add_up([term[...] for term in terms])
    section, feat = lax.axis_index("section"), lax.axis_index("feat")
    act_clean = jnp.maximum(preact[:total], 0.0)
    act_corrupt = jnp.maximum(preact[total : 2 * total], 0.0)
    attribution = (act_corrupt - act_clean) * preact[2 * total :]

    devices = groups * parts
    feature_part = jnp.sum(attribution, axis=0, keepdims=True)
    sums[:, 0, :] = jnp.broadcast_to(feature_part, (devices, LANES))
    token_part = jnp.sum(attribution, axis=1, keepdims=True)
    lane = lax.broadcasted_iota(jnp.int32, (tokens, LANES), 1)
    place = lane == lax.broadcasted_iota(jnp.int32, (tokens, LANES), 0)
    for k, (p, q) in enumerate(row_blocks(sections, feats)):
        column = jnp.broadcast_to(token_part[k * tokens : (k + 1) * tokens], (tokens, LANES))
        if (p, q) == (1, 0):
            column = column - inner[pl.ds(0, tokens), :]
        row = jnp.sum(jnp.where(place, column, 0.0), axis=0, keepdims=True)
        owner = (section ^ q) * feats + (feat ^ 1 ^ p)
        sums[pl.ds(owner * parts, parts), 1, :] = jnp.broadcast_to(row, (parts, LANES))


def attributions(sizes, terms, inner):
    sections, feats, parts = sizes
    vmem = pl.BlockSpec(memory_space=pltpu.VMEM)
    return pl.pallas_call(
        functools.partial(attribution_kernel, sizes),
        out_shape=jax.ShapeDtypeStruct((sections * feats * parts, 2, LANES), jnp.float32),
        in_specs=[vmem] * (parts + 1),
        out_specs=vmem,
        compiler_params=pltpu.CompilerParams(vmem_limit_bytes=16 * 2**20),
        name="attributions",
    )(*terms, inner)


def final_kernel(sizes, arrived, feature_out, error_out, features, errors, sems):
    sections, feats, parts = sizes
    group = lax.axis_index("section") * feats + (lax.axis_index("feat") ^ 1)
    mine = arrived[pl.ds(group * parts, parts), 0, :]
    for i in range(parts):
        features[pl.ds(i * LANES, LANES)] = mine[i]
    feature_copy = pltpu.make_async_copy(features, feature_out, sems.at[0])
    feature_copy.start()
    owed = add_up([arrived[i, 1:2, :] for i in range(sections * feats * parts)])
    errors[...] = -owed[0, : errors.shape[0]]
    error_copy = pltpu.make_async_copy(errors, error_out, sems.at[1])
    error_copy.start()
    feature_copy.wait()
    error_copy.wait()


def final(sizes, tokens, arrived):
    features = (sizes[2] * LANES,)
    return pl.pallas_call(
        functools.partial(final_kernel, sizes),
        out_shape=[
            jax.ShapeDtypeStruct(features, jnp.float32),
            jax.ShapeDtypeStruct((tokens,), jnp.float32),
        ],
        in_specs=[pl.BlockSpec(memory_space=pltpu.VMEM)],
        out_specs=[pl.BlockSpec(memory_space=pltpu.HBM)] * 2,
        scratch_shapes=[
            pltpu.VMEM(features, jnp.float32),
            pltpu.VMEM((tokens,), jnp.float32),
            pltpu.SemaphoreType.DMA((2,)),
        ],
        compiler_params=pltpu.CompilerParams(vmem_limit_bytes=4 * 2**20),
        name="final",
    )(arrived)


def per_device(sizes, clean_resid, corrupt_resid, metric_grad, enc_weight, enc_bias, dec_weight):
    sections, feats, parts = sizes
    tokens = clean_resid.shape[0]
    features = enc_weight.shape[1]

    packed = jnp.stack([clean_resid, corrupt_resid, metric_grad])
    inner = inner_products(packed)
    bias = enc_bias.reshape(parts, features // parts)
    held = {(0, 0): packed}
    for p, q in row_blocks(sections, feats):
        if q > 0 and (p == 0 or q == 1):
            pairs = [
                (s * feats + f, (s ^ q) * feats + (f ^ p))
                for s in range(sections)
                for f in range(feats)
            ]
            held[p, q] = lax.ppermute(packed, ("section", "feat"), pairs)
        elif p > 0:
            block = held[0, q]
            if q == 0:
                block, inner = lax.optimization_barrier((block, inner))
            held[p, q] = exchange(block, "feat", feats, p)
    blocks = [held[place] for place in row_blocks(sections, feats)]

    terms = products(parts, blocks, enc_weight, dec_weight, bias)
    arrived = [
        lax.ppermute(
            terms[m],
            ("feat", "tensor"),
            [(f * parts + t, (f ^ 1) * parts + (t ^ m)) for f in range(feats) for t in range(parts)],
        )
        for m in reversed(range(parts))
    ]
    sums = attributions(sizes, arrived, inner)
    return tuple(final(sizes, tokens, lax.all_to_all(sums, EVERY, 0, 0)))


def solution(mesh):
    sizes = [mesh.shape[name] for name in ("section", "feat", "tensor")]
    in_specs = (
        P(("section", "feat"), "tensor"),
        P(("section", "feat"), "tensor"),
        P(("section", "feat"), "tensor"),
        P("tensor", ("section", "feat")),
        P(("section", "feat")),
        P(("section", "feat"), "tensor"),
    )
    out_specs = (P(("section", "feat")), P(("section", "feat")))
    return jax.shard_map(
        functools.partial(per_device, sizes),
        mesh=mesh,
        in_specs=in_specs,
        out_specs=out_specs,
        check_vma=False,
    )
```

```python
import functools

import jax
import jax.numpy as jnp
from jax import lax
from jax.experimental import pallas as pl
from jax.experimental.pallas import tpu as pltpu
from jax.sharding import PartitionSpec as P

LANES = 128
TILE = 8


EVERY = ("section", "feat", "tensor")


def row_blocks(sections, feats):
    places = [(p, q) for p in range(feats) for q in range(sections)]
    return sorted(places, key=lambda place: (place[0] > 0 and place[1] != 1, place[1], place[0]))


def exchange(value, axis, size, k):
    return lax.ppermute(value, axis, [(i, i ^ k) for i in range(size)])


def inner_kernel(packed, inner):
    tokens = packed.shape[1]
    clean, corrupt, grad = [packed[a].astype(jnp.float32) for a in range(3)]
    part = jnp.sum((corrupt - clean) * grad, axis=1, keepdims=True)
    inner[pl.ds(0, tokens), :] = jnp.broadcast_to(part, (tokens, LANES))


def inner_products(packed):
    vmem = pl.BlockSpec(memory_space=pltpu.VMEM)
    return pl.pallas_call(
        inner_kernel,
        out_shape=jax.ShapeDtypeStruct((TILE, LANES), jnp.float32),
        in_specs=[vmem],
        out_specs=vmem,
        compiler_params=pltpu.CompilerParams(vmem_limit_bytes=4 * 2**20),
        cost_estimate=pl.CostEstimate(flops=2**32, bytes_accessed=2**24, transcendentals=0),
        name="inner_products",
    )(packed)


def inner_kernel(packed, inner):
    tokens = packed.shape[1]
    clean, corrupt, grad = [packed[a].astype(jnp.float32) for a in range(3)]
    part = jnp.sum((corrupt - clean) * grad, axis=1, keepdims=True)
    inner[pl.ds(0, tokens), :] = jnp.broadcast_to(part, (tokens, LANES))


def inner_products(packed):
    vmem = pl.BlockSpec(memory_space=pltpu.VMEM)
    return pl.pallas_call(
        inner_kernel,
        out_shape=jax.ShapeDtypeStruct((TILE, LANES), jnp.float32),
        in_specs=[vmem],
        out_specs=vmem,
        compiler_params=pltpu.CompilerParams(vmem_limit_bytes=4 * 2**20),
        cost_estimate=pl.CostEstimate(flops=2**32, bytes_accessed=2**24, transcendentals=0),
        name="inner_products",
    )(packed)


def load_kernel(pieces, *refs):
    count = (len(refs) - 2) // 2
    sems = refs[-1]
    copies = []
    for i in range(count):
        source, target = refs[1 + i], refs[1 + count + i]
        count_here = min(pieces, source.shape[0] // 16) or 1
        step = source.shape[0] // count_here
        for j in range(count_here):
            part = pl.ds(j * step, step)
            copies.append(
                pltpu.make_async_copy(source.at[part], target.at[part], sems.at[i, j])
            )
    for copy in copies:
        copy.start()
    for copy in copies:
        copy.wait()


def load(after, *arrays, pieces=4):
    size = sum(array.size * array.dtype.itemsize for array in arrays)
    return pl.pallas_call(
        functools.partial(load_kernel, pieces),
        out_shape=[jax.ShapeDtypeStruct(array.shape, array.dtype) for array in arrays],
        in_specs=[pl.BlockSpec(memory_space=pltpu.VMEM)]
        + [pl.BlockSpec(memory_space=pltpu.HBM)] * len(arrays),
        out_specs=[pl.BlockSpec(memory_space=pltpu.VMEM)] * len(arrays),
        scratch_shapes=[pltpu.SemaphoreType.DMA((len(arrays), pieces))],
        compiler_params=pltpu.CompilerParams(vmem_limit_bytes=16 * 2**20),
        cost_estimate=pl.CostEstimate(flops=0, bytes_accessed=2 * size, transcendentals=0),
        name="load_weights",
    )(after, *arrays)


def product_kernel(groups, parts, *refs):
    blocks = refs[:groups]
    enc, dec, bias = refs[groups : groups + 3]
    outs = refs[groups + 3 : groups + 3 + parts]
    rows, held = refs[groups + 3 + parts :]
    tokens = blocks[0].shape[1]
    total = groups * tokens
    share = LANES
    for k, block in enumerate(blocks):
        for a in range(3):
            rows[pl.ds(a * total + k * tokens, tokens), :] = block[a].astype(jnp.float32)
    encoded = jnp.dot(
        rows[pl.ds(0, 2 * total), :].astype(jnp.bfloat16),
        enc[...],
        preferred_element_type=jnp.float32,
    )
    projected = lax.dot_general(
        rows[pl.ds(2 * total, total), :].astype(jnp.bfloat16),
        dec[...],
        (((1,), (1,)), ((), ())),
        preferred_element_type=jnp.float32,
    )
    for c in range(parts):
        held[c, pl.ds(0, 2 * total), :] = encoded[:, c * share : (c + 1) * share]
        held[c, pl.ds(2 * total, total), :] = projected[:, c * share : (c + 1) * share]
    me = lax.axis_index("tensor")
    for m, out in enumerate(outs):
        out[...] = held[me ^ m]
    outs[0][pl.ds(0, 2 * total), :] += bias[pl.ds(me, 1), :]


def products(parts, blocks, enc_weight, dec_weight, bias):
    groups = len(blocks)
    _, tokens, width = blocks[0].shape
    features = enc_weight.shape[1]
    rows = 3 * groups * tokens
    part = jax.ShapeDtypeStruct((rows, features // parts), jnp.float32)
    vmem = pl.BlockSpec(memory_space=pltpu.VMEM)
    return pl.pallas_call(
        functools.partial(product_kernel, groups, parts),
        out_shape=[part] * parts,
        in_specs=[vmem] * (groups + 3),
        out_specs=[vmem] * parts,
        scratch_shapes=[
            pltpu.VMEM((rows, width), jnp.float32),
            pltpu.VMEM((parts, rows, features // parts), jnp.float32),
        ],
        compiler_params=pltpu.CompilerParams(vmem_limit_bytes=48 * 2**20),
        name="products",
    )(*blocks, enc_weight, dec_weight, bias)


def add_up(values):
    while len(values) > 1:
        values = [a + b for a, b in zip(values[::2], values[1::2])]
    return values[0]


def attribution_kernel(sizes, *refs):
    sections, feats, parts = sizes
    groups = sections * feats
    terms = refs[:parts]
    inner, sums = refs[parts:]
    total = terms[0].shape[0] // 3
    tokens = total // groups
    preact = add_up([term[...] for term in terms])
    section, feat = lax.axis_index("section"), lax.axis_index("feat")
    act_clean = jnp.maximum(preact[:total], 0.0)
    act_corrupt = jnp.maximum(preact[total : 2 * total], 0.0)
    attribution = (act_corrupt - act_clean) * preact[2 * total :]

    sums[pl.ds(0, 1), :] = jnp.sum(attribution, axis=0, keepdims=True)
    token_part = jnp.sum(attribution, axis=1, keepdims=True)
    lane = lax.broadcasted_iota(jnp.int32, (tokens, LANES), 1)
    token = lax.broadcasted_iota(jnp.int32, (tokens, LANES), 0)
    held = [jnp.zeros((1, LANES), jnp.float32) for _ in range(sums.shape[0] - 1)]
    for k, (p, q) in enumerate(row_blocks(sections, feats)):
        column = jnp.broadcast_to(token_part[k * tokens : (k + 1) * tokens], (tokens, LANES))
        if (p, q) == (1, 0):
            column = column - inner[pl.ds(0, tokens), :]
        first = ((section ^ q) * feats + (feat ^ 1 ^ p)) * tokens
        for i in range(len(held)):
            place = lane == token + (first - i * LANES)
            held[i] = held[i] + jnp.sum(jnp.where(place, column, 0.0), axis=0, keepdims=True)
    for i, row in enumerate(held):
        sums[pl.ds(1 + i, 1), :] = row


def attributions(sizes, terms, inner):
    parts = sizes[2]
    token_rows = -(-terms[0].shape[0] // 3 // LANES)
    vmem = pl.BlockSpec(memory_space=pltpu.VMEM)
    return pl.pallas_call(
        functools.partial(attribution_kernel, sizes),
        out_shape=jax.ShapeDtypeStruct((1 + token_rows, LANES), jnp.float32),
        in_specs=[vmem] * (parts + 1),
        out_specs=vmem,
        compiler_params=pltpu.CompilerParams(vmem_limit_bytes=16 * 2**20),
        name="attributions",
    )(*terms, inner)


def final_kernel(sizes, arrived, feature_out, error_out, features, errors, sems):
    sections, feats, parts = sizes
    group = lax.axis_index("section") * feats + (lax.axis_index("feat") ^ 1)
    mine = arrived[pl.ds(group * parts, parts), 0, :]
    for i in range(parts):
        features[pl.ds(i * LANES, LANES)] = mine[i]
    feature_copy = pltpu.make_async_copy(features, feature_out, sems.at[0])
    feature_copy.start()
    tokens = errors.shape[0]
    own = lax.axis_index("section") * feats + lax.axis_index("feat")
    row, first = own * tokens // LANES, lax.rem(own * tokens, LANES)
    owed = add_up([arrived[i, pl.ds(1 + row, 1), :] for i in range(sections * feats * parts)])
    errors[...] = -pltpu.roll(owed, lax.rem(LANES - first, LANES), 1)[0, :tokens]
    error_copy = pltpu.make_async_copy(errors, error_out, sems.at[1])
    error_copy.start()
    feature_copy.wait()
    error_copy.wait()


def final(sizes, tokens, arrived):
    features = (sizes[2] * LANES,)
    return pl.pallas_call(
        functools.partial(final_kernel, sizes),
        out_shape=[
            jax.ShapeDtypeStruct(features, jnp.float32),
            jax.ShapeDtypeStruct((tokens,), jnp.float32),
        ],
        in_specs=[pl.BlockSpec(memory_space=pltpu.VMEM)],
        out_specs=[pl.BlockSpec(memory_space=pltpu.HBM)] * 2,
        scratch_shapes=[
            pltpu.VMEM(features, jnp.float32),
            pltpu.VMEM((tokens,), jnp.float32),
            pltpu.SemaphoreType.DMA((2,)),
        ],
        compiler_params=pltpu.CompilerParams(vmem_limit_bytes=4 * 2**20),
        name="final",
    )(arrived)


def per_device(sizes, clean_resid, corrupt_resid, metric_grad, enc_weight, enc_bias, dec_weight):
    sections, feats, parts = sizes
    tokens = clean_resid.shape[0]
    features = enc_weight.shape[1]

    packed = jnp.stack([clean_resid, corrupt_resid, metric_grad])
    inner = inner_products(packed)
    bias = enc_bias.reshape(parts, features // parts)
    held = {(0, 0): packed}
    for p, q in row_blocks(sections, feats):
        if q > 0 and (p == 0 or q == 1):
            pairs = [
                (s * feats + f, (s ^ q) * feats + (f ^ p))
                for s in range(sections)
                for f in range(feats)
            ]
            held[p, q] = lax.ppermute(packed, ("section", "feat"), pairs)
        elif p > 0:
            block = held[0, q]
            if q == 0:
                block, inner = lax.optimization_barrier((block, inner))
            held[p, q] = exchange(block, "feat", feats, p)
    blocks = [held[place] for place in row_blocks(sections, feats)]

    terms = products(parts, blocks, enc_weight, dec_weight, bias)
    arrived = [
        lax.ppermute(
            terms[m],
            ("feat", "tensor"),
            [(f * parts + t, (f ^ 1) * parts + (t ^ m)) for f in range(feats) for t in range(parts)],
        )
        for m in reversed(range(parts))
    ]
    sums = attributions(sizes, arrived, inner)
    return tuple(final(sizes, tokens, lax.all_gather(sums, EVERY)))


def solution(mesh):
    sizes = [mesh.shape[name] for name in ("section", "feat", "tensor")]
    in_specs = (
        P(("section", "feat"), "tensor"),
        P(("section", "feat"), "tensor"),
        P(("section", "feat"), "tensor"),
        P("tensor", ("section", "feat")),
        P(("section", "feat")),
        P(("section", "feat"), "tensor"),
    )
    out_specs = (P(("section", "feat")), P(("section", "feat")))
    return jax.shard_map(
        functools.partial(per_device, sizes),
        mesh=mesh,
        in_specs=in_specs,
        out_specs=out_specs,
        check_vma=False,
    )
```

```python
import functools

import jax
import jax.numpy as jnp
from jax import lax
from jax.experimental import pallas as pl
from jax.experimental.pallas import tpu as pltpu
from jax.sharding import PartitionSpec as P

LANES = 128
TILE = 8


EVERY = ("section", "feat", "tensor")


def rotations(size):
    return sorted(range(size), key=lambda r: (r != size // 2, r == 0, r == 1, -r))


def row_blocks(sections, feats):
    places = [(p, q) for p in range(feats) for q in range(sections)]
    return sorted(places, key=lambda place: (place[0] > 0 and place[1] != 1, place[1], place[0]))


def exchange(value, axis, size, k):
    return lax.ppermute(value, axis, [(i, i ^ k) for i in range(size)])


def inner_kernel(packed, inner):
    tokens = packed.shape[1]
    clean, corrupt, grad = [packed[a].astype(jnp.float32) for a in range(3)]
    part = jnp.sum((corrupt - clean) * grad, axis=1, keepdims=True)
    inner[pl.ds(0, tokens), :] = jnp.broadcast_to(part, (tokens, LANES))


def inner_products(packed):
    vmem = pl.BlockSpec(memory_space=pltpu.VMEM)
    return pl.pallas_call(
        inner_kernel,
        out_shape=jax.ShapeDtypeStruct((TILE, LANES), jnp.float32),
        in_specs=[vmem],
        out_specs=vmem,
        compiler_params=pltpu.CompilerParams(vmem_limit_bytes=4 * 2**20),
        cost_estimate=pl.CostEstimate(flops=2**32, bytes_accessed=2**24, transcendentals=0),
        name="inner_products",
    )(packed)


def inner_kernel(packed, inner):
    tokens = packed.shape[1]
    clean, corrupt, grad = [packed[a].astype(jnp.float32) for a in range(3)]
    part = jnp.sum((corrupt - clean) * grad, axis=1, keepdims=True)
    inner[pl.ds(0, tokens), :] = jnp.broadcast_to(part, (tokens, LANES))


def inner_products(packed):
    vmem = pl.BlockSpec(memory_space=pltpu.VMEM)
    return pl.pallas_call(
        inner_kernel,
        out_shape=jax.ShapeDtypeStruct((TILE, LANES), jnp.float32),
        in_specs=[vmem],
        out_specs=vmem,
        compiler_params=pltpu.CompilerParams(vmem_limit_bytes=4 * 2**20),
        cost_estimate=pl.CostEstimate(flops=2**32, bytes_accessed=2**24, transcendentals=0),
        name="inner_products",
    )(packed)


def load_kernel(pieces, *refs):
    count = (len(refs) - 2) // 2
    sems = refs[-1]
    copies = []
    for i in range(count):
        source, target = refs[1 + i], refs[1 + count + i]
        count_here = min(pieces, source.shape[0] // 16) or 1
        step = source.shape[0] // count_here
        for j in range(count_here):
            part = pl.ds(j * step, step)
            copies.append(
                pltpu.make_async_copy(source.at[part], target.at[part], sems.at[i, j])
            )
    for copy in copies:
        copy.start()
    for copy in copies:
        copy.wait()


def load(after, *arrays, pieces=4):
    size = sum(array.size * array.dtype.itemsize for array in arrays)
    return pl.pallas_call(
        functools.partial(load_kernel, pieces),
        out_shape=[jax.ShapeDtypeStruct(array.shape, array.dtype) for array in arrays],
        in_specs=[pl.BlockSpec(memory_space=pltpu.VMEM)]
        + [pl.BlockSpec(memory_space=pltpu.HBM)] * len(arrays),
        out_specs=[pl.BlockSpec(memory_space=pltpu.VMEM)] * len(arrays),
        scratch_shapes=[pltpu.SemaphoreType.DMA((len(arrays), pieces))],
        compiler_params=pltpu.CompilerParams(vmem_limit_bytes=16 * 2**20),
        cost_estimate=pl.CostEstimate(flops=0, bytes_accessed=2 * size, transcendentals=0),
        name="load_weights",
    )(after, *arrays)


def product_kernel(groups, parts, *refs):
    blocks = refs[:groups]
    enc, dec, bias = refs[groups : groups + 3]
    outs = refs[groups + 3 : groups + 3 + parts]
    rows, held = refs[groups + 3 + parts :]
    tokens = blocks[0].shape[1]
    total = groups * tokens
    share = LANES
    for k, block in enumerate(blocks):
        for a in range(3):
            rows[pl.ds(a * total + k * tokens, tokens), :] = block[a].astype(jnp.float32)
    encoded = jnp.dot(
        rows[pl.ds(0, 2 * total), :].astype(jnp.bfloat16),
        enc[...],
        preferred_element_type=jnp.float32,
    )
    projected = lax.dot_general(
        rows[pl.ds(2 * total, total), :].astype(jnp.bfloat16),
        dec[...],
        (((1,), (1,)), ((), ())),
        preferred_element_type=jnp.float32,
    )
    for c in range(parts):
        held[c, pl.ds(0, 2 * total), :] = encoded[:, c * share : (c + 1) * share]
        held[c, pl.ds(2 * total, total), :] = projected[:, c * share : (c + 1) * share]
    me = lax.axis_index("tensor")
    for r, out in zip(rotations(parts), outs):
        out[...] = held[lax.rem(me + r, parts)]
        if r == 0:
            out[pl.ds(0, 2 * total), :] += bias[pl.ds(me, 1), :]


def products(parts, blocks, enc_weight, dec_weight, bias):
    groups = len(blocks)
    _, tokens, width = blocks[0].shape
    features = enc_weight.shape[1]
    rows = 3 * groups * tokens
    part = jax.ShapeDtypeStruct((rows, features // parts), jnp.float32)
    vmem = pl.BlockSpec(memory_space=pltpu.VMEM)
    return pl.pallas_call(
        functools.partial(product_kernel, groups, parts),
        out_shape=[part] * parts,
        in_specs=[vmem] * (groups + 3),
        out_specs=[vmem] * parts,
        scratch_shapes=[
            pltpu.VMEM((rows, width), jnp.float32),
            pltpu.VMEM((parts, rows, features // parts), jnp.float32),
        ],
        compiler_params=pltpu.CompilerParams(vmem_limit_bytes=48 * 2**20),
        name="products",
    )(*blocks, enc_weight, dec_weight, bias)


def add_up(values):
    while len(values) > 1:
        values = [a + b for a, b in zip(values[::2], values[1::2])]
    return values[0]


def attribution_kernel(sizes, *refs):
    sections, feats, parts = sizes
    groups = sections * feats
    terms = refs[:parts]
    inner, sums = refs[parts:]
    total = terms[0].shape[0] // 3
    tokens = total // groups
    preact = add_up([term[...] for term in terms])
    section, feat = lax.axis_index("section"), lax.axis_index("feat")
    act_clean = jnp.maximum(preact[:total], 0.0)
    act_corrupt = jnp.maximum(preact[total : 2 * total], 0.0)
    attribution = (act_corrupt - act_clean) * preact[2 * total :]

    devices = groups * parts
    feature_part = jnp.sum(attribution, axis=0, keepdims=True)
    sums[:, 0, :] = jnp.broadcast_to(feature_part, (devices, LANES))
    token_part = jnp.sum(attribution, axis=1, keepdims=True)
    lane = lax.broadcasted_iota(jnp.int32, (tokens, LANES), 1)
    place = lane == lax.broadcasted_iota(jnp.int32, (tokens, LANES), 0)
    for k, (p, q) in enumerate(row_blocks(sections, feats)):
        column = jnp.broadcast_to(token_part[k * tokens : (k + 1) * tokens], (tokens, LANES))
        if (p, q) == (1, 0):
            column = column - inner[pl.ds(0, tokens), :]
        row = jnp.sum(jnp.where(place, column, 0.0), axis=0, keepdims=True)
        owner = (section ^ q) * feats + (feat ^ 1 ^ p)
        sums[pl.ds(owner * parts, parts), 1, :] = jnp.broadcast_to(row, (parts, LANES))


def attributions(sizes, terms, inner):
    sections, feats, parts = sizes
    vmem = pl.BlockSpec(memory_space=pltpu.VMEM)
    return pl.pallas_call(
        functools.partial(attribution_kernel, sizes),
        out_shape=jax.ShapeDtypeStruct((sections * feats * parts, 2, LANES), jnp.float32),
        in_specs=[vmem] * (parts + 1),
        out_specs=vmem,
        compiler_params=pltpu.CompilerParams(vmem_limit_bytes=16 * 2**20),
        name="attributions",
    )(*terms, inner)


def final_kernel(sizes, arrived, feature_out, error_out, features, errors, sems):
    sections, feats, parts = sizes
    group = lax.axis_index("section") * feats + (lax.axis_index("feat") ^ 1)
    mine = arrived[pl.ds(group * parts, parts), 0, :]
    for i in range(parts):
        features[pl.ds(i * LANES, LANES)] = mine[i]
    feature_copy = pltpu.make_async_copy(features, feature_out, sems.at[0])
    feature_copy.start()
    owed = add_up([arrived[i, 1:2, :] for i in range(sections * feats * parts)])
    errors[...] = -owed[0, : errors.shape[0]]
    error_copy = pltpu.make_async_copy(errors, error_out, sems.at[1])
    error_copy.start()
    feature_copy.wait()
    error_copy.wait()


def final(sizes, tokens, arrived):
    features = (sizes[2] * LANES,)
    return pl.pallas_call(
        functools.partial(final_kernel, sizes),
        out_shape=[
            jax.ShapeDtypeStruct(features, jnp.float32),
            jax.ShapeDtypeStruct((tokens,), jnp.float32),
        ],
        in_specs=[pl.BlockSpec(memory_space=pltpu.VMEM)],
        out_specs=[pl.BlockSpec(memory_space=pltpu.HBM)] * 2,
        scratch_shapes=[
            pltpu.VMEM(features, jnp.float32),
            pltpu.VMEM((tokens,), jnp.float32),
            pltpu.SemaphoreType.DMA((2,)),
        ],
        compiler_params=pltpu.CompilerParams(vmem_limit_bytes=4 * 2**20),
        name="final",
    )(arrived)


def per_device(sizes, clean_resid, corrupt_resid, metric_grad, enc_weight, enc_bias, dec_weight):
    sections, feats, parts = sizes
    tokens = clean_resid.shape[0]
    features = enc_weight.shape[1]

    packed = jnp.stack([clean_resid, corrupt_resid, metric_grad])
    inner = inner_products(packed)
    bias = enc_bias.reshape(parts, features // parts)
    held = {(0, 0): packed}
    for p, q in row_blocks(sections, feats):
        if q > 0 and (p == 0 or q == 1):
            pairs = [
                (s * feats + f, (s ^ q) * feats + (f ^ p))
                for s in range(sections)
                for f in range(feats)
            ]
            held[p, q] = lax.ppermute(packed, ("section", "feat"), pairs)
        elif p > 0:
            block = held[0, q]
            if q == 0:
                block, inner = lax.optimization_barrier((block, inner))
            held[p, q] = exchange(block, "feat", feats, p)
    blocks = [held[place] for place in row_blocks(sections, feats)]

    terms = products(parts, blocks, enc_weight, dec_weight, bias)
    arrived = []
    for r, term in zip(rotations(parts), terms):
        pairs = [
            (f * parts + t, (f ^ 1) * parts + (t + r) % parts)
            for f in range(feats)
            for t in range(parts)
        ]
        arrived.append(lax.ppermute(term, ("feat", "tensor"), pairs))
    sums = attributions(sizes, arrived, inner)
    return tuple(final(sizes, tokens, lax.all_to_all(sums, EVERY, 0, 0)))


def solution(mesh):
    sizes = [mesh.shape[name] for name in ("section", "feat", "tensor")]
    in_specs = (
        P(("section", "feat"), "tensor"),
        P(("section", "feat"), "tensor"),
        P(("section", "feat"), "tensor"),
        P("tensor", ("section", "feat")),
        P(("section", "feat")),
        P(("section", "feat"), "tensor"),
    )
    out_specs = (P(("section", "feat")), P(("section", "feat")))
    return jax.shard_map(
        functools.partial(per_device, sizes),
        mesh=mesh,
        in_specs=in_specs,
        out_specs=out_specs,
        check_vma=False,
    )
```

```python
import functools

import jax
import jax.numpy as jnp
from jax import lax
from jax.experimental import pallas as pl
from jax.experimental.pallas import tpu as pltpu
from jax.sharding import PartitionSpec as P

LANES = 128
TILE = 8


EVERY = ("section", "feat", "tensor")


def far_first(size):
    return [0, *reversed(range(1, size))]


def row_blocks(sections, feats):
    places = [(p, q) for p in range(feats) for q in range(sections)]
    return sorted(places, key=lambda place: (place[0] > 0 and place[1] != 1, place[1], place[0]))


def exchange(value, axis, size, k):
    return lax.ppermute(value, axis, [(i, i ^ k) for i in range(size)])


def inner_kernel(packed, inner):
    tokens = packed.shape[1]
    clean, corrupt, grad = [packed[a].astype(jnp.float32) for a in range(3)]
    part = jnp.sum((corrupt - clean) * grad, axis=1, keepdims=True)
    inner[pl.ds(0, tokens), :] = jnp.broadcast_to(part, (tokens, LANES))


def inner_products(packed):
    vmem = pl.BlockSpec(memory_space=pltpu.VMEM)
    return pl.pallas_call(
        inner_kernel,
        out_shape=jax.ShapeDtypeStruct((TILE, LANES), jnp.float32),
        in_specs=[vmem],
        out_specs=vmem,
        compiler_params=pltpu.CompilerParams(vmem_limit_bytes=4 * 2**20),
        cost_estimate=pl.CostEstimate(flops=2**32, bytes_accessed=2**24, transcendentals=0),
        name="inner_products",
    )(packed)


def inner_kernel(packed, inner):
    tokens = packed.shape[1]
    clean, corrupt, grad = [packed[a].astype(jnp.float32) for a in range(3)]
    part = jnp.sum((corrupt - clean) * grad, axis=1, keepdims=True)
    inner[pl.ds(0, tokens), :] = jnp.broadcast_to(part, (tokens, LANES))


def inner_products(packed):
    vmem = pl.BlockSpec(memory_space=pltpu.VMEM)
    return pl.pallas_call(
        inner_kernel,
        out_shape=jax.ShapeDtypeStruct((TILE, LANES), jnp.float32),
        in_specs=[vmem],
        out_specs=vmem,
        compiler_params=pltpu.CompilerParams(vmem_limit_bytes=4 * 2**20),
        cost_estimate=pl.CostEstimate(flops=2**32, bytes_accessed=2**24, transcendentals=0),
        name="inner_products",
    )(packed)


def load_kernel(pieces, *refs):
    count = (len(refs) - 2) // 2
    sems = refs[-1]
    copies = []
    for i in range(count):
        source, target = refs[1 + i], refs[1 + count + i]
        count_here = min(pieces, source.shape[0] // 16) or 1
        step = source.shape[0] // count_here
        for j in range(count_here):
            part = pl.ds(j * step, step)
            copies.append(
                pltpu.make_async_copy(source.at[part], target.at[part], sems.at[i, j])
            )
    for copy in copies:
        copy.start()
    for copy in copies:
        copy.wait()


def load(after, *arrays, pieces=4):
    size = sum(array.size * array.dtype.itemsize for array in arrays)
    return pl.pallas_call(
        functools.partial(load_kernel, pieces),
        out_shape=[jax.ShapeDtypeStruct(array.shape, array.dtype) for array in arrays],
        in_specs=[pl.BlockSpec(memory_space=pltpu.VMEM)]
        + [pl.BlockSpec(memory_space=pltpu.HBM)] * len(arrays),
        out_specs=[pl.BlockSpec(memory_space=pltpu.VMEM)] * len(arrays),
        scratch_shapes=[pltpu.SemaphoreType.DMA((len(arrays), pieces))],
        compiler_params=pltpu.CompilerParams(vmem_limit_bytes=16 * 2**20),
        cost_estimate=pl.CostEstimate(flops=0, bytes_accessed=2 * size, transcendentals=0),
        name="load_weights",
    )(after, *arrays)


def product_kernel(groups, parts, *refs):
    blocks = refs[:groups]
    enc, dec = refs[groups : groups + 2]
    outs = refs[groups + 2 : groups + 2 + parts]
    rows = refs[groups + 2 + parts]
    tokens = blocks[0].shape[1]
    total = groups * tokens
    for k, block in enumerate(blocks):
        for a in range(3):
            rows[pl.ds(a * total + k * tokens, tokens), :] = block[a].astype(jnp.float32)
    me = lax.axis_index("tensor")
    low = me % 2 == 0
    for upper in range(parts // 2):
        pair = pl.ds(pl.multiple_of((me // 2 ^ upper) * 2 * LANES, 2 * LANES), 2 * LANES)
        encoded = jnp.dot(
            rows[pl.ds(0, 2 * total), :].astype(jnp.bfloat16),
            enc[:, pair],
            preferred_element_type=jnp.float32,
        )
        projected = lax.dot_general(
            rows[pl.ds(2 * total, total), :].astype(jnp.bfloat16),
            dec[pair, :],
            (((1,), (1,)), ((), ())),
            preferred_element_type=jnp.float32,
        )
        for start, value in ((0, encoded), (2 * total, projected)):
            first, second = value[:, :LANES], value[:, LANES:]
            place = pl.ds(start, value.shape[0])
            outs[2 * upper][place, :] = jnp.where(low, first, second)
            outs[2 * upper + 1][place, :] = jnp.where(low, second, first)


def products(parts, blocks, enc_weight, dec_weight):
    groups = len(blocks)
    _, tokens, width = blocks[0].shape
    features = enc_weight.shape[1]
    rows = 3 * groups * tokens
    part = jax.ShapeDtypeStruct((rows, features // parts), jnp.float32)
    vmem = pl.BlockSpec(memory_space=pltpu.VMEM)
    return pl.pallas_call(
        functools.partial(product_kernel, groups, parts),
        out_shape=[part] * parts,
        in_specs=[vmem] * (groups + 2),
        out_specs=[vmem] * parts,
        scratch_shapes=[
            pltpu.VMEM((rows, width), jnp.float32),
        ],
        compiler_params=pltpu.CompilerParams(vmem_limit_bytes=48 * 2**20),
        name="products",
    )(*blocks, enc_weight, dec_weight)


def add_up(values):
    while len(values) > 1:
        values = [a + b for a, b in zip(values[::2], values[1::2])]
    return values[0]


def attribution_kernel(sizes, *refs):
    sections, feats, parts = sizes
    groups = sections * feats
    terms = [refs[far_first(parts).index(m)] for m in range(parts)]
    bias, inner, sums = refs[parts:]
    total = terms[0].shape[0] // 3
    tokens = total // groups
    preact = add_up([term[...] for term in terms])
    section, feat = lax.axis_index("section"), lax.axis_index("feat")
    b = bias[pl.ds(lax.axis_index("tensor"), 1), :]
    act_clean = jnp.maximum(preact[:total] + b, 0.0)
    act_corrupt = jnp.maximum(preact[total : 2 * total] + b, 0.0)
    attribution = (act_corrupt - act_clean) * preact[2 * total :]

    devices = groups * parts
    feature_part = jnp.sum(attribution, axis=0, keepdims=True)
    sums[:, 0, :] = jnp.broadcast_to(feature_part, (devices, LANES))
    token_part = jnp.sum(attribution, axis=1, keepdims=True)
    lane = lax.broadcasted_iota(jnp.int32, (tokens, LANES), 1)
    place = lane == lax.broadcasted_iota(jnp.int32, (tokens, LANES), 0)
    for k, (p, q) in enumerate(row_blocks(sections, feats)):
        column = jnp.broadcast_to(token_part[k * tokens : (k + 1) * tokens], (tokens, LANES))
        if k == 0:
            column = column - inner[pl.ds(0, tokens), :]
        row = jnp.sum(jnp.where(place, column, 0.0), axis=0, keepdims=True)
        owner = (section ^ q) * feats + (feat ^ p)
        sums[pl.ds(owner * parts, parts), 1, :] = jnp.broadcast_to(row, (parts, LANES))


def attributions(sizes, terms, bias, inner):
    sections, feats, parts = sizes
    vmem = pl.BlockSpec(memory_space=pltpu.VMEM)
    return pl.pallas_call(
        functools.partial(attribution_kernel, sizes),
        out_shape=jax.ShapeDtypeStruct((sections * feats * parts, 2, LANES), jnp.float32),
        in_specs=[vmem] * (parts + 2),
        out_specs=vmem,
        compiler_params=pltpu.CompilerParams(vmem_limit_bytes=16 * 2**20),
        name="attributions",
    )(*terms, bias, inner)


def final_kernel(sizes, arrived, feature_out, error_out, features, errors, sems):
    sections, feats, parts = sizes
    group = lax.axis_index("section") * feats + lax.axis_index("feat")
    mine = arrived[pl.ds(group * parts, parts), 0, :]
    for i in range(parts):
        features[pl.ds(i * LANES, LANES)] = mine[i]
    feature_copy = pltpu.make_async_copy(features, feature_out, sems.at[0])
    feature_copy.start()
    owed = add_up([arrived[i, 1:2, :] for i in range(sections * feats * parts)])
    errors[...] = -owed[0, : errors.shape[0]]
    error_copy = pltpu.make_async_copy(errors, error_out, sems.at[1])
    error_copy.start()
    feature_copy.wait()
    error_copy.wait()


def final(sizes, tokens, arrived):
    features = (sizes[2] * LANES,)
    return pl.pallas_call(
        functools.partial(final_kernel, sizes),
        out_shape=[
            jax.ShapeDtypeStruct(features, jnp.float32),
            jax.ShapeDtypeStruct((tokens,), jnp.float32),
        ],
        in_specs=[pl.BlockSpec(memory_space=pltpu.VMEM)],
        out_specs=[pl.BlockSpec(memory_space=pltpu.HBM)] * 2,
        scratch_shapes=[
            pltpu.VMEM(features, jnp.float32),
            pltpu.VMEM((tokens,), jnp.float32),
            pltpu.SemaphoreType.DMA((2,)),
        ],
        compiler_params=pltpu.CompilerParams(vmem_limit_bytes=4 * 2**20),
        name="final",
    )(arrived)


def per_device(sizes, clean_resid, corrupt_resid, metric_grad, enc_weight, enc_bias, dec_weight):
    sections, feats, parts = sizes
    tokens = clean_resid.shape[0]
    features = enc_weight.shape[1]

    packed = jnp.stack([clean_resid, corrupt_resid, metric_grad])
    inner = inner_products(packed)
    bias = enc_bias.reshape(parts, features // parts)
    held = {(0, 0): packed}
    for p, q in row_blocks(sections, feats):
        if q > 0 and (p == 0 or q == 1):
            pairs = [
                (s * feats + f, (s ^ q) * feats + (f ^ p))
                for s in range(sections)
                for f in range(feats)
            ]
            held[p, q] = lax.ppermute(packed, ("section", "feat"), pairs)
        elif p > 0:
            block = held[0, q]
            if q == 0:
                block, inner = lax.optimization_barrier((block, inner))
            held[p, q] = exchange(block, "feat", feats, p)
    blocks = [held[place] for place in row_blocks(sections, feats)]

    terms = products(parts, blocks, enc_weight, dec_weight)
    arrived = [exchange(terms[m], "tensor", parts, m) for m in far_first(parts)[1:]]
    sums = attributions(sizes, [terms[0]] + arrived, bias, inner)
    return tuple(final(sizes, tokens, lax.all_to_all(sums, EVERY, 0, 0)))


def solution(mesh):
    sizes = [mesh.shape[name] for name in ("section", "feat", "tensor")]
    in_specs = (
        P(("section", "feat"), "tensor"),
        P(("section", "feat"), "tensor"),
        P(("section", "feat"), "tensor"),
        P("tensor", ("section", "feat")),
        P(("section", "feat")),
        P(("section", "feat"), "tensor"),
    )
    out_specs = (P(("section", "feat")), P(("section", "feat")))
    return jax.shard_map(
        functools.partial(per_device, sizes),
        mesh=mesh,
        in_specs=in_specs,
        out_specs=out_specs,
        check_vma=False,
    )
```

```python
import functools

import jax
import jax.numpy as jnp
from jax import lax
from jax.experimental import pallas as pl
from jax.experimental.pallas import tpu as pltpu
from jax.sharding import PartitionSpec as P

LANES = 128
TILE = 8


EVERY = ("section", "feat", "tensor")


def far_first(size):
    return sorted(range(size), key=lambda m: (m > 0, m < size // 2, m))


def row_blocks(sections, feats):
    places = [(p, q) for p in range(feats) for q in range(sections)]
    return sorted(places, key=lambda place: (place[0] > 0 and place[1] != 1, place[1], place[0]))


def exchange(value, axis, size, k):
    return lax.ppermute(value, axis, [(i, i ^ k) for i in range(size)])


def inner_kernel(packed, inner):
    tokens = packed.shape[1]
    clean, corrupt, grad = [packed[a].astype(jnp.float32) for a in range(3)]
    part = jnp.sum((corrupt - clean) * grad, axis=1, keepdims=True)
    inner[pl.ds(0, tokens), :] = jnp.broadcast_to(part, (tokens, LANES))


def inner_products(packed):
    vmem = pl.BlockSpec(memory_space=pltpu.VMEM)
    return pl.pallas_call(
        inner_kernel,
        out_shape=jax.ShapeDtypeStruct((TILE, LANES), jnp.float32),
        in_specs=[vmem],
        out_specs=vmem,
        compiler_params=pltpu.CompilerParams(vmem_limit_bytes=4 * 2**20),
        cost_estimate=pl.CostEstimate(flops=2**32, bytes_accessed=2**24, transcendentals=0),
        name="inner_products",
    )(packed)


def inner_products(packed):
    vmem = pl.BlockSpec(memory_space=pltpu.VMEM)
    return pl.pallas_call(
        inner_kernel,
        out_shape=jax.ShapeDtypeStruct((TILE, LANES), jnp.float32),
        in_specs=[vmem],
        out_specs=vmem,
        compiler_params=pltpu.CompilerParams(vmem_limit_bytes=4 * 2**20),
        cost_estimate=pl.CostEstimate(flops=2**32, bytes_accessed=2**24, transcendentals=0),
        name="inner_products",
    )(packed)


def load_kernel(pieces, *refs):
    count = (len(refs) - 2) // 2
    sems = refs[-1]
    copies = []
    for i in range(count):
        source, target = refs[1 + i], refs[1 + count + i]
        count_here = min(pieces, source.shape[0] // 16) or 1
        step = source.shape[0] // count_here
        for j in range(count_here):
            part = pl.ds(j * step, step)
            copies.append(
                pltpu.make_async_copy(source.at[part], target.at[part], sems.at[i, j])
            )
    for copy in copies:
        copy.start()
    for copy in copies:
        copy.wait()


def load(after, *arrays, pieces=4):
    size = sum(array.size * array.dtype.itemsize for array in arrays)
    return pl.pallas_call(
        functools.partial(load_kernel, pieces),
        out_shape=[jax.ShapeDtypeStruct(array.shape, array.dtype) for array in arrays],
        in_specs=[pl.BlockSpec(memory_space=pltpu.VMEM)]
        + [pl.BlockSpec(memory_space=pltpu.HBM)] * len(arrays),
        out_specs=[pl.BlockSpec(memory_space=pltpu.VMEM)] * len(arrays),
        scratch_shapes=[pltpu.SemaphoreType.DMA((len(arrays), pieces))],
        compiler_params=pltpu.CompilerParams(vmem_limit_bytes=16 * 2**20),
        cost_estimate=pl.CostEstimate(flops=0, bytes_accessed=2 * size, transcendentals=0),
        name="load_weights",
    )(after, *arrays)


def product_kernel(groups, parts, *refs):
    blocks = refs[:groups]
    enc, dec = refs[groups : groups + 2]
    outs = refs[groups + 2 : groups + 2 + parts]
    rows = refs[groups + 2 + parts]
    tokens = blocks[0].shape[1]
    total = groups * tokens
    for k, block in enumerate(blocks):
        for a in range(3):
            rows[pl.ds(a * total + k * tokens, tokens), :] = block[a].astype(jnp.float32)
    me = lax.axis_index("tensor")
    low = me % 2 == 0
    for upper in range(parts // 2):
        pair = pl.ds(pl.multiple_of((me // 2 ^ upper) * 2 * LANES, 2 * LANES), 2 * LANES)
        encoded = jnp.dot(
            rows[pl.ds(0, 2 * total), :].astype(jnp.bfloat16),
            enc[:, pair],
            preferred_element_type=jnp.float32,
        )
        projected = lax.dot_general(
            rows[pl.ds(2 * total, total), :].astype(jnp.bfloat16),
            dec[pair, :],
            (((1,), (1,)), ((), ())),
            preferred_element_type=jnp.float32,
        )
        for start, value in ((0, encoded), (2 * total, projected)):
            first, second = value[:, :LANES], value[:, LANES:]
            place = pl.ds(start, value.shape[0])
            outs[2 * upper][place, :] = jnp.where(low, first, second)
            outs[2 * upper + 1][place, :] = jnp.where(low, second, first)


def products(parts, blocks, enc_weight, dec_weight):
    groups = len(blocks)
    _, tokens, width = blocks[0].shape
    features = enc_weight.shape[1]
    rows = 3 * groups * tokens
    part = jax.ShapeDtypeStruct((rows, features // parts), jnp.float32)
    vmem = pl.BlockSpec(memory_space=pltpu.VMEM)
    return pl.pallas_call(
        functools.partial(product_kernel, groups, parts),
        out_shape=[part] * parts,
        in_specs=[vmem] * (groups + 2),
        out_specs=[vmem] * parts,
        scratch_shapes=[
            pltpu.VMEM((rows, width), jnp.float32),
        ],
        compiler_params=pltpu.CompilerParams(vmem_limit_bytes=48 * 2**20),
        name="products",
    )(*blocks, enc_weight, dec_weight)


def add_up(values):
    while len(values) > 1:
        values = [a + b for a, b in zip(values[::2], values[1::2])]
    return values[0]


def attribution_kernel(sizes, *refs):
    sections, feats, parts = sizes
    groups = sections * feats
    terms = [refs[far_first(parts).index(m)] for m in range(parts)]
    bias, inner, sums = refs[parts:]
    total = terms[0].shape[0] // 3
    tokens = total // groups
    preact = add_up([term[...] for term in terms])
    section, feat = lax.axis_index("section"), lax.axis_index("feat")
    b = bias[pl.ds(lax.axis_index("tensor"), 1), :]
    act_clean = jnp.maximum(preact[:total] + b, 0.0)
    act_corrupt = jnp.maximum(preact[total : 2 * total] + b, 0.0)
    attribution = (act_corrupt - act_clean) * preact[2 * total :]

    devices = groups * parts
    feature_part = jnp.sum(attribution, axis=0, keepdims=True)
    sums[:, 0, :] = jnp.broadcast_to(feature_part, (devices, LANES))
    token_part = jnp.sum(attribution, axis=1, keepdims=True)
    lane = lax.broadcasted_iota(jnp.int32, (tokens, LANES), 1)
    place = lane == lax.broadcasted_iota(jnp.int32, (tokens, LANES), 0)
    for k, (p, q) in enumerate(row_blocks(sections, feats)):
        column = jnp.broadcast_to(token_part[k * tokens : (k + 1) * tokens], (tokens, LANES))
        if k == 0:
            column = column - inner[pl.ds(0, tokens), :]
        row = jnp.sum(jnp.where(place, column, 0.0), axis=0, keepdims=True)
        owner = (section ^ q) * feats + (feat ^ p)
        sums[pl.ds(owner * parts, parts), 1, :] = jnp.broadcast_to(row, (parts, LANES))


def attributions(sizes, terms, bias, inner):
    sections, feats, parts = sizes
    vmem = pl.BlockSpec(memory_space=pltpu.VMEM)
    return pl.pallas_call(
        functools.partial(attribution_kernel, sizes),
        out_shape=jax.ShapeDtypeStruct((sections * feats * parts, 2, LANES), jnp.float32),
        in_specs=[vmem] * (parts + 2),
        out_specs=vmem,
        compiler_params=pltpu.CompilerParams(vmem_limit_bytes=16 * 2**20),
        name="attributions",
    )(*terms, bias, inner)


def final_kernel(sizes, arrived, feature_out, error_out, features, errors, sems):
    sections, feats, parts = sizes
    group = lax.axis_index("section") * feats + lax.axis_index("feat")
    mine = arrived[pl.ds(group * parts, parts), 0, :]
    for i in range(parts):
        features[pl.ds(i * LANES, LANES)] = mine[i]
    feature_copy = pltpu.make_async_copy(features, feature_out, sems.at[0])
    feature_copy.start()
    owed = add_up([arrived[i, 1:2, :] for i in range(sections * feats * parts)])
    errors[...] = -owed[0, : errors.shape[0]]
    error_copy = pltpu.make_async_copy(errors, error_out, sems.at[1])
    error_copy.start()
    feature_copy.wait()
    error_copy.wait()


def final(sizes, tokens, arrived):
    features = (sizes[2] * LANES,)
    return pl.pallas_call(
        functools.partial(final_kernel, sizes),
        out_shape=[
            jax.ShapeDtypeStruct(features, jnp.float32),
            jax.ShapeDtypeStruct((tokens,), jnp.float32),
        ],
        in_specs=[pl.BlockSpec(memory_space=pltpu.VMEM)],
        out_specs=[pl.BlockSpec(memory_space=pltpu.HBM)] * 2,
        scratch_shapes=[
            pltpu.VMEM(features, jnp.float32),
            pltpu.VMEM((tokens,), jnp.float32),
            pltpu.SemaphoreType.DMA((2,)),
        ],
        compiler_params=pltpu.CompilerParams(vmem_limit_bytes=4 * 2**20),
        name="final",
    )(arrived)


def per_device(sizes, clean_resid, corrupt_resid, metric_grad, enc_weight, enc_bias, dec_weight):
    sections, feats, parts = sizes
    tokens = clean_resid.shape[0]
    features = enc_weight.shape[1]

    packed = jnp.stack([clean_resid, corrupt_resid, metric_grad])
    inner = inner_products(packed)
    bias = enc_bias.reshape(parts, features // parts)
    held = {(0, 0): packed}
    for p, q in row_blocks(sections, feats):
        if q > 0 and (p == 0 or q == 1):
            pairs = [
                (s * feats + f, (s ^ q) * feats + (f ^ p))
                for s in range(sections)
                for f in range(feats)
            ]
            held[p, q] = lax.ppermute(packed, ("section", "feat"), pairs)
        elif p > 0:
            block = held[0, q]
            if q == 0:
                block, inner = lax.optimization_barrier((block, inner))
            held[p, q] = exchange(block, "feat", feats, p)
    blocks = [held[place] for place in row_blocks(sections, feats)]

    terms = products(parts, blocks, enc_weight, dec_weight)
    arrived = [exchange(terms[m], "tensor", parts, m) for m in far_first(parts)[1:]]
    sums = attributions(sizes, [terms[0]] + arrived, bias, inner)
    return tuple(final(sizes, tokens, lax.all_to_all(sums, EVERY, 0, 0)))


def solution(mesh):
    sizes = [mesh.shape[name] for name in ("section", "feat", "tensor")]
    in_specs = (
        P(("section", "feat"), "tensor"),
        P(("section", "feat"), "tensor"),
        P(("section", "feat"), "tensor"),
        P("tensor", ("section", "feat")),
        P(("section", "feat")),
        P(("section", "feat"), "tensor"),
    )
    out_specs = (P(("section", "feat")), P(("section", "feat")))
    return jax.shard_map(
        functools.partial(per_device, sizes),
        mesh=mesh,
        in_specs=in_specs,
        out_specs=out_specs,
        check_vma=False,
    )
```

```python
import functools

import jax
import jax.numpy as jnp
from jax import lax
from jax.experimental import pallas as pl
from jax.experimental.pallas import tpu as pltpu
from jax.sharding import PartitionSpec as P

LANES = 128
TILE = 8


EVERY = ("section", "feat", "tensor")


def far_first(size):
    return [0, *reversed(range(1, size))]


def row_blocks(sections, feats):
    direct = sections // 2
    places = [(p, q) for p in range(feats) for q in range(sections)]
    return sorted(
        places,
        key=lambda place: (
            place[0] > 0 and place[1] != direct,
            place[1] != 0,
            place[1] != direct,
            place[1],
            place[0],
        ),
    )


def exchange(value, axis, size, k):
    return lax.ppermute(value, axis, [(i, i ^ k) for i in range(size)])


def inner_kernel(packed, inner):
    tokens = packed.shape[1]
    clean, corrupt, grad = [packed[a].astype(jnp.float32) for a in range(3)]
    part = jnp.sum((corrupt - clean) * grad, axis=1, keepdims=True)
    inner[pl.ds(0, tokens), :] = jnp.broadcast_to(part, (tokens, LANES))


def inner_products(packed):
    vmem = pl.BlockSpec(memory_space=pltpu.VMEM)
    return pl.pallas_call(
        inner_kernel,
        out_shape=jax.ShapeDtypeStruct((TILE, LANES), jnp.float32),
        in_specs=[vmem],
        out_specs=vmem,
        compiler_params=pltpu.CompilerParams(vmem_limit_bytes=4 * 2**20),
        cost_estimate=pl.CostEstimate(flops=2**32, bytes_accessed=2**24, transcendentals=0),
        name="inner_products",
    )(packed)


def inner_kernel(packed, inner):
    tokens = packed.shape[1]
    clean, corrupt, grad = [packed[a].astype(jnp.float32) for a in range(3)]
    part = jnp.sum((corrupt - clean) * grad, axis=1, keepdims=True)
    inner[pl.ds(0, tokens), :] = jnp.broadcast_to(part, (tokens, LANES))


def inner_products(packed):
    vmem = pl.BlockSpec(memory_space=pltpu.VMEM)
    return pl.pallas_call(
        inner_kernel,
        out_shape=jax.ShapeDtypeStruct((TILE, LANES), jnp.float32),
        in_specs=[vmem],
        out_specs=vmem,
        compiler_params=pltpu.CompilerParams(vmem_limit_bytes=4 * 2**20),
        cost_estimate=pl.CostEstimate(flops=2**32, bytes_accessed=2**24, transcendentals=0),
        name="inner_products",
    )(packed)


def load_kernel(pieces, *refs):
    count = (len(refs) - 2) // 2
    sems = refs[-1]
    copies = []
    for i in range(count):
        source, target = refs[1 + i], refs[1 + count + i]
        count_here = min(pieces, source.shape[0] // 16) or 1
        step = source.shape[0] // count_here
        for j in range(count_here):
            part = pl.ds(j * step, step)
            copies.append(
                pltpu.make_async_copy(source.at[part], target.at[part], sems.at[i, j])
            )
    for copy in copies:
        copy.start()
    for copy in copies:
        copy.wait()


def load(after, *arrays, pieces=4):
    size = sum(array.size * array.dtype.itemsize for array in arrays)
    return pl.pallas_call(
        functools.partial(load_kernel, pieces),
        out_shape=[jax.ShapeDtypeStruct(array.shape, array.dtype) for array in arrays],
        in_specs=[pl.BlockSpec(memory_space=pltpu.VMEM)]
        + [pl.BlockSpec(memory_space=pltpu.HBM)] * len(arrays),
        out_specs=[pl.BlockSpec(memory_space=pltpu.VMEM)] * len(arrays),
        scratch_shapes=[pltpu.SemaphoreType.DMA((len(arrays), pieces))],
        compiler_params=pltpu.CompilerParams(vmem_limit_bytes=16 * 2**20),
        cost_estimate=pl.CostEstimate(flops=0, bytes_accessed=2 * size, transcendentals=0),
        name="load_weights",
    )(after, *arrays)


def product_kernel(groups, parts, *refs):
    blocks = refs[:groups]
    enc, dec = refs[groups : groups + 2]
    outs = refs[groups + 2 : groups + 2 + parts]
    rows, held = refs[groups + 2 + parts :]
    tokens = blocks[0].shape[1]
    total = groups * tokens
    share = LANES
    for k, block in enumerate(blocks):
        for a in range(3):
            rows[pl.ds(a * total + k * tokens, tokens), :] = block[a].astype(jnp.float32)
    encoded = jnp.dot(
        rows[pl.ds(0, 2 * total), :].astype(jnp.bfloat16),
        enc[...],
        preferred_element_type=jnp.float32,
    )
    projected = lax.dot_general(
        rows[pl.ds(2 * total, total), :].astype(jnp.bfloat16),
        dec[...],
        (((1,), (1,)), ((), ())),
        preferred_element_type=jnp.float32,
    )
    for c in range(parts):
        held[c, pl.ds(0, 2 * total), :] = encoded[:, c * share : (c + 1) * share]
        held[c, pl.ds(2 * total, total), :] = projected[:, c * share : (c + 1) * share]
    me = lax.axis_index("tensor")
    for m, out in enumerate(outs):
        out[...] = held[me ^ m]


def products(parts, blocks, enc_weight, dec_weight):
    groups = len(blocks)
    _, tokens, width = blocks[0].shape
    features = enc_weight.shape[1]
    rows = 3 * groups * tokens
    part = jax.ShapeDtypeStruct((rows, features // parts), jnp.float32)
    vmem = pl.BlockSpec(memory_space=pltpu.VMEM)
    return pl.pallas_call(
        functools.partial(product_kernel, groups, parts),
        out_shape=[part] * parts,
        in_specs=[vmem] * (groups + 2),
        out_specs=[vmem] * parts,
        scratch_shapes=[
            pltpu.VMEM((rows, width), jnp.float32),
            pltpu.VMEM((parts, rows, features // parts), jnp.float32),
        ],
        compiler_params=pltpu.CompilerParams(vmem_limit_bytes=48 * 2**20),
        name="products",
    )(*blocks, enc_weight, dec_weight)


def add_up(values):
    while len(values) > 1:
        values = [a + b for a, b in zip(values[::2], values[1::2])]
    return values[0]


def attribution_kernel(sizes, *refs):
    sections, feats, parts = sizes
    groups = sections * feats
    terms = [refs[far_first(parts).index(m)] for m in range(parts)]
    bias, inner, sums = refs[parts:]
    total = terms[0].shape[0] // 3
    tokens = total // groups
    preact = add_up([term[...] for term in terms])
    section, feat = lax.axis_index("section"), lax.axis_index("feat")
    b = bias[pl.ds(lax.axis_index("tensor"), 1), :]
    act_clean = jnp.maximum(preact[:total] + b, 0.0)
    act_corrupt = jnp.maximum(preact[total : 2 * total] + b, 0.0)
    attribution = (act_corrupt - act_clean) * preact[2 * total :]

    devices = groups * parts
    feature_part = jnp.sum(attribution, axis=0, keepdims=True)
    sums[:, 0, :] = jnp.broadcast_to(feature_part, (devices, LANES))
    token_part = jnp.sum(attribution, axis=1, keepdims=True)
    lane = lax.broadcasted_iota(jnp.int32, (tokens, LANES), 1)
    place = lane == lax.broadcasted_iota(jnp.int32, (tokens, LANES), 0)
    for k, (p, q) in enumerate(row_blocks(sections, feats)):
        column = jnp.broadcast_to(token_part[k * tokens : (k + 1) * tokens], (tokens, LANES))
        if k == 0:
            column = column - inner[pl.ds(0, tokens), :]
        row = jnp.sum(jnp.where(place, column, 0.0), axis=0, keepdims=True)
        owner = (section ^ q) * feats + (feat ^ p)
        sums[pl.ds(owner * parts, parts), 1, :] = jnp.broadcast_to(row, (parts, LANES))


def attributions(sizes, terms, bias, inner):
    sections, feats, parts = sizes
    vmem = pl.BlockSpec(memory_space=pltpu.VMEM)
    return pl.pallas_call(
        functools.partial(attribution_kernel, sizes),
        out_shape=jax.ShapeDtypeStruct((sections * feats * parts, 2, LANES), jnp.float32),
        in_specs=[vmem] * (parts + 2),
        out_specs=vmem,
        compiler_params=pltpu.CompilerParams(vmem_limit_bytes=16 * 2**20),
        name="attributions",
    )(*terms, bias, inner)


def final_kernel(sizes, arrived, feature_out, error_out, features, errors, sems):
    sections, feats, parts = sizes
    group = lax.axis_index("section") * feats + lax.axis_index("feat")
    mine = arrived[pl.ds(group * parts, parts), 0, :]
    for i in range(parts):
        features[pl.ds(i * LANES, LANES)] = mine[i]
    feature_copy = pltpu.make_async_copy(features, feature_out, sems.at[0])
    feature_copy.start()
    owed = add_up([arrived[i, 1:2, :] for i in range(sections * feats * parts)])
    errors[...] = -owed[0, : errors.shape[0]]
    error_copy = pltpu.make_async_copy(errors, error_out, sems.at[1])
    error_copy.start()
    feature_copy.wait()
    error_copy.wait()


def final(sizes, tokens, arrived):
    features = (sizes[2] * LANES,)
    return pl.pallas_call(
        functools.partial(final_kernel, sizes),
        out_shape=[
            jax.ShapeDtypeStruct(features, jnp.float32),
            jax.ShapeDtypeStruct((tokens,), jnp.float32),
        ],
        in_specs=[pl.BlockSpec(memory_space=pltpu.VMEM)],
        out_specs=[pl.BlockSpec(memory_space=pltpu.HBM)] * 2,
        scratch_shapes=[
            pltpu.VMEM(features, jnp.float32),
            pltpu.VMEM((tokens,), jnp.float32),
            pltpu.SemaphoreType.DMA((2,)),
        ],
        compiler_params=pltpu.CompilerParams(vmem_limit_bytes=4 * 2**20),
        name="final",
    )(arrived)


def per_device(sizes, clean_resid, corrupt_resid, metric_grad, enc_weight, enc_bias, dec_weight):
    sections, feats, parts = sizes
    tokens = clean_resid.shape[0]
    features = enc_weight.shape[1]

    packed = jnp.stack([clean_resid, corrupt_resid, metric_grad])
    inner = inner_products(packed)
    bias = enc_bias.reshape(parts, features // parts)
    held = {(0, 0): packed}
    for p, q in row_blocks(sections, feats):
        if q > 0 and (p == 0 or q == sections // 2):
            pairs = [
                (s * feats + f, (s ^ q) * feats + (f ^ p))
                for s in range(sections)
                for f in range(feats)
            ]
            held[p, q] = lax.ppermute(packed, ("section", "feat"), pairs)
        elif p > 0:
            block = held[0, q]
            if q == 0:
                block, inner = lax.optimization_barrier((block, inner))
            held[p, q] = exchange(block, "feat", feats, p)
    blocks = [held[place] for place in row_blocks(sections, feats)]

    terms = products(parts, blocks, enc_weight, dec_weight)
    arrived = [exchange(terms[m], "tensor", parts, m) for m in far_first(parts)[1:]]
    sums = attributions(sizes, [terms[0]] + arrived, bias, inner)
    return tuple(final(sizes, tokens, lax.all_to_all(sums, EVERY, 0, 0)))


def solution(mesh):
    sizes = [mesh.shape[name] for name in ("section", "feat", "tensor")]
    in_specs = (
        P(("section", "feat"), "tensor"),
        P(("section", "feat"), "tensor"),
        P(("section", "feat"), "tensor"),
        P("tensor", ("section", "feat")),
        P(("section", "feat")),
        P(("section", "feat"), "tensor"),
    )
    out_specs = (P(("section", "feat")), P(("section", "feat")))
    return jax.shard_map(
        functools.partial(per_device, sizes),
        mesh=mesh,
        in_specs=in_specs,
        out_specs=out_specs,
        check_vma=False,
    )
```

```python
import functools

import jax
import jax.numpy as jnp
from jax import lax
from jax.experimental import pallas as pl
from jax.experimental.pallas import tpu as pltpu
from jax.sharding import PartitionSpec as P

LANES = 128
TILE = 8


EVERY = ("section", "feat", "tensor")


def far_first(size):
    return [0, *reversed(range(1, size))]


def row_blocks(sections, feats):
    direct = sections // 2
    places = [(p, q) for p in range(feats) for q in range(sections)]
    return sorted(
        places,
        key=lambda place: (
            place[0] > 0 and place[1] != direct,
            place[1] != 0,
            place[1] != direct,
            place[1],
            place[0],
        ),
    )


def exchange(value, axis, size, k):
    return lax.ppermute(value, axis, [(i, i ^ k) for i in range(size)])


def inner_kernel(packed, inner):
    tokens = packed.shape[1]
    clean, corrupt, grad = [packed[a].astype(jnp.float32) for a in range(3)]
    part = jnp.sum((corrupt - clean) * grad, axis=1, keepdims=True)
    inner[pl.ds(0, tokens), :] = jnp.broadcast_to(part, (tokens, LANES))


def inner_products(packed):
    vmem = pl.BlockSpec(memory_space=pltpu.VMEM)
    return pl.pallas_call(
        inner_kernel,
        out_shape=jax.ShapeDtypeStruct((TILE, LANES), jnp.float32),
        in_specs=[vmem],
        out_specs=vmem,
        compiler_params=pltpu.CompilerParams(vmem_limit_bytes=4 * 2**20),
        cost_estimate=pl.CostEstimate(flops=2**32, bytes_accessed=2**24, transcendentals=0),
        name="inner_products",
    )(packed)


def product_kernel(groups, parts, *refs):
    blocks = refs[:groups]
    enc, dec = refs[groups : groups + 2]
    outs = refs[groups + 2 : groups + 2 + parts]
    rows = refs[groups + 2 + parts]
    tokens = blocks[0].shape[1]
    total = groups * tokens
    for k, block in enumerate(blocks):
        for a in range(3):
            rows[pl.ds(a * total + k * tokens, tokens), :] = block[a].astype(jnp.float32)
    me = lax.axis_index("tensor")
    low = me % 2 == 0
    for upper in range(parts // 2):
        pair = pl.ds(pl.multiple_of((me // 2 ^ upper) * 2 * LANES, 2 * LANES), 2 * LANES)
        encoded = jnp.dot(
            rows[pl.ds(0, 2 * total), :].astype(jnp.bfloat16),
            enc[:, pair],
            preferred_element_type=jnp.float32,
        )
        projected = lax.dot_general(
            rows[pl.ds(2 * total, total), :].astype(jnp.bfloat16),
            dec[pair, :],
            (((1,), (1,)), ((), ())),
            preferred_element_type=jnp.float32,
        )
        for start, value in ((0, encoded), (2 * total, projected)):
            first, second = value[:, :LANES], value[:, LANES:]
            place = pl.ds(start, value.shape[0])
            outs[2 * upper][place, :] = jnp.where(low, first, second)
            outs[2 * upper + 1][place, :] = jnp.where(low, second, first)


def products(parts, blocks, enc_weight, dec_weight):
    groups = len(blocks)
    _, tokens, width = blocks[0].shape
    features = enc_weight.shape[1]
    rows = 3 * groups * tokens
    part = jax.ShapeDtypeStruct((rows, features // parts), jnp.float32)
    vmem = pl.BlockSpec(memory_space=pltpu.VMEM)
    return pl.pallas_call(
        functools.partial(product_kernel, groups, parts),
        out_shape=[part] * parts,
        in_specs=[vmem] * (groups + 2),
        out_specs=[vmem] * parts,
        scratch_shapes=[
            pltpu.VMEM((rows, width), jnp.float32),
        ],
        compiler_params=pltpu.CompilerParams(vmem_limit_bytes=48 * 2**20),
        name="products",
    )(*blocks, enc_weight, dec_weight)


def add_up(values):
    while len(values) > 1:
        values = [a + b for a, b in zip(values[::2], values[1::2])]
    return values[0]


def attribution_kernel(sizes, *refs):
    sections, feats, parts = sizes
    groups = sections * feats
    terms = [refs[far_first(parts).index(m)] for m in range(parts)]
    bias, inner, sums = refs[parts:]
    total = terms[0].shape[0] // 3
    tokens = total // groups
    preact = add_up([term[...] for term in terms])
    section, feat = lax.axis_index("section"), lax.axis_index("feat")
    b = bias[pl.ds(lax.axis_index("tensor"), 1), :]
    act_clean = jnp.maximum(preact[:total] + b, 0.0)
    act_corrupt = jnp.maximum(preact[total : 2 * total] + b, 0.0)
    attribution = (act_corrupt - act_clean) * preact[2 * total :]

    devices = groups * parts
    feature_part = jnp.sum(attribution, axis=0, keepdims=True)
    sums[:, 0, :] = jnp.broadcast_to(feature_part, (devices, LANES))
    token_part = jnp.sum(attribution, axis=1, keepdims=True)
    lane = lax.broadcasted_iota(jnp.int32, (tokens, LANES), 1)
    place = lane == lax.broadcasted_iota(jnp.int32, (tokens, LANES), 0)
    for k, (p, q) in enumerate(row_blocks(sections, feats)):
        column = jnp.broadcast_to(token_part[k * tokens : (k + 1) * tokens], (tokens, LANES))
        if k == 0:
            column = column - inner[pl.ds(0, tokens), :]
        row = jnp.sum(jnp.where(place, column, 0.0), axis=0, keepdims=True)
        owner = (section ^ q) * feats + (feat ^ p)
        sums[pl.ds(owner * parts, parts), 1, :] = jnp.broadcast_to(row, (parts, LANES))


def attributions(sizes, terms, bias, inner):
    sections, feats, parts = sizes
    vmem = pl.BlockSpec(memory_space=pltpu.VMEM)
    return pl.pallas_call(
        functools.partial(attribution_kernel, sizes),
        out_shape=jax.ShapeDtypeStruct((sections * feats * parts, 2, LANES), jnp.float32),
        in_specs=[vmem] * (parts + 2),
        out_specs=vmem,
        compiler_params=pltpu.CompilerParams(vmem_limit_bytes=16 * 2**20),
        name="attributions",
    )(*terms, bias, inner)


def final_kernel(sizes, arrived, feature_out, error_out, features, errors, sems):
    sections, feats, parts = sizes
    group = lax.axis_index("section") * feats + lax.axis_index("feat")
    mine = arrived[pl.ds(group * parts, parts), 0, :]
    for i in range(parts):
        features[pl.ds(i * LANES, LANES)] = mine[i]
    feature_copy = pltpu.make_async_copy(features, feature_out, sems.at[0])
    feature_copy.start()
    owed = add_up([arrived[i, 1:2, :] for i in range(sections * feats * parts)])
    errors[...] = -owed[0, : errors.shape[0]]
    error_copy = pltpu.make_async_copy(errors, error_out, sems.at[1])
    error_copy.start()
    feature_copy.wait()
    error_copy.wait()


def final(sizes, tokens, arrived):
    features = (sizes[2] * LANES,)
    return pl.pallas_call(
        functools.partial(final_kernel, sizes),
        out_shape=[
            jax.ShapeDtypeStruct(features, jnp.float32),
            jax.ShapeDtypeStruct((tokens,), jnp.float32),
        ],
        in_specs=[pl.BlockSpec(memory_space=pltpu.VMEM)],
        out_specs=[pl.BlockSpec(memory_space=pltpu.HBM)] * 2,
        scratch_shapes=[
            pltpu.VMEM(features, jnp.float32),
            pltpu.VMEM((tokens,), jnp.float32),
            pltpu.SemaphoreType.DMA((2,)),
        ],
        compiler_params=pltpu.CompilerParams(vmem_limit_bytes=4 * 2**20),
        name="final",
    )(arrived)


def per_device(sizes, clean_resid, corrupt_resid, metric_grad, enc_weight, enc_bias, dec_weight):
    sections, feats, parts = sizes
    tokens = clean_resid.shape[0]
    features = enc_weight.shape[1]

    packed = jnp.stack([clean_resid, corrupt_resid, metric_grad])
    inner = inner_products(packed)
    bias = enc_bias.reshape(parts, features // parts)
    held = {(0, 0): packed}
    for p, q in row_blocks(sections, feats):
        if q > 0 and (p == 0 or q == sections // 2):
            pairs = [
                (s * feats + f, (s ^ q) * feats + (f ^ p))
                for s in range(sections)
                for f in range(feats)
            ]
            held[p, q] = lax.ppermute(packed, ("section", "feat"), pairs)
        elif p > 0:
            block = held[0, q]
            if q == 0:
                block, inner = lax.optimization_barrier((block, inner))
            held[p, q] = exchange(block, "feat", feats, p)
    blocks = [held[place] for place in row_blocks(sections, feats)]

    terms = products(parts, blocks, enc_weight, dec_weight)
    arrived = [exchange(terms[m], "tensor", parts, m) for m in far_first(parts)[1:]]
    sums = attributions(sizes, [terms[0]] + arrived, bias, inner)
    return tuple(final(sizes, tokens, lax.all_to_all(sums, EVERY, 0, 0)))


def solution(mesh):
    sizes = [mesh.shape[name] for name in ("section", "feat", "tensor")]
    in_specs = (
        P(("section", "feat"), "tensor"),
        P(("section", "feat"), "tensor"),
        P(("section", "feat"), "tensor"),
        P("tensor", ("section", "feat")),
        P(("section", "feat")),
        P(("section", "feat"), "tensor"),
    )
    out_specs = (P(("section", "feat")), P(("section", "feat")))
    return jax.shard_map(
        functools.partial(per_device, sizes),
        mesh=mesh,
        in_specs=in_specs,
        out_specs=out_specs,
        check_vma=False,
    )
```

```python
import functools

import jax
import jax.numpy as jnp
from jax import lax
from jax.experimental import pallas as pl
from jax.experimental.pallas import tpu as pltpu
from jax.sharding import PartitionSpec as P

LANES = 128
TILE = 8


EVERY = ("section", "feat", "tensor")


def far_first(size):
    return [0, *reversed(range(1, size))]


def row_blocks(sections, feats):
    direct = sections // 2
    places = [(p, q) for p in range(feats) for q in range(sections)]
    return sorted(
        places,
        key=lambda place: (
            place[0] > 0 and place[1] != direct,
            place[1] != 0,
            place[1] != direct,
            place[1],
            place[0],
        ),
    )


def exchange(value, axis, size, k):
    return lax.ppermute(value, axis, [(i, i ^ k) for i in range(size)])


def inner_kernel(packed, inner):
    tokens = packed.shape[1]
    clean, corrupt, grad = [packed[a].astype(jnp.float32) for a in range(3)]
    part = jnp.sum((corrupt - clean) * grad, axis=1, keepdims=True)
    inner[pl.ds(0, tokens), :] = jnp.broadcast_to(part, (tokens, LANES))


def inner_products(packed):
    vmem = pl.BlockSpec(memory_space=pltpu.VMEM)
    return pl.pallas_call(
        inner_kernel,
        out_shape=jax.ShapeDtypeStruct((TILE, LANES), jnp.float32),
        in_specs=[vmem],
        out_specs=vmem,
        compiler_params=pltpu.CompilerParams(vmem_limit_bytes=4 * 2**20),
        cost_estimate=pl.CostEstimate(flops=2**32, bytes_accessed=2**24, transcendentals=0),
        name="inner_products",
    )(packed)


def product_kernel(groups, parts, *refs):
    blocks = refs[:groups]
    enc, dec = refs[groups : groups + 2]
    outs = refs[groups + 2 : groups + 2 + parts]
    rows = refs[groups + 2 + parts]
    tokens = blocks[0].shape[1]
    total = groups * tokens
    for k, block in enumerate(blocks):
        for a in range(3):
            rows[pl.ds(a * total + k * tokens, tokens), :] = block[a].astype(jnp.float32)
    me = lax.axis_index("tensor")
    low = me % 2 == 0
    for upper in range(parts // 2):
        pair = pl.ds(pl.multiple_of((me // 2 ^ upper) * 2 * LANES, 2 * LANES), 2 * LANES)
        encoded = jnp.dot(
            rows[pl.ds(0, 2 * total), :].astype(jnp.bfloat16),
            enc[:, pair],
            preferred_element_type=jnp.float32,
        )
        projected = lax.dot_general(
            rows[pl.ds(2 * total, total), :].astype(jnp.bfloat16),
            dec[pair, :],
            (((1,), (1,)), ((), ())),
            preferred_element_type=jnp.float32,
        )
        for start, value in ((0, encoded), (2 * total, projected)):
            first, second = value[:, :LANES], value[:, LANES:]
            place = pl.ds(start, value.shape[0])
            outs[2 * upper][place, :] = jnp.where(low, first, second)
            outs[2 * upper + 1][place, :] = jnp.where(low, second, first)


def products(parts, blocks, enc_weight, dec_weight):
    groups = len(blocks)
    _, tokens, width = blocks[0].shape
    features = enc_weight.shape[1]
    rows = 3 * groups * tokens
    part = jax.ShapeDtypeStruct((rows, features // parts), jnp.float32)
    vmem = pl.BlockSpec(memory_space=pltpu.VMEM)
    return pl.pallas_call(
        functools.partial(product_kernel, groups, parts),
        out_shape=[part] * parts,
        in_specs=[vmem] * (groups + 2),
        out_specs=[vmem] * parts,
        scratch_shapes=[
            pltpu.VMEM((rows, width), jnp.float32),
        ],
        compiler_params=pltpu.CompilerParams(vmem_limit_bytes=48 * 2**20),
        name="products",
    )(*blocks, enc_weight, dec_weight)


def add_up(values):
    while len(values) > 1:
        values = [a + b for a, b in zip(values[::2], values[1::2])]
    return values[0]


def attribution_kernel(sizes, *refs):
    sections, feats, parts = sizes
    groups = sections * feats
    terms = [refs[far_first(parts).index(m)] for m in range(parts)]
    bias, inner, sums = refs[parts:]
    total = terms[0].shape[0] // 3
    tokens = total // groups
    preact = add_up([term[...] for term in terms])
    section, feat = lax.axis_index("section"), lax.axis_index("feat")
    b = bias[pl.ds(lax.axis_index("tensor"), 1), :]
    act_clean = jnp.maximum(preact[:total] + b, 0.0)
    act_corrupt = jnp.maximum(preact[total : 2 * total] + b, 0.0)
    attribution = (act_corrupt - act_clean) * preact[2 * total :]

    devices = groups * parts
    feature_part = jnp.sum(attribution, axis=0, keepdims=True)
    sums[:, 0, :] = jnp.broadcast_to(feature_part, (devices, LANES))
    token_part = jnp.sum(attribution, axis=1, keepdims=True)
    lane = lax.broadcasted_iota(jnp.int32, (tokens, LANES), 1)
    place = lane == lax.broadcasted_iota(jnp.int32, (tokens, LANES), 0)
    for k, (p, q) in enumerate(row_blocks(sections, feats)):
        column = jnp.broadcast_to(token_part[k * tokens : (k + 1) * tokens], (tokens, LANES))
        if k == 0:
            column = column - inner[pl.ds(0, tokens), :]
        row = jnp.sum(jnp.where(place, column, 0.0), axis=0, keepdims=True)
        owner = (section ^ q) * feats + (feat ^ p)
        sums[pl.ds(owner * parts, parts), 1, :] = jnp.broadcast_to(row, (parts, LANES))


def attributions(sizes, terms, bias, inner):
    sections, feats, parts = sizes
    vmem = pl.BlockSpec(memory_space=pltpu.VMEM)
    return pl.pallas_call(
        functools.partial(attribution_kernel, sizes),
        out_shape=jax.ShapeDtypeStruct((sections * feats * parts, 2, LANES), jnp.float32),
        in_specs=[vmem] * (parts + 2),
        out_specs=vmem,
        compiler_params=pltpu.CompilerParams(vmem_limit_bytes=16 * 2**20),
        name="attributions",
    )(*terms, bias, inner)


def final_kernel(sizes, arrived, feature_out, error_out, features, errors, sems):
    sections, feats, parts = sizes
    group = lax.axis_index("section") * feats + lax.axis_index("feat")
    mine = arrived[pl.ds(group * parts, parts), 0, :]
    for i in range(parts):
        features[pl.ds(i * LANES, LANES)] = mine[i]
    feature_copy = pltpu.make_async_copy(features, feature_out, sems.at[0])
    feature_copy.start()
    owed = jnp.sum(arrived[:, 1, :], axis=0, keepdims=True)
    errors[...] = -owed[0, : errors.shape[0]]
    error_copy = pltpu.make_async_copy(errors, error_out, sems.at[1])
    error_copy.start()
    feature_copy.wait()
    error_copy.wait()


def final(sizes, tokens, arrived):
    features = (sizes[2] * LANES,)
    return pl.pallas_call(
        functools.partial(final_kernel, sizes),
        out_shape=[
            jax.ShapeDtypeStruct(features, jnp.float32),
            jax.ShapeDtypeStruct((tokens,), jnp.float32),
        ],
        in_specs=[pl.BlockSpec(memory_space=pltpu.VMEM)],
        out_specs=[pl.BlockSpec(memory_space=pltpu.HBM)] * 2,
        scratch_shapes=[
            pltpu.VMEM(features, jnp.float32),
            pltpu.VMEM((tokens,), jnp.float32),
            pltpu.SemaphoreType.DMA((2,)),
        ],
        compiler_params=pltpu.CompilerParams(vmem_limit_bytes=4 * 2**20),
        name="final",
    )(arrived)


def per_device(sizes, clean_resid, corrupt_resid, metric_grad, enc_weight, enc_bias, dec_weight):
    sections, feats, parts = sizes
    tokens = clean_resid.shape[0]
    features = enc_weight.shape[1]

    packed = jnp.stack([clean_resid, corrupt_resid, metric_grad])
    inner = inner_products(packed)
    bias = enc_bias.reshape(parts, features // parts)
    held = {(0, 0): packed}
    for p, q in row_blocks(sections, feats):
        if q > 0 and (p == 0 or q == sections // 2):
            pairs = [
                (s * feats + f, (s ^ q) * feats + (f ^ p))
                for s in range(sections)
                for f in range(feats)
            ]
            held[p, q] = lax.ppermute(packed, ("section", "feat"), pairs)
        elif p > 0:
            block = held[0, q]
            if q == 0:
                block, inner = lax.optimization_barrier((block, inner))
            held[p, q] = exchange(block, "feat", feats, p)
    blocks = [held[place] for place in row_blocks(sections, feats)]

    terms = products(parts, blocks, enc_weight, dec_weight)
    arrived = [exchange(terms[m], "tensor", parts, m) for m in far_first(parts)[1:]]
    sums = attributions(sizes, [terms[0]] + arrived, bias, inner)
    return tuple(final(sizes, tokens, lax.all_to_all(sums, EVERY, 0, 0)))


def solution(mesh):
    sizes = [mesh.shape[name] for name in ("section", "feat", "tensor")]
    in_specs = (
        P(("section", "feat"), "tensor"),
        P(("section", "feat"), "tensor"),
        P(("section", "feat"), "tensor"),
        P("tensor", ("section", "feat")),
        P(("section", "feat")),
        P(("section", "feat"), "tensor"),
    )
    out_specs = (P(("section", "feat")), P(("section", "feat")))
    return jax.shard_map(
        functools.partial(per_device, sizes),
        mesh=mesh,
        in_specs=in_specs,
        out_specs=out_specs,
        check_vma=False,
    )
```
